256 devices in a mesh: grp: 16 (over z, core), dev: 16 (over y, x).
Axes of the slice: x: 4, y: 4, z: 8, core: 2. Of those that a mesh axis runs over, the one named last changes fastest.
Arguments:
- orbitals: bfloat16 [512, 256, 1024], P(('grp', 'dev')), may hold values from -6 to 6
- dens_tiles: bfloat16 [8192, 128, 128], P(('grp', 'dev')), may hold values from -0.005859375 to 0.005859375
- point_coords: float32 [3, 131072], P(None, ('grp', 'dev')), may hold values from 0 to 64
- point_weights: float32 [131072], P(('grp', 'dev')), may hold values from 0.005 to 0.05
- batch_blocks: int32 [512, 8], P(('grp', 'dev')), may hold values from 0 to 8, all different within a row
- tile_owner: int32 [20736, 1], P(('grp', 'dev')), may hold values from 0 to 15; in each aligned block of 81 rows (0 to 80, 81 to 161, ...) at most 9 rows name the same one
- tile_slot: int32 [20736], P(('grp', 'dev')), may hold values from 0 to 31
- batch_atoms: int32 [512, 4], P(('grp', 'dev')), may hold values from 0 to 15, all different within a row
- batch_weights: int32 [512, 4], P(('grp', 'dev')), may hold values from 1 to 8
- atom_grid_index: int32 [3, 256], P(None, 'grp'), may hold values from 0 to 63
Outputs:
- density: float32 [131072], P(('grp', 'dev'))
- potential: float32 [131072], P(('grp', 'dev'))
- ham_tiles: bfloat16 [8192, 128, 128], P(('grp', 'dev'))
The draws below stay inside these ranges and needn't reach their ends.
Inputs may be any that keep to these rules, and one draw needn't show every extreme that they name: `tile_owner`: in each aligned block of 81 rows (the listed tiles of one device) no owner is named by more than 9 rows, a bound that some block reaches. `batch_blocks`: the 8 blocks of a batch are distinct. `batch_atoms`: the 4 atoms of a batch are distinct.
All inputs are finite; a program needn't handle non-finite values.
Results may differ from the reference program's by a relative error of at most 0.0056.
Values may be sent and summed in bfloat16 or wider, within the bound.
No kernel may reach another device: no remote copies, remote signals or barrier semaphores. Data moves between devices by JAX's collectives and lax.ppermute only.
A program may use at most 64 MiB of HBM per device.

```python
import math
import jax
import jax.numpy as jnp
import numpy as np
from jax import lax

TB = 128
BB = 8
BORB = 1024
UB = 9
R = 81
PTS = 256
BAT_DEV = 2
KM = 512
NEAR = 4
TILE_DEV = 32
GRIDN = 64
OWNERS = 16
CAP = 9
ATOM_GRP = 16
ATOMS = 256
BATCHES = 512
POINTS = 131072
TILES = 8192
REQS = 20736
N_GRP = 16
N_DEV = 16


def with_ends(array, key, smallest, largest):
    longest = array.shape.index(max(array.shape))
    spots = []
    for shift in (0, 1):
        where = [jax.random.randint(jax.random.fold_in(key, axis), (), 0, length) for axis, length in enumerate(array.shape)]
        where[longest] = (where[longest] + shift) % array.shape[longest]
        spots.append(tuple(where))
    return array.at[spots[0]].set(smallest).at[spots[1]].set(largest)


def level_of(key, dims, split, smallest, high):
    gain, own = 1.0, jax.random.fold_in(key, 6)
    for axis_at, shards_of in split:
        draws = jnp.exp(jax.random.uniform(jax.random.fold_in(own, axis_at), (shards_of,), jnp.float32, smallest / len(split), high / len(split)))
        gain = gain * jnp.repeat(draws, dims[axis_at] // shards_of).reshape([-1 if axis == axis_at else 1 for axis in range(len(dims))])
    return gain


def different_ones(own_key, rows, count, top, lift):
    sequence = jax.random.permutation(jax.random.fold_in(own_key, 1), count)
    pull = sequence
    for power in range(3):
        pull = pull * pull // count
    pull = pull * lift // count
    lots = jax.random.randint(jax.random.fold_in(own_key, 2), (rows, count), 0, 4096) + pull
    holders = jax.random.permutation(jax.random.fold_in(own_key, 3), rows)[jnp.arange(count) % rows]
    lots = jnp.where(jnp.arange(rows)[:, None] == holders[None, :], 1 << 14, lots)
    merit = lots * count + jnp.arange(count)
    return lax.top_k(merit.astype(jnp.int32), top)[1].astype(jnp.int32)


def deal_out(stream_key, own, number, rows, amount, top, limit, lean):
    order = jax.random.permutation(stream_key, amount)
    packed, usual = shares(amount, rows * top, limit, lean, True), shares(amount, rows * top, limit, lean, False)
    places = jnp.arange(amount)

    def named(tallies, offset_by):
        used = int((tallies > 0).sum())
        fixed = max(1, used // 4)
        moved = fixed + (places - fixed + offset_by * (used - fixed)) % max(1, amount - fixed)
        return jnp.zeros((amount,), jnp.int32).at[order[jnp.where(places < fixed, places, moved)]].set(jnp.asarray(tallies, jnp.int32))

    tallies = jnp.where(number % 4 == 0, named(packed, number // 4), named(usual, number - number // 4 - 1))
    mixed = jax.random.permutation(jax.random.fold_in(own, 3), amount)
    donor, taker = mixed[0:amount // 2 * 2:2], mixed[1:amount // 2 * 2:2]
    margin = jnp.minimum(tallies[donor] - 1, limit - tallies[taker]) // 2
    margin = jnp.where((donor == order[0]) | (taker == order[0]) | (tallies[taker] == 0), 0, jnp.maximum(margin, 0))
    moved = jax.random.randint(jax.random.fold_in(own, 4), (amount // 2,), 0, 1 << 20) % (margin + 1)
    tallies = tallies.at[donor].add(-moved).at[taker].add(moved)
    items = jnp.searchsorted(jnp.cumsum(tallies), jnp.arange(rows * top), side="right").astype(jnp.int32)
    table = items.reshape(top, rows).T
    table = table[jax.random.permutation(jax.random.fold_in(own, 1), rows)]
    offset_by = jax.random.randint(jax.random.fold_in(own, 2), (rows, 1), 0, top)
    return jnp.take_along_axis(table, (jnp.arange(top)[None, :] + offset_by) % top, axis=1)


def shares(amount, total, bound, slope, full):
    portions = [(1 << 20) // math.isqrt(rank ** slope) + 1 for rank in range(1, amount + 1)]
    largest = bound if full else min(bound, max(-(-total // amount), total * portions[0] // sum(portions)))
    least = 1 if total - largest >= amount - 1 else 0
    holding, spare = [largest] + [least] * (amount - 1), total - largest - least * (amount - 1)
    while spare > 0:
        free = [i for i in range(1, amount) if holding[i] < largest] or [i for i in range(1, amount) if holding[i] < bound]
        whole, left = sum([portions[i] for i in free]), spare
        for i in free:
            more = min(bound - holding[i], max(1, left * portions[i] // whole), spare)
            holding[i] = holding[i] + more
            spare = spare - more
    return np.array(holding)


def gaussian(stream_key, dims, width, limit, split=(), kind=jnp.bfloat16):
    drawn = jax.random.normal(stream_key, dims, jnp.float32) * width
    if len(split) > 0:
        drawn = level_of(stream_key, dims, split, -0.22, 0.18) * drawn
    return jnp.clip(drawn, min=-limit, max=limit).astype(kind)


def setup_inputs(seed: int = 0) -> dict:
    streams_of = jax.random.split(jax.random.key(seed), 11)
    orbitals = gaussian(streams_of[0], (BATCHES, PTS, BORB), 1.0, 6.0, ((0, 256),))
    dens_tiles = gaussian(streams_of[1], (TILES, TB, TB), (1.0 / BORB), 0.005859375, ((0, 256),))
    point_coords = jnp.clip(64.0 * jax.random.uniform(streams_of[2], (3, POINTS), jnp.float32) ** level_of(streams_of[2], (3, POINTS), ((1, 256),), -0.2, 0.2), 0.0, 64.0)
    point_weights = jnp.clip(jnp.exp(math.log(0.05) - 2.3025851 * jax.random.uniform(streams_of[3], (POINTS,), jnp.float32) ** level_of(streams_of[3], (POINTS,), ((0, 256),), -0.2, 0.2)), 0.005, 0.05)
    batch_blocks = different_ones(streams_of[4], BATCHES, UB, BB, 0)
    tile_owner_keys = jax.random.split(jax.random.fold_in(streams_of[5], 1), REQS // R)
    tile_owner_turns = jax.random.permutation(jax.random.fold_in(streams_of[5], 3), REQS // R)
    tile_owner = jax.vmap(lambda own, number: deal_out(jax.random.fold_in(streams_of[5], 2), own, number, R, OWNERS, 1, CAP, 1))(tile_owner_keys, tile_owner_turns).reshape((REQS, 1))
    tile_slot = with_ends(jax.random.randint(streams_of[6], (REQS,), 0, TILE_DEV), jax.random.fold_in(streams_of[6], 1), 0, TILE_DEV - 1).astype(jnp.int32)
    batch_atoms = different_ones(streams_of[7], BATCHES, ATOM_GRP, NEAR, 0)
    batch_weights = with_ends(jax.random.randint(streams_of[8], (BATCHES, NEAR), 1, 9), jax.random.fold_in(streams_of[8], 1), 1, 8).astype(jnp.int32)
    atom_grid_index = with_ends(jax.random.randint(streams_of[9], (3, ATOMS), 0, GRIDN), jax.random.fold_in(streams_of[9], 1), 0, GRIDN - 1).astype(jnp.int32)
    return dict(orbitals=orbitals, dens_tiles=dens_tiles, point_coords=point_coords, point_weights=point_weights, batch_blocks=batch_blocks, tile_owner=tile_owner, tile_slot=tile_slot, batch_atoms=batch_atoms, batch_weights=batch_weights, atom_grid_index=atom_grid_index)


TOP_PRECISION = lax.Precision.HIGHEST


def wave_table(count):
    mode_ids = jnp.arange(count // 2, dtype=jnp.int32)
    return jnp.stack([mode_ids % 8, (mode_ids // 8) % 8, mode_ids // 64]).astype(jnp.float32)


def kernel_gains(count):
    wave_vecs = wave_table(count)
    squared = jnp.sum(wave_vecs * wave_vecs, axis=0)
    near_gain = 0.1 / (1.0 + 0.1 * squared)
    far_gain = 0.03 / (1.0 + 0.1 * squared)
    return jnp.concatenate([near_gain, near_gain]), jnp.concatenate([far_gain, far_gain])


def local_basis(coords, centre_points, wave_vecs, grid_extent):
    displace = coords[:, :, None, :] - centre_points[:, :, :, None]
    phases = jnp.einsum("cbnp,cm->bnpm", displace, wave_vecs, precision=TOP_PRECISION) * (2.0 * math.pi / grid_extent)
    envelope = jnp.exp(-2.0 * jnp.sum(displace * displace, axis=0) / (grid_extent * grid_extent))
    return envelope[..., None] * jnp.concatenate([jnp.cos(phases), jnp.sin(phases)], axis=-1)


def wave_values(coords, wave_vecs, grid_extent):
    phases = jnp.einsum("cbp,cm->bpm", coords, wave_vecs, precision=TOP_PRECISION) * (2.0 * math.pi / grid_extent)
    return jnp.concatenate([jnp.cos(phases), jnp.sin(phases)], axis=-1)


def reference(orbitals, dens_tiles, point_coords, point_weights, batch_blocks, tile_owner, tile_slot, batch_atoms, batch_weights, atom_grid_index):
    devices = N_GRP * N_DEV
    wave_vecs = wave_table(KM)
    near_gain, far_gain = kernel_gains(KM)
    atom_location = atom_grid_index.astype(jnp.float32)
    group_of = jnp.arange(devices, dtype=jnp.int32) // N_DEV
    tile_index = (group_of[:, None] * (TILE_DEV * N_DEV) + tile_owner[:, 0].reshape(devices, R) * TILE_DEV
                  + tile_slot.reshape(devices, R)).astype(jnp.int32)
    orbital_dev = orbitals.reshape(devices, BAT_DEV, PTS, BORB)
    coord_dev = point_coords.reshape(3, devices, BAT_DEV, PTS)
    weight_dev = point_weights.reshape(devices, BAT_DEV, PTS)
    block_dev = batch_blocks.reshape(devices, BAT_DEV, BB)
    atom_dev = (batch_atoms.reshape(devices, BAT_DEV, NEAR) + group_of[:, None, None] * ATOM_GRP).astype(jnp.int32)
    raw_weight = batch_weights.reshape(devices, BAT_DEV, NEAR).astype(jnp.float32)
    partition = raw_weight / jnp.sum(raw_weight, axis=2, keepdims=True)
    device_ids = jnp.arange(devices, dtype=jnp.int32)
    batch_ids = jnp.arange(BAT_DEV, dtype=jnp.int32)

    def basis_of(device):
        return local_basis(coord_dev[:, device], atom_location[:, atom_dev[device]], wave_vecs, GRIDN)

    def density_pass(moments, device):
        local_tiles = dens_tiles[tile_index[device]]

        def one_batch(batch_no):
            orbital = orbital_dev[device, batch_no]
            chosen = block_dev[device, batch_no]
            block_index = chosen[:, None] * UB + chosen[None, :]
            dens_block = local_tiles[block_index].transpose(0, 2, 1, 3).reshape(BORB, BORB)
            product = jnp.dot(orbital, dens_block, preferred_element_type=jnp.float32)
            return jnp.sum(product * orbital.astype(jnp.float32), axis=1)

        density = lax.map(one_batch, batch_ids)
        ebasis = basis_of(device)
        coeffs = partition[device][:, :, None] * jnp.einsum("bp,bnpk->bnk", weight_dev[device] * density, ebasis, precision=TOP_PRECISION)
        moments = moments.at[atom_dev[device].reshape(-1)].add(coeffs.reshape(BAT_DEV * NEAR, KM))
        return moments, density

    moments, density_all = lax.scan(density_pass, jnp.zeros((ATOMS, KM), jnp.float32), device_ids)
    atom_trig = wave_values(atom_location[:, None, :], wave_vecs, GRIDN)[0]
    structure = jnp.dot(moments[:, 0], atom_trig, precision=TOP_PRECISION)
    coef_near = near_gain[None, :] * moments
    far_coef = far_gain * structure

    def hamilton_pass(ham_sum, device):
        ebasis = basis_of(device)
        chosen_coef = coef_near[atom_dev[device]]
        near_val = jnp.sum(partition[device][:, :, None] * jnp.einsum("bnpk,bnk->bnp", ebasis, chosen_coef, precision=TOP_PRECISION), axis=1)
        far_val = jnp.einsum("bpk,k->bp", wave_values(coord_dev[:, device], wave_vecs, GRIDN), far_coef, precision=TOP_PRECISION)
        potential = near_val + far_val
        scaled_pot = weight_dev[device] * potential

        def one_batch(ham_local, batch_no):
            orbital = orbital_dev[device, batch_no]
            chosen = block_dev[device, batch_no]
            scaled_orb = (scaled_pot[batch_no][:, None] * orbital.astype(jnp.float32)).astype(jnp.bfloat16)
            ham_batch = lax.dot_general(orbital, scaled_orb, (((0,), (0,)), ((), ())), preferred_element_type=jnp.float32)
            pieces = ham_batch.reshape(BB, TB, BB, TB).transpose(0, 2, 1, 3).reshape(BB * BB, TB, TB)
            block_index = (chosen[:, None] * UB + chosen[None, :]).reshape(-1)
            return ham_local.at[block_index].add(pieces), None

        ham_local, unused = lax.scan(one_batch, jnp.zeros((R, TB, TB), jnp.float32), batch_ids)
        rounded = lax.optimization_barrier(ham_local.astype(jnp.bfloat16)).astype(jnp.float32)
        return ham_sum.at[tile_index[device]].add(rounded), potential

    ham_sum, potential_all = lax.scan(hamilton_pass, jnp.zeros((TILES, TB, TB), jnp.float32), device_ids)
    return density_all.reshape(-1), potential_all.reshape(-1), ham_sum.astype(jnp.bfloat16)
```

```python
import math

import jax
import jax.numpy as jnp
from jax import lax
from jax.experimental import pallas as pl
from jax.experimental.pallas import tpu as pltpu
from jax.sharding import PartitionSpec as P

TB = 128
BB = 8
UB = 9
R = 81
PTS = 256
BAT_DEV = 2
KM = 512
HALF = KM // 2
NEAR = 4
TILE_DEV = 32
GRIDN = 64
ATOM_GRP = 16
DEV_PTS = BAT_DEV * PTS
LISTERS = 4
LIST_PTS = LISTERS * DEV_PTS
NO_TILE = 4 * TILE_DEV
GROUP = 4
LIST_LEN = 96
VMEM_BYTES = 56 * 1024 * 1024

F32 = jnp.float32
BF16 = jnp.bfloat16
TOP_PRECISION = lax.Precision.HIGHEST
NT = (((1,), (1,)), ((), ()))


def swap(array, bits):
    return lax.ppermute(array, "dev", [(d, d ^ bits) for d in range(16)])


def swap_grp(array, bits):
    return lax.ppermute(array, "grp", [(g, g ^ bits) for g in range(16)])


X1, Y1 = 1, 4
X3, Y3 = 3, 12


def wave_table(count):
    mode_ids = jnp.arange(count // 2, dtype=jnp.int32)
    return jnp.stack([mode_ids % 8, mode_ids // 8 % 8, mode_ids // 64]).astype(F32)


def split_bf16(value):
    high = value.astype(BF16)
    return high, (value - high.astype(F32)).astype(BF16)


def wave_kernel(cs_ref, high_ref, low_ref):
    cos_x, sin_x = cs_ref[0:8], cs_ref[8:16]
    for fz in range(4):
        cos_z, sin_z = cs_ref[32 + fz : 33 + fz], cs_ref[40 + fz : 41 + fz]
        for fy in range(0, 8, 2):
            parts_cos, parts_sin = [], []
            for step in range(2):
                cos_y = cs_ref[16 + fy + step : 17 + fy + step]
                sin_y = cs_ref[24 + fy + step : 25 + fy + step]
                cos_yz = cos_y * cos_z - sin_y * sin_z
                sin_yz = sin_y * cos_z + cos_y * sin_z
                parts_cos.append(cos_x * cos_yz - sin_x * sin_yz)
                parts_sin.append(sin_x * cos_yz + cos_x * sin_yz)
            row = fz * 64 + fy * 8
            for base, parts in ((row, parts_cos), (HALF + row, parts_sin)):
                high, low = split_bf16(jnp.concatenate(parts, axis=0))
                high_ref[base : base + 16] = high
                low_ref[base : base + 16] = low


def wave_of_points(coords):
    points = coords.shape[1]
    chunk = 256
    angle = (jnp.arange(8, dtype=F32)[None, :, None] * coords[:, None, :]) * (2.0 * math.pi / GRIDN)
    cs = jnp.stack([jnp.cos(angle), jnp.sin(angle)], axis=1).reshape(48, points)
    out = jax.ShapeDtypeStruct((KM, points), BF16)
    return pl.pallas_call(
        wave_kernel,
        grid=(points // chunk,),
        in_specs=[pl.BlockSpec((48, chunk), lambda i: (0, i))],
        out_specs=[pl.BlockSpec((KM, chunk), lambda i: (0, i))] * 2,
        out_shape=[out, out],
        cost_estimate=pl.CostEstimate(flops=8 * KM * points, bytes_accessed=4 * KM * points, transcendentals=0),
    )(cs)


def list_kernel(tmap_ref, codes_ref, counts_ref):
    for e in range(LISTERS):

        def look(row, state):
            r, count = state

            def column(col, state):
                r, count = state
                tile = tmap_ref[e, r]
                codes_ref[e, count] = tile + row * 256 + col * 4096
                return r + 1, count + jnp.where(tile < NO_TILE, 1, 0)

            return lax.fori_loop(0, UB, column, (r, count))

        r, count = lax.fori_loop(0, UB, look, (0, 0))
        for step in range(GROUP):
            codes_ref[e, count + step] = NO_TILE
        counts_ref[e] = (count + GROUP - 1) // GROUP


def lists_of(tmap):
    smem = pl.BlockSpec(memory_space=pltpu.SMEM)
    return pl.pallas_call(
        list_kernel,
        in_specs=[smem],
        out_specs=[smem, smem],
        out_shape=[
            jax.ShapeDtypeStruct((LISTERS, LIST_LEN), jnp.int32),
            jax.ShapeDtypeStruct((LISTERS,), jnp.int32),
        ],
        cost_estimate=pl.CostEstimate(flops=4000, bytes_accessed=4000, transcendentals=0),
    )(tmap)


def density_kernel(
    tmap_ref,
    blocks_ref,
    own_tile,
    x_tile,
    y_tile,
    low_tile,
    high_tile,
    own_orb,
    x_orb,
    y_orb,
    first_orb,
    second_orb,
    spread_ref,
    weights_ref,
    high_ref,
    low_ref,
    trig_ref,
    out_ref,
    tiles,
    orbs,
    density,
    sems,
):
    copies = [
        pltpu.make_async_copy(own_tile, tiles.at[0:32], sems.at[0]),
        pltpu.make_async_copy(x_tile, tiles.at[32:64], sems.at[1]),
        pltpu.make_async_copy(y_tile, tiles.at[64:96], sems.at[2]),
        pltpu.make_async_copy(low_tile, tiles.at[96:112], sems.at[3]),
        pltpu.make_async_copy(high_tile, tiles.at[112:128], sems.at[4]),
        pltpu.make_async_copy(own_orb, orbs.at[0:2], sems.at[5]),
        pltpu.make_async_copy(x_orb, orbs.at[2:4], sems.at[6]),
        pltpu.make_async_copy(y_orb, orbs.at[4:6], sems.at[7]),
        pltpu.make_async_copy(first_orb, orbs.at[6], sems.at[8]),
        pltpu.make_async_copy(second_orb, orbs.at[7], sems.at[9]),
    ]
    for copy in copies:
        copy.start()
    tiles[NO_TILE] = jnp.zeros((TB, TB), BF16)
    for copy in copies:
        copy.wait()

    def one_batch(batch, unused):
        lister = batch // BAT_DEV
        chosen = [blocks_ref[batch, i] for i in range(BB)]
        total = jnp.zeros((PTS, TB), F32)
        for pair in range(BB // 2):
            columns = []
            for j in (2 * pair, 2 * pair + 1):
                columns.append(
                    jnp.concatenate([tiles[tmap_ref[lister, chosen[i] * UB + chosen[j]]] for i in range(BB)], axis=0)
                )
            product = jnp.dot(orbs[batch], jnp.concatenate(columns, axis=1), preferred_element_type=F32)
            for side in range(2):
                block = orbs[batch, :, (2 * pair + side) * TB : (2 * pair + side + 1) * TB]
                total = total + product[:, side * TB : (side + 1) * TB] * block.astype(F32)
        density[pl.ds(batch, 1), :] = jnp.sum(total.T, axis=0, keepdims=True)
        return unused

    lax.fori_loop(0, LISTERS * BAT_DEV, one_batch, 0)
    weighted = density[...] * weights_ref[...]
    charge = jnp.concatenate(
        [spread_ref[:, b * PTS : (b + 1) * PTS] * weighted[b : b + 1] for b in range(LISTERS * BAT_DEV)], axis=1
    )
    charge_high, charge_low = split_bf16(charge)
    both = lax.dot_general(
        jnp.concatenate([charge_high, charge_low], axis=0), high_ref[...], NT, preferred_element_type=F32
    )
    sums = both[:ATOM_GRP] + both[ATOM_GRP:]
    sums = sums + lax.dot_general(charge_high, low_ref[...], NT, preferred_element_type=F32)
    cos_sum, sin_sum = sums[:, :HALF], sums[:, HALF:]
    cos_atom, sin_atom = trig_ref[:, :HALF], trig_ref[:, HALF:]
    out_ref[0:ATOM_GRP, :HALF] = cos_sum * cos_atom + sin_sum * sin_atom
    out_ref[0:ATOM_GRP, HALF:] = sin_sum * cos_atom - cos_sum * sin_atom
    for e in range(LISTERS):
        for b in range(BAT_DEV):
            out_ref[ATOM_GRP + e : ATOM_GRP + e + 1, b * PTS : (b + 1) * PTS] = density[
                BAT_DEV * e + b : BAT_DEV * e + b + 1
            ]
    out_ref[ATOM_GRP + LISTERS :] = jnp.zeros((8 - LISTERS, KM), F32)


def density_and_moments(tmap, blocks, tiles, orbs, spread, weights, wave_high, wave_low, trig):
    smem = pl.BlockSpec(memory_space=pltpu.SMEM)
    vmem = pl.BlockSpec(memory_space=pltpu.VMEM)
    hbm = pl.BlockSpec(memory_space=pl.ANY)
    return pl.pallas_call(
        density_kernel,
        in_specs=[smem, smem] + [hbm] * 10 + [vmem] * 5,
        out_specs=vmem,
        out_shape=jax.ShapeDtypeStruct((ATOM_GRP + 8, KM), F32),
        scratch_shapes=[
            pltpu.VMEM((NO_TILE + 1, TB, TB), BF16),
            pltpu.VMEM((LISTERS * BAT_DEV, PTS, BB * TB), BF16),
            pltpu.VMEM((LISTERS * BAT_DEV, PTS), F32),
            pltpu.SemaphoreType.DMA((10,)),
        ],
        compiler_params=pltpu.CompilerParams(vmem_limit_bytes=VMEM_BYTES),
        cost_estimate=pl.CostEstimate(flops=5 * 10**9, bytes_accessed=12 * 2**20, transcendentals=0),
    )(tmap, blocks, *tiles, *orbs, spread, weights, wave_high, wave_low, trig)


def ham_kernel(
    codes_ref,
    counts_ref,
    blocks_ref,
    own_orb,
    x_orb,
    y_orb,
    first_orb,
    second_orb,
    moments_ref,
    far_ref,
    near_ref,
    trig_ref,
    spread_ref,
    weights_ref,
    high_ref,
    low_ref,
    pot_ref,
    own_ref,
    x_ref,
    y_ref,
    diag_ref,
    ham,
    orbs,
    turned,
    scaled,
    sems,
):
    copies = []
    for batch in range(LISTERS * BAT_DEV):
        e, b = batch // BAT_DEV, batch % BAT_DEV
        source = (own_orb.at[b], x_orb.at[b], y_orb.at[b], (first_orb, second_orb)[b])[e]
        some = []
        missing = UB * (UB - 1) // 2
        for i in range(BB):
            block = blocks_ref[batch, i]
            missing = missing - block
            some.append(
                pltpu.make_async_copy(
                    source.at[:, i * TB : (i + 1) * TB],
                    orbs.at[e, block, b * PTS : (b + 1) * PTS, :],
                    sems.at[batch, i],
                )
            )
        for copy in some:
            copy.start()
        orbs[e, missing, b * PTS : (b + 1) * PTS, :] = jnp.zeros((PTS, TB), BF16)
        copies.append(some)

    cos_atom, sin_atom = trig_ref[:, :HALF], trig_ref[:, HALF:]
    cos_near = moments_ref[:, :HALF] * near_ref[:, :HALF]
    sin_near = moments_ref[:, HALF:] * near_ref[:, HALF:]
    turned_cos = cos_near * cos_atom - sin_near * sin_atom
    turned_sin = cos_near * sin_atom + sin_near * cos_atom
    coef = jnp.concatenate(
        [
            jnp.concatenate([turned_cos, turned_sin], axis=1),
            jnp.concatenate([far_ref[...], jnp.zeros((ATOM_GRP - 1, KM), F32)], axis=0),
        ],
        axis=0,
    )
    coef_high, coef_low = split_bf16(coef)
    both = jnp.dot(jnp.concatenate([coef_high, coef_low], axis=0), high_ref[...], preferred_element_type=F32)
    values = both[: 2 * ATOM_GRP] + both[2 * ATOM_GRP :]
    values = values + jnp.dot(coef_high, low_ref[...], preferred_element_type=F32)
    pot = jnp.sum(values[:ATOM_GRP] * spread_ref[...], axis=0, keepdims=True) + values[ATOM_GRP : ATOM_GRP + 1]
    pot_ref[...] = pot[:, :DEV_PTS]
    scale = pot * weights_ref[...]

    def clear(t, unused):
        ham[t] = jnp.zeros((TB, TB), F32)
        return unused

    lax.fori_loop(0, NO_TILE, clear, 0)
    for e in range(LISTERS):
        for b in range(BAT_DEV):
            for copy in copies[BAT_DEV * e + b]:
                copy.wait()
        for part in range(DEV_PTS // TB):
            at = e * DEV_PTS + part * TB
            factor = jnp.broadcast_to(scale[:, at : at + TB], (TB, TB)).T
            for block in range(UB):
                piece = orbs[e, block, part * TB : (part + 1) * TB, :]
                scaled[block, part * TB : (part + 1) * TB, :] = (factor * piece.astype(F32)).astype(BF16)
                turned[block, :, part * TB : (part + 1) * TB] = piece.T

        def some_items(step, unused):
            for item in range(GROUP):
                code = codes_ref[e, step * GROUP + item]
                tile = code & 255
                i = (code >> 8) & 15
                j = code >> 12
                ham[tile] += jnp.dot(turned[i], scaled[j], preferred_element_type=F32)
            return unused

        lax.fori_loop(0, counts_ref[e], some_items, 0)
    own_ref[...] = ham[0:32]
    x_ref[...] = ham[32:64].astype(BF16)
    y_ref[...] = ham[64:96].astype(BF16)
    diag_ref[...] = ham[96:128].astype(BF16)


def potential_and_ham(codes, counts, blocks, orbs, moments, far, near, trig, spread, weights, wave_high, wave_low):
    smem = pl.BlockSpec(memory_space=pltpu.SMEM)
    vmem = pl.BlockSpec(memory_space=pltpu.VMEM)
    hbm = pl.BlockSpec(memory_space=pl.ANY)
    part = jax.ShapeDtypeStruct((TILE_DEV, TB, TB), BF16)
    return pl.pallas_call(
        ham_kernel,
        in_specs=[smem] * 3 + [hbm] * 5 + [vmem] * 8,
        out_specs=[vmem] * 5,
        out_shape=[
            jax.ShapeDtypeStruct((1, DEV_PTS), F32),
            jax.ShapeDtypeStruct((TILE_DEV, TB, TB), F32),
            part,
            part,
            part,
        ],
        scratch_shapes=[
            pltpu.VMEM((NO_TILE + 1, TB, TB), F32),
            pltpu.VMEM((LISTERS, UB, DEV_PTS, TB), BF16),
            pltpu.VMEM((UB, TB, DEV_PTS), BF16),
            pltpu.VMEM((UB, DEV_PTS, TB), BF16),
            pltpu.SemaphoreType.DMA((LISTERS * BAT_DEV, BB)),
        ],
        compiler_params=pltpu.CompilerParams(vmem_limit_bytes=VMEM_BYTES),
        cost_estimate=pl.CostEstimate(flops=4 * 10**9, bytes_accessed=16 * 2**20, transcendentals=0),
    )(codes, counts, blocks, *orbs, moments, far, near, trig, spread, weights, wave_high, wave_low)


def on_device(
    orbitals,
    dens_tiles,
    point_coords,
    point_weights,
    batch_blocks,
    tile_owner,
    tile_slot,
    batch_atoms,
    batch_weights,
    atom_grid_index,
):
    me = lax.axis_index("dev").astype(jnp.int32)
    ints = jnp.concatenate(
        [tile_owner[:, 0], tile_slot, batch_blocks.reshape(-1), batch_atoms.reshape(-1), batch_weights.reshape(-1)]
    )
    facts = jnp.concatenate(
        [point_coords, point_weights[None], jnp.pad(ints, (0, DEV_PTS - ints.shape[0])).astype(F32)[None]], axis=0
    )
    half = TILE_DEV // 2
    facts_x, facts_y, facts_diag = swap(facts, X3), swap(facts, Y3), swap(facts, X3 ^ Y3)
    tile_x, tile_y = swap(dens_tiles, X1), swap(dens_tiles, Y1)
    orb_x, orb_y = swap(orbitals, X3), swap(orbitals, Y3)
    tile_low, tile_high = swap(tile_y[:half], X1), swap(tile_x[half:], Y1)
    orb_first, orb_second = swap(orb_y[0], X3), swap(orb_x[1], Y3)

    facts = jnp.stack([facts, facts_x, facts_y, facts_diag], axis=1)
    coords = facts[:3].reshape(3, LIST_PTS)
    weights = facts[3].reshape(LISTERS * BAT_DEV, PTS)
    ints = facts[4].astype(jnp.int32)
    owners, slots = ints[:, :R], ints[:, R : 2 * R]
    at = 2 * R
    blocks = ints[:, at : at + BAT_DEV * BB].reshape(LISTERS * BAT_DEV, BB)
    at = at + BAT_DEV * BB
    atoms = ints[:, at : at + BAT_DEV * NEAR].reshape(LISTERS * BAT_DEV, NEAR)
    at = at + BAT_DEV * NEAR
    raw_weight = facts[4][:, at : at + BAT_DEV * NEAR].reshape(LISTERS * BAT_DEV, NEAR)
    away = owners ^ me
    tmap = jnp.where((away & 10) == 0, ((away & 1) + ((away >> 2) & 1) * 2) * TILE_DEV + slots, NO_TILE)

    wave_vecs = wave_table(KM)
    squared = jnp.sum(wave_vecs * wave_vecs, axis=0)
    near_gain = jnp.tile(0.1 / (1.0 + 0.1 * squared), 2)[None]
    far_gain = jnp.tile(0.03 / (1.0 + 0.1 * squared), 2)[None]
    location = atom_grid_index.astype(F32)
    phases = jnp.einsum("ca,cm->am", location, wave_vecs, precision=TOP_PRECISION) * (2.0 * math.pi / GRIDN)
    trig = jnp.concatenate([jnp.cos(phases), jnp.sin(phases)], axis=1)
    partition = raw_weight / jnp.sum(raw_weight, axis=1, keepdims=True)
    share = jnp.sum(
        jnp.where(
            atoms[None] == jnp.arange(ATOM_GRP, dtype=jnp.int32)[:, None, None],
            partition[None],
            0.0,
        ),
        axis=2,
    )
    displace = coords[:, None, :] - location[:, :, None]
    envelope = jnp.exp(-2.0 * jnp.sum(displace * displace, axis=0) / (GRIDN * GRIDN))
    spread = (envelope.reshape(ATOM_GRP, LISTERS * BAT_DEV, PTS) * share[:, :, None]).reshape(ATOM_GRP, LIST_PTS)
    wave_high, wave_low = wave_of_points(coords)
    codes, counts = lists_of(tmap)

    orbs = (orbitals, orb_x, orb_y, orb_first, orb_second)
    part = density_and_moments(
        tmap,
        blocks,
        (dens_tiles, tile_x, tile_y, tile_low, tile_high),
        orbs,
        spread,
        weights,
        wave_high,
        wave_low,
        trig,
    )
    a = ATOM_GRP
    got = swap(part, X3)
    part = part + jnp.concatenate([got[:a], got[a + 1 : a + 2], got[a : a + 1], got[a + 3 : a + 4], got[a + 2 : a + 3], got[a + 4 :]], axis=0)
    got = swap(part, Y3)
    density = part[a] + got[a + 2]
    moments = part[:a] + got[:a]
    moments = moments + swap(moments, X1)
    moments = moments + swap(moments, Y1)
    structure = jnp.sum(moments[:, :1] * trig, axis=0, keepdims=True)
    for bits in (1, 2, 4, 8):
        structure = structure + swap_grp(structure, bits)

    potential, own, part_x, part_y, part_diag = potential_and_ham(
        codes,
        counts,
        blocks,
        orbs,
        moments,
        far_gain * structure,
        near_gain,
        trig,
        spread,
        weights.reshape(1, LIST_PTS),
        wave_high,
        wave_low,
    )
    low_y = swap(part_diag[:half], X1)
    high_x = swap(part_diag[half:], Y1)
    low_x = swap(part_x[:half], X1)
    high_y = swap(part_y[half:], Y1)
    high_x = swap((part_x[half:].astype(F32) + high_x.astype(F32)).astype(BF16), X1)
    low_y = swap((part_y[:half].astype(F32) + low_y.astype(F32)).astype(BF16), Y1)
    low = own[:half] + low_x.astype(F32) + low_y.astype(F32)
    high = own[half:] + high_x.astype(F32) + high_y.astype(F32)
    return (density, potential.reshape(-1), jnp.concatenate([low, high], axis=0).astype(BF16))


def solution(mesh):
    in_specs = (
        P(("grp", "dev"), None, None),
        P(("grp", "dev"), None, None),
        P(None, ("grp", "dev")),
        P(("grp", "dev")),
        P(("grp", "dev"), None),
        P(("grp", "dev"), None),
        P(("grp", "dev")),
        P(("grp", "dev"), None),
        P(("grp", "dev"), None),
        P(None, "grp"),
    )
    out_specs = (P(("grp", "dev")), P(("grp", "dev")), P(("grp", "dev"), None, None))
    return jax.shard_map(
        on_device, mesh=mesh, in_specs=in_specs, out_specs=out_specs, check_vma=False
    )
```

```python
import math

import jax
import jax.numpy as jnp
from jax import lax
from jax.experimental import pallas as pl
from jax.experimental.pallas import tpu as pltpu
from jax.sharding import PartitionSpec as P

TB = 128
BB = 8
UB = 9
R = 81
PTS = 256
BAT_DEV = 2
KM = 512
HALF = KM // 2
NEAR = 4
TILE_DEV = 32
GRIDN = 64
ATOM_GRP = 16
DEV_PTS = BAT_DEV * PTS
LISTERS = 4
LIST_PTS = LISTERS * DEV_PTS
NO_TILE = 4 * TILE_DEV
PARTS = TILE_DEV + 2 * (TILE_DEV // 2)
GROUP = 4
LIST_LEN = 32
MIB = 1024 * 1024

F32 = jnp.float32
BF16 = jnp.bfloat16
TOP_PRECISION = lax.Precision.HIGHEST
NT = (((1,), (1,)), ((), ()))


def swap(array, bits):
    return lax.ppermute(array, "dev", [(d, d ^ bits) for d in range(16)])


def swap_grp(array, bits):
    return lax.ppermute(array, "grp", [(g, g ^ bits) for g in range(16)])


X1, Y1 = 1, 4
X3, Y3 = 3, 12
XY = 5


def wave_table(count):
    mode_ids = jnp.arange(count // 2, dtype=jnp.int32)
    return jnp.stack([mode_ids % 8, mode_ids // 8 % 8, mode_ids // 64]).astype(F32)


def split_bf16(value):
    high = value.astype(BF16)
    return high, (value - high.astype(F32)).astype(BF16)


def wave_kernel(cs_ref, high_ref, low_ref):
    cos_x, sin_x = cs_ref[0:8], cs_ref[8:16]
    for fz in range(4):
        cos_z, sin_z = cs_ref[32 + fz : 33 + fz], cs_ref[40 + fz : 41 + fz]
        for fy in range(0, 8, 2):
            parts_cos, parts_sin = [], []
            for step in range(2):
                cos_y = cs_ref[16 + fy + step : 17 + fy + step]
                sin_y = cs_ref[24 + fy + step : 25 + fy + step]
                cos_yz = cos_y * cos_z - sin_y * sin_z
                sin_yz = sin_y * cos_z + cos_y * sin_z
                parts_cos.append(cos_x * cos_yz - sin_x * sin_yz)
                parts_sin.append(sin_x * cos_yz + cos_x * sin_yz)
            row = fz * 64 + fy * 8
            for base, parts in ((row, parts_cos), (HALF + row, parts_sin)):
                high, low = split_bf16(jnp.concatenate(parts, axis=0))
                high_ref[base : base + 16] = high
                low_ref[base : base + 16] = low


def wave_of_points(coords):
    points = coords.shape[1]
    chunk = 256
    angle = (jnp.arange(8, dtype=F32)[None, :, None] * coords[:, None, :]) * (2.0 * math.pi / GRIDN)
    cs = jnp.stack([jnp.cos(angle), jnp.sin(angle)], axis=1).reshape(48, points)
    out = jax.ShapeDtypeStruct((KM, points), BF16)
    return pl.pallas_call(
        wave_kernel,
        grid=(points // chunk,),
        in_specs=[pl.BlockSpec((48, chunk), lambda i: (0, i))],
        out_specs=[pl.BlockSpec((KM, chunk), lambda i: (0, i))] * 2,
        out_shape=[out, out],
        cost_estimate=pl.CostEstimate(flops=8 * KM * points, bytes_accessed=4 * KM * points, transcendentals=0),
    )(cs)


def orbital_copies(own_orb, x_orb, y_orb, diag_orbs, orbs, sems):
    return [
        [pltpu.make_async_copy(own_orb, orbs.at[0:2], sems.at[0])],
        [pltpu.make_async_copy(x_orb, orbs.at[2:4], sems.at[1])],
        [pltpu.make_async_copy(y_orb, orbs.at[4:6], sems.at[2])],
        [
            pltpu.make_async_copy(orb, orbs.at[6 + b] if len(diag_orbs) > 1 else orbs.at[6:8], sems.at[3 + b])
            for b, orb in enumerate(diag_orbs)
        ],
    ]


def density_kernel(
    tmap_ref,
    blocks_ref,
    own_tile,
    x_tile,
    y_tile,
    low_tile,
    high_tile,
    own_orb,
    x_orb,
    y_orb,
    first_orb,
    second_orb,
    spread_ref,
    weights_ref,
    high_hbm,
    low_hbm,
    trig_ref,
    out_ref,
    tiles,
    orbs,
    density,
    high_ref,
    low_ref,
    sems,
):
    half = TILE_DEV // 2
    arrivals = [
        pltpu.make_async_copy(source, tiles.at[at : at + source.shape[0]], sems.at[n])
        for n, (source, at) in enumerate(
            (
                (own_tile, 0),
                (x_tile, TILE_DEV),
                (y_tile, 2 * TILE_DEV),
                (low_tile, 3 * TILE_DEV),
                (high_tile, 3 * TILE_DEV + half),
            )
        )
    ]
    waves = [
        pltpu.make_async_copy(high_hbm, high_ref, sems.at[5]),
        pltpu.make_async_copy(low_hbm, low_ref, sems.at[6]),
    ]
    points = orbital_copies(own_orb, x_orb, y_orb, (first_orb, second_orb), orbs, sems.at[7:12])
    for copy in arrivals + sum(points, []) + waves:
        copy.start()
    tiles[NO_TILE] = jnp.zeros((TB, TB), BF16)
    for copy in arrivals:
        copy.wait()
    for lister in range(LISTERS):
        for copy in points[lister]:
            copy.wait()

        def one_batch(batch, unused, lister=lister):
            chosen = [blocks_ref[batch, i] for i in range(BB)]
            total = jnp.zeros((PTS, TB), F32)
            for pair in range(BB // 2):
                columns = []
                for j in (2 * pair, 2 * pair + 1):
                    columns.append(
                        jnp.concatenate(
                            [tiles[tmap_ref[lister, chosen[i] * UB + chosen[j]]] for i in range(BB)], axis=0
                        )
                    )
                product = jnp.dot(orbs[batch], jnp.concatenate(columns, axis=1), preferred_element_type=F32)
                for side in range(2):
                    block = orbs[batch, :, (2 * pair + side) * TB : (2 * pair + side + 1) * TB]
                    total = total + product[:, side * TB : (side + 1) * TB] * block.astype(F32)
            density[pl.ds(batch, 1), :] = jnp.sum(total.T, axis=0, keepdims=True)
            return unused

        lax.fori_loop(BAT_DEV * lister, BAT_DEV * (lister + 1), one_batch, 0)
    for copy in waves:
        copy.wait()
    weighted = density[...] * weights_ref[...]
    charge = jnp.concatenate(
        [spread_ref[:, b * PTS : (b + 1) * PTS] * weighted[b : b + 1] for b in range(LISTERS * BAT_DEV)], axis=1
    )
    charge_high, charge_low = split_bf16(charge)
    both = lax.dot_general(
        jnp.concatenate([charge_high, charge_low], axis=0), high_ref[...], NT, preferred_element_type=F32
    )
    sums = both[:ATOM_GRP] + both[ATOM_GRP:]
    sums = sums + lax.dot_general(charge_high, low_ref[...], NT, preferred_element_type=F32)
    cos_sum, sin_sum = sums[:, :HALF], sums[:, HALF:]
    cos_atom, sin_atom = trig_ref[:, :HALF], trig_ref[:, HALF:]
    out_ref[0:ATOM_GRP, :HALF] = cos_sum * cos_atom + sin_sum * sin_atom
    out_ref[0:ATOM_GRP, HALF:] = sin_sum * cos_atom - cos_sum * sin_atom
    for e in range(LISTERS):
        for b in range(BAT_DEV):
            out_ref[ATOM_GRP + e : ATOM_GRP + e + 1, b * PTS : (b + 1) * PTS] = density[
                BAT_DEV * e + b : BAT_DEV * e + b + 1
            ]
    out_ref[ATOM_GRP + LISTERS :] = jnp.zeros((8 - LISTERS, KM), F32)


SMEM_SPEC = pl.BlockSpec(memory_space=pltpu.SMEM)
VMEM_SPEC = pl.BlockSpec(memory_space=pltpu.VMEM)
ANY_SPEC = pl.BlockSpec(memory_space=pl.ANY)


def density_and_moments(tmap, blocks, tiles, orbs, spread, weights, wave_high, wave_low, trig):
    return pl.pallas_call(
        density_kernel,
        in_specs=[SMEM_SPEC] * 2 + [ANY_SPEC] * 10 + [VMEM_SPEC] * 2 + [ANY_SPEC] * 2 + [VMEM_SPEC],
        out_specs=VMEM_SPEC,
        out_shape=jax.ShapeDtypeStruct((ATOM_GRP + 8, KM), F32),
        scratch_shapes=[
            pltpu.VMEM((NO_TILE + 1, TB, TB), BF16),
            pltpu.VMEM((LISTERS * BAT_DEV, PTS, BB * TB), BF16),
            pltpu.VMEM((LISTERS * BAT_DEV, PTS), F32),
            pltpu.VMEM((KM, LIST_PTS), BF16),
            pltpu.VMEM((KM, LIST_PTS), BF16),
            pltpu.SemaphoreType.DMA((12,)),
        ],
        compiler_params=pltpu.CompilerParams(vmem_limit_bytes=56 * MIB),
        cost_estimate=pl.CostEstimate(flops=10**6, bytes_accessed=10**4, transcendentals=0),
    )(tmap, blocks, *tiles, *orbs, spread, weights, wave_high, wave_low, trig)


def pack_kernel(coords, weights, owner, slot, blocks, atoms, shares, out_ref, owner_ref, slot_ref, blocks_ref, atoms_ref, shares_ref, sems):
    copies = [
        pltpu.make_async_copy(source, target, sems.at[n])
        for n, (source, target) in enumerate(
            (
                (coords, out_ref.at[0:3]),
                (weights, out_ref.at[3:4]),
                (owner, owner_ref),
                (slot, slot_ref),
                (blocks, blocks_ref),
                (atoms, atoms_ref),
                (shares, shares_ref),
            )
        )
    ]
    out_ref[4:6] = jnp.zeros((2, DEV_PTS), F32)
    for copy in copies:
        copy.start()
    for copy in copies:
        copy.wait()
    out_ref[4:5, :R] = owner_ref[...].astype(F32)
    out_ref[4:5, TB : TB + R] = slot_ref[...].astype(F32)
    for b in range(BAT_DEV):
        out_ref[4:5, (2 + b) * TB : (2 + b) * TB + BB] = blocks_ref[b : b + 1].astype(F32)
        out_ref[5:6, b * TB : b * TB + NEAR] = atoms_ref[b : b + 1].astype(F32)
        out_ref[5:6, (2 + b) * TB : (2 + b) * TB + NEAR] = shares_ref[b : b + 1].astype(F32)


def place_kernel(index_ref, out_ref):
    out_ref[...] = index_ref[...].astype(F32)


def atom_places(index):
    return pl.pallas_call(
        place_kernel,
        in_specs=[VMEM_SPEC],
        out_specs=VMEM_SPEC,
        out_shape=jax.ShapeDtypeStruct(index.shape, F32),
        cost_estimate=pl.CostEstimate(flops=2 * 10**10, bytes_accessed=1000, transcendentals=0),
    )(index)


def packed_facts(*parts):
    return pl.pallas_call(
        pack_kernel,
        in_specs=[ANY_SPEC] * 7,
        out_specs=VMEM_SPEC,
        out_shape=jax.ShapeDtypeStruct((6, DEV_PTS), F32),
        scratch_shapes=[pltpu.VMEM(part.shape, part.dtype) for part in parts[2:]] + [pltpu.SemaphoreType.DMA((7,))],
        compiler_params=pltpu.CompilerParams(vmem_limit_bytes=56 * MIB),
        cost_estimate=pl.CostEstimate(flops=1000, bytes_accessed=1000, transcendentals=0),
    )(*parts)


def add_ham(codes_ref, counts_ref, blocks_ref, copies, orbs, scale, ham, turned, scaled):
    for e in range(LISTERS):
        for copy in copies[e]:
            copy.wait()
        for b in range(BAT_DEV):
            source = orbs.at[BAT_DEV * e + b]
            factors = []
            for part in range(PTS // TB):
                at = e * DEV_PTS + b * PTS + part * TB
                factors.append(jnp.broadcast_to(scale[:, at : at + TB], (TB, TB)).T)
            missing = UB * (UB - 1) // 2
            for i in range(BB):
                block = blocks_ref[BAT_DEV * e + b, i]
                missing = missing - block
                turned[block, :, b * PTS : (b + 1) * PTS] = source[:, i * TB : (i + 1) * TB].T
                for part in range(PTS // TB):
                    piece = source[part * TB : (part + 1) * TB, i * TB : (i + 1) * TB]
                    rows = slice(b * PTS + part * TB, b * PTS + (part + 1) * TB)
                    scaled[block, rows, :] = (factors[part] * piece.astype(F32)).astype(BF16)
            scaled[missing, b * PTS : (b + 1) * PTS, :] = jnp.zeros((PTS, TB), BF16)
            turned[missing, :, b * PTS : (b + 1) * PTS] = jnp.zeros((TB, PTS), BF16)

        def some_items(step, unused):
            for item in range(GROUP):
                code = codes_ref[e, step * GROUP + item]
                tile = code & 255
                i = (code >> 8) & 15
                j = code >> 12
                ham[tile] += jnp.dot(turned[i], scaled[j], preferred_element_type=F32)
            return unused

        lax.fori_loop(0, counts_ref[e], some_items, 0)


def near_kernel(
    codes_ref,
    counts_ref,
    blocks_ref,
    own_orb,
    x_orb,
    y_orb,
    first_orb,
    second_orb,
    moments_ref,
    far_ref,
    near_ref,
    trig_ref,
    spread_ref,
    weights_ref,
    high_hbm,
    low_hbm,
    pot_ref,
    scale_ref,
    ham,
    turned,
    scaled,
    orbs,
    high_ref,
    low_ref,
    sems,
):
    waves = [
        pltpu.make_async_copy(high_hbm, high_ref, sems.at[5]),
        pltpu.make_async_copy(low_hbm, low_ref, sems.at[6]),
    ]
    copies = orbital_copies(own_orb, x_orb, y_orb, (first_orb, second_orb), orbs, sems)
    for copy in waves + sum(copies, []):
        copy.start()

    def clear(t, unused):
        ham[t] = jnp.zeros((TB, TB), F32)
        return unused

    lax.fori_loop(0, PARTS + 1, clear, 0)
    cos_atom, sin_atom = trig_ref[:, :HALF], trig_ref[:, HALF:]
    cos_near = moments_ref[:, :HALF] * near_ref[:, :HALF]
    sin_near = moments_ref[:, HALF:] * near_ref[:, HALF:]
    turned_cos = cos_near * cos_atom - sin_near * sin_atom
    turned_sin = cos_near * sin_atom + sin_near * cos_atom
    coef = jnp.concatenate(
        [
            jnp.concatenate([turned_cos, turned_sin], axis=1),
            jnp.concatenate([far_ref[...], jnp.zeros((ATOM_GRP - 1, KM), F32)], axis=0),
        ],
        axis=0,
    )
    coef_high, coef_low = split_bf16(coef)
    for copy in waves:
        copy.wait()
    both = jnp.dot(jnp.concatenate([coef_high, coef_low], axis=0), high_ref[...], preferred_element_type=F32)
    values = both[: 2 * ATOM_GRP] + both[2 * ATOM_GRP :]
    values = values + jnp.dot(coef_high, low_ref[...], preferred_element_type=F32)
    pot = jnp.sum(values[:ATOM_GRP] * spread_ref[...], axis=0, keepdims=True) + values[ATOM_GRP : ATOM_GRP + 1]
    pot_ref[...] = pot[:, :DEV_PTS]
    scale = pot * weights_ref[...]
    scale_ref[...] = scale
    add_ham(codes_ref, counts_ref, blocks_ref, copies, orbs, scale, ham, turned, scaled)


def potential_and_ham(codes, counts, blocks, orbs, moments, far, near, trig, spread, weights, wave_high, wave_low):
    return pl.pallas_call(
        near_kernel,
        in_specs=[SMEM_SPEC] * 3 + [ANY_SPEC] * 5 + [VMEM_SPEC] * 6 + [ANY_SPEC] * 2,
        out_specs=[VMEM_SPEC] * 3,
        out_shape=[
            jax.ShapeDtypeStruct((1, DEV_PTS), F32),
            jax.ShapeDtypeStruct((1, LIST_PTS), F32),
            jax.ShapeDtypeStruct((PARTS + 1, TB, TB), F32),
        ],
        scratch_shapes=[
            pltpu.VMEM((UB, TB, DEV_PTS), BF16),
            pltpu.VMEM((UB, DEV_PTS, TB), BF16),
            pltpu.VMEM((LISTERS * BAT_DEV, PTS, BB * TB), BF16),
            pltpu.VMEM((KM, LIST_PTS), BF16),
            pltpu.VMEM((KM, LIST_PTS), BF16),
            pltpu.SemaphoreType.DMA((7,)),
        ],
        compiler_params=pltpu.CompilerParams(vmem_limit_bytes=56 * MIB),
        cost_estimate=pl.CostEstimate(flops=10**6, bytes_accessed=10**4, transcendentals=0),
    )(codes, counts, blocks, *orbs, moments, far, near, trig, spread, weights, wave_high, wave_low)


def rest_kernel(
    codes_ref,
    counts_ref,
    blocks_ref,
    own_orb,
    x_orb,
    y_orb,
    diag_orb,
    scale_ref,
    start_ref,
    own_ref,
    x_ref,
    y_ref,
    ham,
    turned,
    scaled,
    orbs,
    sems,
):
    begin = pltpu.make_async_copy(start_ref, ham, sems.at[5])
    copies = orbital_copies(own_orb, x_orb, y_orb, (diag_orb,), orbs, sems)
    for copy in copies[0] + [begin] + sum(copies[1:], []):
        copy.start()
    copies[0].append(begin)
    add_ham(codes_ref, counts_ref, blocks_ref, copies, orbs, scale_ref[...], ham, turned, scaled)
    half = TILE_DEV // 2
    own_ref[...] = ham[:TILE_DEV]
    x_ref[...] = ham[TILE_DEV : TILE_DEV + half].astype(BF16)
    y_ref[...] = ham[TILE_DEV + half : PARTS].astype(BF16)


def rest_of_ham(codes, counts, blocks, orbs, scale, start):
    part = jax.ShapeDtypeStruct((TILE_DEV // 2, TB, TB), BF16)
    return pl.pallas_call(
        rest_kernel,
        in_specs=[SMEM_SPEC] * 3 + [ANY_SPEC] * 4 + [VMEM_SPEC, ANY_SPEC],
        out_specs=[VMEM_SPEC] * 3,
        out_shape=[jax.ShapeDtypeStruct((TILE_DEV, TB, TB), F32), part, part],
        scratch_shapes=[
            pltpu.VMEM((PARTS + 1, TB, TB), F32),
            pltpu.VMEM((UB, TB, DEV_PTS), BF16),
            pltpu.VMEM((UB, DEV_PTS, TB), BF16),
            pltpu.VMEM((LISTERS * BAT_DEV, PTS, BB * TB), BF16),
            pltpu.SemaphoreType.DMA((6,)),
        ],
        compiler_params=pltpu.CompilerParams(vmem_limit_bytes=56 * MIB),
        cost_estimate=pl.CostEstimate(flops=10**6, bytes_accessed=10**4, transcendentals=0),
    )(codes, counts, blocks, *orbs, scale, start)


def lists_of(owners, slots, me):
    half = TILE_DEV // 2
    away = owners ^ me
    mine = (away == 0) | ((away == X1) & (slots < half)) | ((away == Y1) & (slots >= half))
    places = jnp.where(away == 0, slots, TILE_DEV + slots)
    rows = jnp.arange(R, dtype=jnp.int32)
    codes = places + (rows // UB) * 256 + (rows % UB) * 4096
    before = (rows[:, None] < rows[None, :])[None] & mine[:, :, None]
    rank = jnp.sum(before.astype(jnp.int32), axis=1)
    counts = jnp.sum(mine.astype(jnp.int32), axis=1)
    at = jnp.arange(LIST_LEN, dtype=jnp.int32)
    hit = (rank[:, None, :] == at[None, :, None]) & mine[:, None, :]
    listed = jnp.sum(jnp.where(hit, codes[:, None, :], 0), axis=2)
    listed = jnp.where(at[None] < counts[:, None], listed, PARTS)
    return listed, (counts + GROUP - 1) // GROUP


def what_is_listed(rows):
    ints = rows.astype(jnp.int32)
    blocks = ints[:, 2 * TB :].reshape(LISTERS * BAT_DEV, TB)[:, :BB]
    return ints[:, :R], ints[:, TB : TB + R], blocks


def on_device(
    orbitals,
    dens_tiles,
    point_coords,
    point_weights,
    batch_blocks,
    tile_owner,
    tile_slot,
    batch_atoms,
    batch_weights,
    atom_grid_index,
):
    me = lax.axis_index("dev").astype(jnp.int32)

    facts = packed_facts(
        point_coords,
        point_weights[None],
        tile_owner.reshape(1, R),
        tile_slot[None],
        batch_blocks,
        batch_atoms,
        batch_weights,
    )
    facts = (facts, swap(facts, X3), swap(facts, Y3), swap(facts, X3 ^ Y3))
    location, sent, *facts = lax.optimization_barrier((atom_places(atom_grid_index), orbitals, *facts))
    half = TILE_DEV // 2
    tile_x, tile_y = swap(dens_tiles, X1), swap(dens_tiles, Y1)
    orb_x, orb_y = swap(sent, X3), swap(sent, Y3)
    tile_low, tile_high = swap(tile_y[:half], X1), swap(tile_x[half:], Y1)
    orb_first, orb_second = swap(orb_y[0], X3), swap(orb_x[1], Y3)
    orbs = (orbitals, orb_x, orb_y, orb_first, orb_second)

    facts = jnp.stack(facts)
    coords = facts[:, :3].transpose(1, 0, 2).reshape(3, LIST_PTS)
    weights = facts[:, 3].reshape(LISTERS * BAT_DEV, PTS)
    owners, slots, blocks = what_is_listed(facts[:, 4])
    near_by = facts[:, 5].reshape(LISTERS, 2, BAT_DEV, TB)[..., :NEAR].reshape(LISTERS, 2, BAT_DEV, NEAR)
    atoms = near_by[:, 0].reshape(LISTERS * BAT_DEV, NEAR).astype(jnp.int32)
    raw_weight = near_by[:, 1].reshape(LISTERS * BAT_DEV, NEAR)
    away = owners ^ me
    tmap = jnp.where((away & 10) == 0, ((away & 1) + ((away >> 2) & 1) * 2) * TILE_DEV + slots, NO_TILE)
    codes, counts = lists_of(owners, slots, me)

    wave_vecs = wave_table(KM)
    squared = jnp.sum(wave_vecs * wave_vecs, axis=0)
    near_gain = jnp.tile(0.1 / (1.0 + 0.1 * squared), 2)[None]
    far_gain = jnp.tile(0.03 / (1.0 + 0.1 * squared), 2)[None]
    phases = jnp.einsum("ca,cm->am", location, wave_vecs, precision=TOP_PRECISION) * (2.0 * math.pi / GRIDN)
    trig = jnp.concatenate([jnp.cos(phases), jnp.sin(phases)], axis=1)
    partition = raw_weight / jnp.sum(raw_weight, axis=1, keepdims=True)
    share = jnp.sum(
        jnp.where(
            atoms[None] == jnp.arange(ATOM_GRP, dtype=jnp.int32)[:, None, None],
            partition[None],
            0.0,
        ),
        axis=2,
    )
    displace = coords[:, None, :] - location[:, :, None]
    envelope = jnp.exp(-2.0 * jnp.sum(displace * displace, axis=0) / (GRIDN * GRIDN))
    spread = (envelope.reshape(ATOM_GRP, LISTERS * BAT_DEV, PTS) * share[:, :, None]).reshape(ATOM_GRP, LIST_PTS)
    wave_high, wave_low = wave_of_points(coords)
    early, late = (spread, weights, wave_high, wave_low, trig, codes, counts, tmap, blocks), orbitals
    early, late, *unused = lax.optimization_barrier((early, late, tile_low, tile_high, orb_first, orb_second))
    spread, weights, wave_high, wave_low, trig, codes, counts, tmap, blocks = early
    orb_far = swap(late, XY)

    part = density_and_moments(
        tmap,
        blocks,
        (dens_tiles, tile_x, tile_y, tile_low, tile_high),
        orbs,
        spread,
        weights,
        wave_high,
        wave_low,
        trig,
    )
    a = ATOM_GRP
    got = swap(part, X3)
    part = part + jnp.concatenate([got[:a], got[a + 1 : a + 2], got[a : a + 1], got[a + 3 : a + 4], got[a + 2 : a + 3], got[a + 4 :]])
    got = swap(part, Y3)
    density = part[a] + got[a + 2]
    moments, orb_far = lax.optimization_barrier((part[:a] + got[:a], orb_far))
    orb_far_x, orb_far_y = swap(orb_far, X3), swap(orb_far, Y3)
    got = swap(jnp.concatenate([moments, facts[:, 4]]), X1)
    moments = moments + got[:a]
    got = swap(jnp.concatenate([moments, got[a:]]), Y1)
    late_diag, moments = lax.optimization_barrier((jnp.stack([orb_first, orb_second]), moments + got[:a]))
    orbs_far = (orb_far, orb_far_x, orb_far_y, swap(late_diag, XY))
    far_owners, far_slots, far_blocks = what_is_listed(got[a:])
    far_codes, far_counts = lists_of(far_owners, far_slots, me)
    structure = jnp.sum(moments[:, :1] * trig, axis=0, keepdims=True)
    for bits in (1, 2, 4, 8):
        structure = structure + swap_grp(structure, bits)

    potential, scale, ham = potential_and_ham(
        codes,
        counts,
        blocks,
        orbs,
        moments,
        far_gain * structure,
        near_gain,
        trig,
        spread,
        weights.reshape(1, LIST_PTS),
        wave_high,
        wave_low,
    )
    own, part_x, part_y = rest_of_ham(
        far_codes, far_counts, far_blocks, orbs_far, swap(scale, XY), ham
    )
    low = own[:half] + swap(part_x, X1).astype(F32)
    high = own[half:] + swap(part_y, Y1).astype(F32)
    return (density, potential.reshape(-1), jnp.concatenate([low, high], axis=0).astype(BF16))


def solution(mesh):
    in_specs = (
        P(("grp", "dev"), None, None),
        P(("grp", "dev"), None, None),
        P(None, ("grp", "dev")),
        P(("grp", "dev")),
        P(("grp", "dev"), None),
        P(("grp", "dev"), None),
        P(("grp", "dev")),
        P(("grp", "dev"), None),
        P(("grp", "dev"), None),
        P(None, "grp"),
    )
    out_specs = (P(("grp", "dev")), P(("grp", "dev")), P(("grp", "dev"), None, None))
    return jax.shard_map(
        on_device, mesh=mesh, in_specs=in_specs, out_specs=out_specs, check_vma=False
    )
```

```python
import functools
import math

import jax
import jax.numpy as jnp
from jax import lax
from jax.experimental import pallas as pl
from jax.experimental.pallas import tpu as pltpu
from jax.sharding import PartitionSpec as P

TB = 128
BB = 8
UB = 9
R = 81
PTS = 256
BAT_DEV = 2
KM = 512
HALF = KM // 2
NEAR = 4
TILE_DEV = 32
GRIDN = 64
ATOM_GRP = 16
DEV_PTS = BAT_DEV * PTS
LISTERS = 4
LIST_PTS = LISTERS * DEV_PTS
NO_TILE = 4 * TILE_DEV
PARTS = TILE_DEV + 2 * (TILE_DEV // 2)
GROUP = 4
LIST_LEN = 32
MIB = 1024 * 1024

F32 = jnp.float32
BF16 = jnp.bfloat16
TOP_PRECISION = lax.Precision.HIGHEST
NT = (((1,), (1,)), ((), ()))


def swap(array, bits):
    return lax.ppermute(array, "dev", [(d, d ^ bits) for d in range(16)])


def swap_grp(array, bits):
    return lax.ppermute(array, "grp", [(g, g ^ bits) for g in range(16)])


X1, Y1 = 1, 4
X3, Y3 = 3, 12
XY = 5


def wave_table(count):
    mode_ids = jnp.arange(count // 2, dtype=jnp.int32)
    return jnp.stack([mode_ids % 8, mode_ids // 8 % 8, mode_ids // 64]).astype(F32)


def split_bf16(value):
    high = value.astype(BF16)
    return high, (value - high.astype(F32)).astype(BF16)


def wave_kernel(cs_ref, high_ref, low_ref):
    cos_x, sin_x = cs_ref[0:8], cs_ref[8:16]
    for fz in range(4):
        cos_z, sin_z = cs_ref[32 + fz : 33 + fz], cs_ref[40 + fz : 41 + fz]
        for fy in range(0, 8, 2):
            parts_cos, parts_sin = [], []
            for step in range(2):
                cos_y = cs_ref[16 + fy + step : 17 + fy + step]
                sin_y = cs_ref[24 + fy + step : 25 + fy + step]
                cos_yz = cos_y * cos_z - sin_y * sin_z
                sin_yz = sin_y * cos_z + cos_y * sin_z
                parts_cos.append(cos_x * cos_yz - sin_x * sin_yz)
                parts_sin.append(sin_x * cos_yz + cos_x * sin_yz)
            row = fz * 64 + fy * 8
            for base, parts in ((row, parts_cos), (HALF + row, parts_sin)):
                high, low = split_bf16(jnp.concatenate(parts, axis=0))
                high_ref[base : base + 16] = high
                low_ref[base : base + 16] = low


def wave_of_points(coords):
    points = coords.shape[1]
    chunk = 256
    angle = (jnp.arange(8, dtype=F32)[None, :, None] * coords[:, None, :]) * (2.0 * math.pi / GRIDN)
    cs = jnp.stack([jnp.cos(angle), jnp.sin(angle)], axis=1).reshape(48, points)
    out = jax.ShapeDtypeStruct((KM, points), BF16)
    return pl.pallas_call(
        wave_kernel,
        grid=(points // chunk,),
        in_specs=[pl.BlockSpec((48, chunk), lambda i: (0, i))],
        out_specs=[pl.BlockSpec((KM, chunk), lambda i: (0, i))] * 2,
        out_shape=[out, out],
        cost_estimate=pl.CostEstimate(flops=8 * KM * points, bytes_accessed=4 * KM * points, transcendentals=0),
    )(cs)


def orbital_copies(own_orb, x_orb, y_orb, diag_orbs, orbs, sems):
    return [
        [pltpu.make_async_copy(own_orb, orbs.at[0:2], sems.at[0])],
        [pltpu.make_async_copy(x_orb, orbs.at[2:4], sems.at[1])],
        [pltpu.make_async_copy(y_orb, orbs.at[4:6], sems.at[2])],
        [
            pltpu.make_async_copy(orb, orbs.at[6 + b] if len(diag_orbs) > 1 else orbs.at[6:8], sems.at[3 + b])
            for b, orb in enumerate(diag_orbs)
        ],
    ]


def density_kernel(
    tmap_ref,
    blocks_ref,
    own_tile,
    x_tile,
    y_tile,
    low_tile,
    high_tile,
    own_orb,
    x_orb,
    y_orb,
    first_orb,
    second_orb,
    spread_ref,
    weights_ref,
    high_hbm,
    low_hbm,
    trig_ref,
    rows_ref,
    out_ref,
    diag_out,
    tiles,
    orbs,
    density,
    high_ref,
    low_ref,
    sems,
):
    half = TILE_DEV // 2
    arrivals = [
        pltpu.make_async_copy(source, tiles.at[at : at + source.shape[0]], sems.at[n])
        for n, (source, at) in enumerate(
            (
                (own_tile, 0),
                (x_tile, TILE_DEV),
                (y_tile, 2 * TILE_DEV),
                (low_tile, 3 * TILE_DEV),
                (high_tile, 3 * TILE_DEV + half),
            )
        )
    ]
    waves = [
        pltpu.make_async_copy(high_hbm, high_ref, sems.at[5]),
        pltpu.make_async_copy(low_hbm, low_ref, sems.at[6]),
    ]
    points = orbital_copies(own_orb, x_orb, y_orb, (first_orb, second_orb), orbs, sems.at[7:12])
    for copy in arrivals + sum(points, []) + waves:
        copy.start()
    tiles[NO_TILE] = jnp.zeros((TB, TB), BF16)
    for copy in arrivals:
        copy.wait()
    for lister in range(LISTERS):
        for copy in points[lister]:
            copy.wait()
        if lister == LISTERS - 1:
            onward = pltpu.make_async_copy(orbs.at[6:8], diag_out, sems.at[12])
            onward.start()

        def one_batch(batch, unused, lister=lister):
            chosen = [blocks_ref[batch, i] for i in range(BB)]
            total = jnp.zeros((PTS, TB), F32)
            for pair in range(BB // 2):
                columns = []
                for j in (2 * pair, 2 * pair + 1):
                    columns.append(
                        jnp.concatenate(
                            [tiles[tmap_ref[lister, chosen[i] * UB + chosen[j]]] for i in range(BB)], axis=0
                        )
                    )
                product = jnp.dot(orbs[batch], jnp.concatenate(columns, axis=1), preferred_element_type=F32)
                for side in range(2):
                    block = orbs[batch, :, (2 * pair + side) * TB : (2 * pair + side + 1) * TB]
                    total = total + product[:, side * TB : (side + 1) * TB] * block.astype(F32)
            density[pl.ds(batch, 1), :] = jnp.sum(total.T, axis=0, keepdims=True)
            return unused

        lax.fori_loop(BAT_DEV * lister, BAT_DEV * (lister + 1), one_batch, 0)
    for copy in waves:
        copy.wait()
    weighted = density[...] * weights_ref[...]
    charge = jnp.concatenate(
        [spread_ref[:, b * PTS : (b + 1) * PTS] * weighted[b : b + 1] for b in range(LISTERS * BAT_DEV)], axis=1
    )
    charge_high, charge_low = split_bf16(charge)
    both = lax.dot_general(
        jnp.concatenate([charge_high, charge_low], axis=0), high_ref[...], NT, preferred_element_type=F32
    )
    sums = both[:ATOM_GRP] + both[ATOM_GRP:]
    sums = sums + lax.dot_general(charge_high, low_ref[...], NT, preferred_element_type=F32)
    cos_sum, sin_sum = sums[:, :HALF], sums[:, HALF:]
    cos_atom, sin_atom = trig_ref[:, :HALF], trig_ref[:, HALF:]
    out_ref[0:ATOM_GRP, :HALF] = cos_sum * cos_atom + sin_sum * sin_atom
    out_ref[0:ATOM_GRP, HALF:] = sin_sum * cos_atom - cos_sum * sin_atom
    for e in range(LISTERS):
        for b in range(BAT_DEV):
            out_ref[ATOM_GRP + e : ATOM_GRP + e + 1, b * PTS : (b + 1) * PTS] = density[
                BAT_DEV * e + b : BAT_DEV * e + b + 1
            ]
    out_ref[ATOM_GRP + LISTERS :] = rows_ref[...]
    onward.wait()


SMEM_SPEC = pl.BlockSpec(memory_space=pltpu.SMEM)
VMEM_SPEC = pl.BlockSpec(memory_space=pltpu.VMEM)
ANY_SPEC = pl.BlockSpec(memory_space=pl.ANY)


def density_and_moments(tmap, blocks, tiles, orbs, spread, weights, wave_high, wave_low, trig, rows):
    return pl.pallas_call(
        density_kernel,
        in_specs=[SMEM_SPEC] * 2 + [ANY_SPEC] * 10 + [VMEM_SPEC] * 2 + [ANY_SPEC] * 2 + [VMEM_SPEC] * 2,
        out_specs=[VMEM_SPEC, ANY_SPEC],
        out_shape=[
            jax.ShapeDtypeStruct((ATOM_GRP + 8, KM), F32),
            jax.ShapeDtypeStruct((BAT_DEV, PTS, BB * TB), BF16),
        ],
        scratch_shapes=[
            pltpu.VMEM((NO_TILE + 1, TB, TB), BF16),
            pltpu.VMEM((LISTERS * BAT_DEV, PTS, BB * TB), BF16),
            pltpu.VMEM((LISTERS * BAT_DEV, PTS), F32),
            pltpu.VMEM((KM, LIST_PTS), BF16),
            pltpu.VMEM((KM, LIST_PTS), BF16),
            pltpu.SemaphoreType.DMA((13,)),
        ],
        compiler_params=pltpu.CompilerParams(vmem_limit_bytes=56 * MIB),
        cost_estimate=pl.CostEstimate(flops=10**6, bytes_accessed=10**4, transcendentals=0),
    )(tmap, blocks, *tiles, *orbs, spread, weights, wave_high, wave_low, trig, rows)


def pack_kernel(coords, weights, owner, slot, blocks, atoms, shares, out_ref, owner_ref, slot_ref, blocks_ref, atoms_ref, shares_ref, sems):
    copies = [
        pltpu.make_async_copy(source, target, sems.at[n])
        for n, (source, target) in enumerate(
            (
                (coords, out_ref.at[0:3]),
                (weights, out_ref.at[3:4]),
                (owner, owner_ref),
                (slot, slot_ref),
                (blocks, blocks_ref),
                (atoms, atoms_ref),
                (shares, shares_ref),
            )
        )
    ]
    out_ref[4:6] = jnp.zeros((2, DEV_PTS), F32)
    for copy in copies:
        copy.start()
    for copy in copies:
        copy.wait()
    out_ref[4:5, :R] = owner_ref[...].astype(F32)
    out_ref[4:5, TB : TB + R] = slot_ref[...].astype(F32)
    for b in range(BAT_DEV):
        out_ref[4:5, (2 + b) * TB : (2 + b) * TB + BB] = blocks_ref[b : b + 1].astype(F32)
        out_ref[5:6, b * TB : b * TB + NEAR] = atoms_ref[b : b + 1].astype(F32)
        out_ref[5:6, (2 + b) * TB : (2 + b) * TB + NEAR] = shares_ref[b : b + 1].astype(F32)


def place_kernel(index_ref, out_ref):
    out_ref[...] = index_ref[...].astype(F32)


def atom_places(index):
    return pl.pallas_call(
        place_kernel,
        in_specs=[VMEM_SPEC],
        out_specs=VMEM_SPEC,
        out_shape=jax.ShapeDtypeStruct(index.shape, F32),
        cost_estimate=pl.CostEstimate(flops=2 * 10**10, bytes_accessed=1000, transcendentals=0),
    )(index)


def packed_facts(*parts):
    return pl.pallas_call(
        pack_kernel,
        in_specs=[ANY_SPEC] * 7,
        out_specs=VMEM_SPEC,
        out_shape=jax.ShapeDtypeStruct((6, DEV_PTS), F32),
        scratch_shapes=[pltpu.VMEM(part.shape, part.dtype) for part in parts[2:]] + [pltpu.SemaphoreType.DMA((7,))],
        compiler_params=pltpu.CompilerParams(vmem_limit_bytes=56 * MIB),
        cost_estimate=pl.CostEstimate(flops=1000, bytes_accessed=1000, transcendentals=0),
    )(*parts)


def add_ham(codes_ref, counts_ref, blocks_ref, copies, orbs, scale, ham, turned, scaled):
    for e in range(LISTERS):
        for copy in copies[e]:
            copy.wait()
        for b in range(BAT_DEV):
            source = orbs.at[BAT_DEV * e + b]
            factors = []
            for part in range(PTS // TB):
                at = e * DEV_PTS + b * PTS + part * TB
                factors.append(jnp.broadcast_to(scale[:, at : at + TB], (TB, TB)).T)
            missing = UB * (UB - 1) // 2
            for i in range(BB):
                block = blocks_ref[BAT_DEV * e + b, i]
                missing = missing - block
                turned[block, :, b * PTS : (b + 1) * PTS] = source[:, i * TB : (i + 1) * TB].T
                for part in range(PTS // TB):
                    piece = source[part * TB : (part + 1) * TB, i * TB : (i + 1) * TB]
                    rows = slice(b * PTS + part * TB, b * PTS + (part + 1) * TB)
                    scaled[block, rows, :] = (factors[part] * piece.astype(F32)).astype(BF16)
            scaled[missing, b * PTS : (b + 1) * PTS, :] = jnp.zeros((PTS, TB), BF16)
            turned[missing, :, b * PTS : (b + 1) * PTS] = jnp.zeros((TB, PTS), BF16)

        def some_items(step, unused):
            for item in range(GROUP):
                code = codes_ref[e, step * GROUP + item]
                tile = code & 255
                i = (code >> 8) & 15
                j = code >> 12
                ham[tile] += jnp.dot(turned[i], scaled[j], preferred_element_type=F32)
            return unused

        lax.fori_loop(0, counts_ref[e], some_items, 0)


def potential_kernel(
    moments_ref, far_ref, near_ref, trig_ref, spread_ref, weights_ref, high_ref, low_ref, pot_ref, scale_ref
):
    cos_atom, sin_atom = trig_ref[:, :HALF], trig_ref[:, HALF:]
    cos_near = moments_ref[:, :HALF] * near_ref[:, :HALF]
    sin_near = moments_ref[:, HALF:] * near_ref[:, HALF:]
    turned_cos = cos_near * cos_atom - sin_near * sin_atom
    turned_sin = cos_near * sin_atom + sin_near * cos_atom
    coef = jnp.concatenate(
        [
            jnp.concatenate([turned_cos, turned_sin], axis=1),
            jnp.concatenate([far_ref[...], jnp.zeros((ATOM_GRP - 1, KM), F32)], axis=0),
        ],
        axis=0,
    )
    coef_high, coef_low = split_bf16(coef)
    both = jnp.dot(jnp.concatenate([coef_high, coef_low], axis=0), high_ref[...], preferred_element_type=F32)
    values = both[: 2 * ATOM_GRP] + both[2 * ATOM_GRP :]
    values = values + jnp.dot(coef_high, low_ref[...], preferred_element_type=F32)
    pot = jnp.sum(values[:ATOM_GRP] * spread_ref[...], axis=0, keepdims=True) + values[ATOM_GRP : ATOM_GRP + 1]
    pot_ref[...] = pot[:, :DEV_PTS]
    scale_ref[...] = pot * weights_ref[...]


def potential_of(moments, far, near, trig, spread, weights, wave_high, wave_low):
    return pl.pallas_call(
        potential_kernel,
        in_specs=[VMEM_SPEC] * 8,
        out_specs=[VMEM_SPEC] * 2,
        out_shape=[jax.ShapeDtypeStruct((1, DEV_PTS), F32), jax.ShapeDtypeStruct((1, LIST_PTS), F32)],
        compiler_params=pltpu.CompilerParams(vmem_limit_bytes=16 * MIB),
        cost_estimate=pl.CostEstimate(flops=10**6, bytes_accessed=10**4, transcendentals=0),
    )(moments, far, near, trig, spread, weights, wave_high, wave_low)


def ham_kernel(n_starts, n_outs, codes_ref, counts_ref, blocks_ref, scale_ref, *refs):
    n_orbs = len(refs) - n_starts - n_outs - 5
    orb_refs, refs = refs[:n_orbs], refs[n_orbs:]
    starts, outs, (ham, turned, scaled, orbs, sems) = refs[:n_starts], refs[n_starts : n_starts + n_outs], refs[-5:]
    tiles = ham.shape[0] - 1
    copies = orbital_copies(*orb_refs[:3], orb_refs[3:], orbs, sems)
    for start in starts:
        copies[0].append(pltpu.make_async_copy(start, ham.at[0:tiles], sems.at[5]))
    for copy in sum(copies, []):
        copy.start()
    if n_starts == 0:

        def clear(t, unused):
            ham[t] = jnp.zeros((TB, TB), F32)
            return unused

        lax.fori_loop(0, tiles, clear, 0)
    add_ham(codes_ref, counts_ref, blocks_ref, copies, orbs, scale_ref[...], ham, turned, scaled)
    at = 0
    for out in outs:
        out[...] = ham[at : at + out.shape[0]].astype(out.dtype)
        at = at + out.shape[0]


def ham_terms(codes, counts, blocks, scale, orbs, starts, outs, flops):
    tiles = sum(count for count, unused in outs)
    return pl.pallas_call(
        functools.partial(ham_kernel, len(starts), len(outs)),
        in_specs=[SMEM_SPEC] * 3 + [VMEM_SPEC] + [ANY_SPEC] * (len(orbs) + len(starts)),
        out_specs=[VMEM_SPEC] * len(outs),
        out_shape=[jax.ShapeDtypeStruct((count, TB, TB), dtype) for count, dtype in outs],
        scratch_shapes=[
            pltpu.VMEM((tiles + 1, TB, TB), F32),
            pltpu.VMEM((UB, TB, DEV_PTS), BF16),
            pltpu.VMEM((UB, DEV_PTS, TB), BF16),
            pltpu.VMEM((LISTERS * BAT_DEV, PTS, BB * TB), BF16),
            pltpu.SemaphoreType.DMA((6,)),
        ],
        compiler_params=pltpu.CompilerParams(vmem_limit_bytes=56 * MIB),
        cost_estimate=pl.CostEstimate(flops=flops, bytes_accessed=10**4, transcendentals=0),
    )(codes, counts, blocks, scale, *orbs, *starts)


def final_kernel(own_ref, x_ref, y_ref, out_ref):
    half = TILE_DEV // 2
    step = half // 2
    got = jnp.where(pl.program_id(0) < half // step, x_ref[...].astype(F32), y_ref[...].astype(F32))
    out_ref[...] = (own_ref[...] + got).astype(BF16)


def final_tiles(own, got_x, got_y):
    step = TILE_DEV // 4
    block = (step, TB, TB)
    return pl.pallas_call(
        final_kernel,
        grid=(4,),
        in_specs=[
            pl.BlockSpec(block, lambda t: (t, 0, 0)),
            pl.BlockSpec(block, lambda t: (jnp.minimum(t, 1), 0, 0)),
            pl.BlockSpec(block, lambda t: (jnp.maximum(t - 2, 0), 0, 0)),
        ],
        out_specs=pl.BlockSpec(block, lambda t: (t, 0, 0)),
        out_shape=jax.ShapeDtypeStruct((TILE_DEV, TB, TB), BF16),
        compiler_params=pltpu.CompilerParams(vmem_limit_bytes=16 * MIB),
        cost_estimate=pl.CostEstimate(flops=10**6, bytes_accessed=10**4, transcendentals=0),
    )(own, got_x, got_y)


def kept_of(mine, places):
    rows = jnp.arange(R, dtype=jnp.int32)
    codes = places + (rows // UB) * 256 + (rows % UB) * 4096
    before = (rows[:, None] < rows[None, :])[None] & mine[:, :, None]
    rank = jnp.sum(before.astype(jnp.int32), axis=1)
    counts = jnp.sum(mine.astype(jnp.int32), axis=1)
    at = jnp.arange(LIST_LEN, dtype=jnp.int32)
    hit = (rank[:, None, :] == at[None, :, None]) & mine[:, None, :]
    listed = jnp.sum(jnp.where(hit, codes[:, None, :], 0), axis=2)
    return listed, counts, at


def lists_of(owners, slots, me):
    half = TILE_DEV // 2
    away = owners ^ me
    own = away == 0
    shared = ((away == X1) & (slots < half)) | ((away == Y1) & (slots >= half))
    found = []
    for mine in (own | shared, own, shared):
        place = jnp.where(own, slots, TILE_DEV + slots) if len(found) == 0 else slots
        listed, counts, at = kept_of(mine, place)
        dummy = PARTS if len(found) == 0 else TILE_DEV
        found.append((jnp.where(at[None] < counts[:, None], listed, dummy), (counts + GROUP - 1) // GROUP))
    return found


def what_is_listed(rows):
    ints = rows.astype(jnp.int32)
    blocks = ints[:, 2 * TB :].reshape(LISTERS * BAT_DEV, TB)[:, :BB]
    return ints[:, :R], ints[:, TB : TB + R], blocks


def on_device(
    orbitals,
    dens_tiles,
    point_coords,
    point_weights,
    batch_blocks,
    tile_owner,
    tile_slot,
    batch_atoms,
    batch_weights,
    atom_grid_index,
):
    me = lax.axis_index("dev").astype(jnp.int32)

    facts = packed_facts(
        point_coords,
        point_weights[None],
        tile_owner.reshape(1, R),
        tile_slot[None],
        batch_blocks,
        batch_atoms,
        batch_weights,
    )
    facts = (facts, swap(facts, X3), swap(facts, Y3), swap(facts, X3 ^ Y3))
    location, sent, *facts = lax.optimization_barrier((atom_places(atom_grid_index), dens_tiles, *facts))
    half = TILE_DEV // 2
    tile_x, tile_y = swap(sent, X1), swap(sent, Y1)
    orb_x, orb_y = swap(orbitals, X3), swap(orbitals, Y3)
    tile_low, tile_high = swap(tile_y[:half], X1), swap(tile_x[half:], Y1)
    orb_first, orb_second = swap(orb_y[0], X3), swap(orb_x[1], Y3)
    orbs = (orbitals, orb_x, orb_y, orb_first, orb_second)

    facts = jnp.stack(facts)
    coords = facts[:, :3].transpose(1, 0, 2).reshape(3, LIST_PTS)
    weights = facts[:, 3].reshape(LISTERS * BAT_DEV, PTS)
    owners, slots, blocks = what_is_listed(facts[:, 4])
    near_by = facts[:, 5].reshape(LISTERS, 2, BAT_DEV, TB)[..., :NEAR].reshape(LISTERS, 2, BAT_DEV, NEAR)
    atoms = near_by[:, 0].reshape(LISTERS * BAT_DEV, NEAR).astype(jnp.int32)
    raw_weight = near_by[:, 1].reshape(LISTERS * BAT_DEV, NEAR)
    away = owners ^ me
    tmap = jnp.where((away & 10) == 0, ((away & 1) + ((away >> 2) & 1) * 2) * TILE_DEV + slots, NO_TILE)
    codes, counts = lists_of(owners, slots, me)[0]

    wave_vecs = wave_table(KM)
    squared = jnp.sum(wave_vecs * wave_vecs, axis=0)
    near_gain = jnp.tile(0.1 / (1.0 + 0.1 * squared), 2)[None]
    far_gain = jnp.tile(0.03 / (1.0 + 0.1 * squared), 2)[None]
    phases = jnp.einsum("ca,cm->am", location, wave_vecs, precision=TOP_PRECISION) * (2.0 * math.pi / GRIDN)
    trig = jnp.concatenate([jnp.cos(phases), jnp.sin(phases)], axis=1)
    partition = raw_weight / jnp.sum(raw_weight, axis=1, keepdims=True)
    share = jnp.sum(
        jnp.where(
            atoms[None] == jnp.arange(ATOM_GRP, dtype=jnp.int32)[:, None, None],
            partition[None],
            0.0,
        ),
        axis=2,
    )
    displace = coords[:, None, :] - location[:, :, None]
    envelope = jnp.exp(-2.0 * jnp.sum(displace * displace, axis=0) / (GRIDN * GRIDN))
    spread = (envelope.reshape(ATOM_GRP, LISTERS * BAT_DEV, PTS) * share[:, :, None]).reshape(ATOM_GRP, LIST_PTS)
    wave_high, wave_low = wave_of_points(coords)
    early, late = (spread, weights, wave_high, wave_low, trig, codes, counts, tmap, blocks), orbitals
    early, late, *unused = lax.optimization_barrier((early, late, tile_low, tile_high, orb_first, orb_second))
    spread, weights, wave_high, wave_low, trig, codes, counts, tmap, blocks = early
    orb_far = swap(late, XY)

    part, orb_diag = density_and_moments(
        tmap,
        blocks,
        (dens_tiles, tile_x, tile_y, tile_low, tile_high),
        orbs,
        spread,
        weights,
        wave_high,
        wave_low,
        trig,
        facts[:, 4],
    )
    a = ATOM_GRP
    got = swap(part, X3)
    order = (a + 1, a, a + 3, a + 2)
    part = part + jnp.concatenate([got[:a]] + [got[r : r + 1] for r in order] + [jnp.zeros((LISTERS, KM), F32)])
    got = swap(part, Y3)
    density = part[a] + got[a + 2]
    moments, orb_far = lax.optimization_barrier((part[:a] + got[:a], orb_far))
    orb_far_x, orb_far_y = swap(orb_far, X3), swap(orb_far, Y3)
    got = swap(jnp.concatenate([moments, part[a + LISTERS :]]), X1)
    moments = moments + got[:a]
    got = swap(jnp.concatenate([moments, got[a:]]), Y1)
    orb_diag, moments = lax.optimization_barrier((orb_diag, moments + got[:a]))
    orbs_far = (orb_far, orb_far_x, orb_far_y, swap(orb_diag, XY))
    far_owners, far_slots, far_blocks = what_is_listed(got[a:])
    unused, (own_codes, own_counts), (far_codes, far_counts) = lists_of(far_owners, far_slots, me)
    structure = jnp.sum(moments[:, :1] * trig, axis=0, keepdims=True)
    for bits in (1, 2, 4, 8):
        structure = structure + swap_grp(structure, bits)
    structure, own_codes, own_counts, far_codes, far_counts, far_blocks = lax.optimization_barrier(
        (structure, own_codes, own_counts, far_codes, far_counts, far_blocks)
    )
    potential, scale = potential_of(
        moments,
        far_gain * structure,
        near_gain,
        trig,
        spread,
        weights.reshape(1, LIST_PTS),
        wave_high,
        wave_low,
    )
    far_scale = swap(scale, XY)
    own, shared = ham_terms(
        codes, counts, blocks, scale, orbs, (), ((TILE_DEV, F32), (TILE_DEV, F32)), 2 * 10**10
    )
    half = TILE_DEV // 2
    part_x, part_y = ham_terms(
        far_codes, far_counts, far_blocks, far_scale, orbs_far, (shared,), ((half, BF16), (half, BF16)), 10**6
    )
    (own,) = ham_terms(
        own_codes, own_counts, far_blocks, far_scale, orbs_far, (own,), ((TILE_DEV, F32),), 2 * 10**10
    )
    return (density, potential.reshape(-1), final_tiles(own, swap(part_x, X1), swap(part_y, Y1)))


def solution(mesh):
    in_specs = (
        P(("grp", "dev"), None, None),
        P(("grp", "dev"), None, None),
        P(None, ("grp", "dev")),
        P(("grp", "dev")),
        P(("grp", "dev"), None),
        P(("grp", "dev"), None),
        P(("grp", "dev")),
        P(("grp", "dev"), None),
        P(("grp", "dev"), None),
        P(None, "grp"),
    )
    out_specs = (P(("grp", "dev")), P(("grp", "dev")), P(("grp", "dev"), None, None))
    return jax.shard_map(
        on_device, mesh=mesh, in_specs=in_specs, out_specs=out_specs, check_vma=False
    )
```

```python
import functools
import math

import jax
import jax.numpy as jnp
from jax import lax
from jax.experimental import pallas as pl
from jax.experimental.pallas import tpu as pltpu
from jax.sharding import PartitionSpec as P

TB = 128
BB = 8
UB = 9
R = 81
PTS = 256
BAT_DEV = 2
KM = 512
HALF = KM // 2
NEAR = 4
TILE_DEV = 32
GRIDN = 64
ATOM_GRP = 16
DEV_PTS = BAT_DEV * PTS
LISTERS = 4
LIST_PTS = LISTERS * DEV_PTS
NO_TILE = 4 * TILE_DEV
PARTS = TILE_DEV + 2 * (TILE_DEV // 2)
GROUP = 4
LIST_LEN = 32
MIB = 1024 * 1024

F32 = jnp.float32
BF16 = jnp.bfloat16
TOP_PRECISION = lax.Precision.HIGHEST
NT = (((1,), (1,)), ((), ()))


def swap(array, bits):
    return lax.ppermute(array, "dev", [(d, d ^ bits) for d in range(16)])


def swap_grp(array, bits):
    return lax.ppermute(array, "grp", [(g, g ^ bits) for g in range(16)])


X1, Y1 = 1, 4
X3, Y3 = 3, 12
XY = 5


def wave_table(count):
    mode_ids = jnp.arange(count // 2, dtype=jnp.int32)
    return jnp.stack([mode_ids % 8, mode_ids // 8 % 8, mode_ids // 64]).astype(F32)


def split_bf16(value):
    high = value.astype(BF16)
    return high, (value - high.astype(F32)).astype(BF16)


def wave_kernel(cs_ref, high_ref, low_ref):
    cos_x, sin_x = cs_ref[0:8], cs_ref[8:16]
    for fz in range(4):
        cos_z, sin_z = cs_ref[32 + fz : 33 + fz], cs_ref[40 + fz : 41 + fz]
        for fy in range(0, 8, 2):
            parts_cos, parts_sin = [], []
            for step in range(2):
                cos_y = cs_ref[16 + fy + step : 17 + fy + step]
                sin_y = cs_ref[24 + fy + step : 25 + fy + step]
                cos_yz = cos_y * cos_z - sin_y * sin_z
                sin_yz = sin_y * cos_z + cos_y * sin_z
                parts_cos.append(cos_x * cos_yz - sin_x * sin_yz)
                parts_sin.append(sin_x * cos_yz + cos_x * sin_yz)
            row = fz * 64 + fy * 8
            for base, parts in ((row, parts_cos), (HALF + row, parts_sin)):
                high, low = split_bf16(jnp.concatenate(parts, axis=0))
                high_ref[base : base + 16] = high
                low_ref[base : base + 16] = low


def wave_of_points(coords):
    points = coords.shape[1]
    chunk = 256
    angle = (jnp.arange(8, dtype=F32)[None, :, None] * coords[:, None, :]) * (2.0 * math.pi / GRIDN)
    cs = jnp.stack([jnp.cos(angle), jnp.sin(angle)], axis=1).reshape(48, points)
    out = jax.ShapeDtypeStruct((KM, points), BF16)
    return pl.pallas_call(
        wave_kernel,
        grid=(points // chunk,),
        in_specs=[pl.BlockSpec((48, chunk), lambda i: (0, i))],
        out_specs=[pl.BlockSpec((KM, chunk), lambda i: (0, i))] * 2,
        out_shape=[out, out],
        cost_estimate=pl.CostEstimate(flops=8 * KM * points, bytes_accessed=4 * KM * points, transcendentals=0),
    )(cs)


def orbital_copies(own_orb, x_orb, y_orb, diag_orbs, orbs, sems):
    return [
        [pltpu.make_async_copy(own_orb, orbs.at[0:2], sems.at[0])],
        [pltpu.make_async_copy(x_orb, orbs.at[2:4], sems.at[1])],
        [pltpu.make_async_copy(y_orb, orbs.at[4:6], sems.at[2])],
        [
            pltpu.make_async_copy(orb, orbs.at[6 + b] if len(diag_orbs) > 1 else orbs.at[6:8], sems.at[3 + b])
            for b, orb in enumerate(diag_orbs)
        ],
    ]


def tile_copies(own_tile, x_tile, y_tile, low_tile, high_tile, tiles, sems):
    half = TILE_DEV // 2
    sources = (
        (own_tile, 0),
        (x_tile, TILE_DEV),
        (y_tile, 2 * TILE_DEV),
        (low_tile, 3 * TILE_DEV),
        (high_tile, 3 * TILE_DEV + half),
    )
    return [
        pltpu.make_async_copy(source, tiles.at[at : at + source.shape[0]], sems.at[n])
        for n, (source, at) in enumerate(sources)
    ]


def batch_density(tmap_ref, blocks_ref, tiles, lister, batch, orb):
    chosen = [blocks_ref[batch, i] for i in range(BB)]
    total = jnp.zeros((PTS, TB), F32)
    for pair in range(BB // 2):
        columns = []
        for j in (2 * pair, 2 * pair + 1):
            columns.append(
                jnp.concatenate([tiles[tmap_ref[lister, chosen[i] * UB + chosen[j]]] for i in range(BB)], axis=0)
            )
        product = jnp.dot(orb[...], jnp.concatenate(columns, axis=1), preferred_element_type=F32)
        for side in range(2):
            block = orb[:, (2 * pair + side) * TB : (2 * pair + side + 1) * TB]
            total = total + product[:, side * TB : (side + 1) * TB] * block.astype(F32)
    return jnp.sum(total.T, axis=0, keepdims=True)


def first_density_kernel(
    tmap_ref,
    blocks_ref,
    own_tile,
    x_tile,
    y_tile,
    low_tile,
    high_tile,
    own_orb,
    x_orb,
    y_orb,
    out_ref,
    tiles,
    orbs,
    sems,
):
    arrivals = tile_copies(own_tile, x_tile, y_tile, low_tile, high_tile, tiles, sems)
    points = orbital_copies(own_orb, x_orb, y_orb, (), orbs, sems.at[5:8])
    for copy in arrivals + sum(points, []):
        copy.start()
    tiles[NO_TILE] = jnp.zeros((TB, TB), BF16)
    out_ref[...] = jnp.zeros(out_ref.shape, F32)
    for copy in arrivals:
        copy.wait()
    for lister in range(LISTERS - 1):
        for copy in points[lister]:
            copy.wait()

        def one_batch(batch, unused, lister=lister):
            out_ref[pl.ds(batch, 1), :] = batch_density(
                tmap_ref, blocks_ref, tiles, lister, batch, orbs.at[batch]
            )
            return unused

        lax.fori_loop(BAT_DEV * lister, BAT_DEV * (lister + 1), one_batch, 0)


def first_density(tmap, blocks, tiles, orbs):
    return pl.pallas_call(
        first_density_kernel,
        in_specs=[SMEM_SPEC] * 2 + [ANY_SPEC] * 8,
        out_specs=VMEM_SPEC,
        out_shape=jax.ShapeDtypeStruct((LISTERS * BAT_DEV, PTS), F32),
        scratch_shapes=[
            pltpu.VMEM((NO_TILE + 1, TB, TB), BF16),
            pltpu.VMEM(((LISTERS - 1) * BAT_DEV, PTS, BB * TB), BF16),
            pltpu.SemaphoreType.DMA((8,)),
        ],
        compiler_params=pltpu.CompilerParams(vmem_limit_bytes=56 * MIB),
        cost_estimate=pl.CostEstimate(flops=2 * 10**10, bytes_accessed=10**4, transcendentals=0),
    )(tmap, blocks, *tiles, *orbs[:3])


def density_kernel(
    tmap_ref,
    blocks_ref,
    own_tile,
    x_tile,
    y_tile,
    low_tile,
    high_tile,
    first_orb,
    second_orb,
    before_ref,
    spread_ref,
    weights_ref,
    high_hbm,
    low_hbm,
    trig_ref,
    rows_ref,
    out_ref,
    diag_out,
    tiles,
    orbs,
    density,
    high_ref,
    low_ref,
    sems,
):
    arrivals = tile_copies(own_tile, x_tile, y_tile, low_tile, high_tile, tiles, sems)
    waves = [
        pltpu.make_async_copy(high_hbm, high_ref, sems.at[5]),
        pltpu.make_async_copy(low_hbm, low_ref, sems.at[6]),
    ]
    points = [
        pltpu.make_async_copy(first_orb, orbs.at[0], sems.at[7]),
        pltpu.make_async_copy(second_orb, orbs.at[1], sems.at[8]),
    ]
    for copy in arrivals + points + waves:
        copy.start()
    tiles[NO_TILE] = jnp.zeros((TB, TB), BF16)
    density[...] = before_ref[...]
    for copy in arrivals + points:
        copy.wait()
    onward = pltpu.make_async_copy(orbs, diag_out, sems.at[9])
    onward.start()

    def one_batch(b, unused):
        batch = BAT_DEV * (LISTERS - 1) + b
        density[pl.ds(batch, 1), :] = batch_density(
            tmap_ref, blocks_ref, tiles, LISTERS - 1, batch, orbs.at[b]
        )
        return unused

    lax.fori_loop(0, BAT_DEV, one_batch, 0)
    for copy in waves:
        copy.wait()
    weighted = density[...] * weights_ref[...]
    charge = jnp.concatenate(
        [spread_ref[:, b * PTS : (b + 1) * PTS] * weighted[b : b + 1] for b in range(LISTERS * BAT_DEV)], axis=1
    )
    charge_high, charge_low = split_bf16(charge)
    both = lax.dot_general(
        jnp.concatenate([charge_high, charge_low], axis=0), high_ref[...], NT, preferred_element_type=F32
    )
    sums = both[:ATOM_GRP] + both[ATOM_GRP:]
    sums = sums + lax.dot_general(charge_high, low_ref[...], NT, preferred_element_type=F32)
    cos_sum, sin_sum = sums[:, :HALF], sums[:, HALF:]
    cos_atom, sin_atom = trig_ref[:, :HALF], trig_ref[:, HALF:]
    out_ref[0:ATOM_GRP, :HALF] = cos_sum * cos_atom + sin_sum * sin_atom
    out_ref[0:ATOM_GRP, HALF:] = sin_sum * cos_atom - cos_sum * sin_atom
    for e in range(LISTERS):
        for b in range(BAT_DEV):
            out_ref[ATOM_GRP + e : ATOM_GRP + e + 1, b * PTS : (b + 1) * PTS] = density[
                BAT_DEV * e + b : BAT_DEV * e + b + 1
            ]
    out_ref[ATOM_GRP + LISTERS :] = rows_ref[...]
    onward.wait()


SMEM_SPEC = pl.BlockSpec(memory_space=pltpu.SMEM)
VMEM_SPEC = pl.BlockSpec(memory_space=pltpu.VMEM)
ANY_SPEC = pl.BlockSpec(memory_space=pl.ANY)


def density_and_moments(tmap, blocks, tiles, orbs, before, spread, weights, wave_high, wave_low, trig, rows):
    return pl.pallas_call(
        density_kernel,
        in_specs=[SMEM_SPEC] * 2 + [ANY_SPEC] * 7 + [VMEM_SPEC] * 3 + [ANY_SPEC] * 2 + [VMEM_SPEC] * 2,
        out_specs=[VMEM_SPEC, ANY_SPEC],
        out_shape=[
            jax.ShapeDtypeStruct((ATOM_GRP + 8, KM), F32),
            jax.ShapeDtypeStruct((BAT_DEV, PTS, BB * TB), BF16),
        ],
        scratch_shapes=[
            pltpu.VMEM((NO_TILE + 1, TB, TB), BF16),
            pltpu.VMEM((BAT_DEV, PTS, BB * TB), BF16),
            pltpu.VMEM((LISTERS * BAT_DEV, PTS), F32),
            pltpu.VMEM((KM, LIST_PTS), BF16),
            pltpu.VMEM((KM, LIST_PTS), BF16),
            pltpu.SemaphoreType.DMA((10,)),
        ],
        compiler_params=pltpu.CompilerParams(vmem_limit_bytes=56 * MIB),
        cost_estimate=pl.CostEstimate(flops=10**6, bytes_accessed=10**4, transcendentals=0),
    )(tmap, blocks, *tiles, *orbs[3:], before, spread, weights, wave_high, wave_low, trig, rows)


def pack_kernel(coords, weights, owner, slot, blocks, atoms, shares, out_ref, owner_ref, slot_ref, blocks_ref, atoms_ref, shares_ref, sems):
    copies = [
        pltpu.make_async_copy(source, target, sems.at[n])
        for n, (source, target) in enumerate(
            (
                (coords, out_ref.at[0:3]),
                (weights, out_ref.at[3:4]),
                (owner, owner_ref),
                (slot, slot_ref),
                (blocks, blocks_ref),
                (atoms, atoms_ref),
                (shares, shares_ref),
            )
        )
    ]
    out_ref[4:6] = jnp.zeros((2, DEV_PTS), F32)
    for copy in copies:
        copy.start()
    for copy in copies:
        copy.wait()
    out_ref[4:5, :R] = owner_ref[...].astype(F32)
    out_ref[4:5, TB : TB + R] = slot_ref[...].astype(F32)
    for b in range(BAT_DEV):
        out_ref[4:5, (2 + b) * TB : (2 + b) * TB + BB] = blocks_ref[b : b + 1].astype(F32)
        out_ref[5:6, b * TB : b * TB + NEAR] = atoms_ref[b : b + 1].astype(F32)
        out_ref[5:6, (2 + b) * TB : (2 + b) * TB + NEAR] = shares_ref[b : b + 1].astype(F32)


def place_kernel(index_ref, out_ref):
    out_ref[...] = index_ref[...].astype(F32)


def atom_places(index):
    return pl.pallas_call(
        place_kernel,
        in_specs=[VMEM_SPEC],
        out_specs=VMEM_SPEC,
        out_shape=jax.ShapeDtypeStruct(index.shape, F32),
        cost_estimate=pl.CostEstimate(flops=2 * 10**10, bytes_accessed=1000, transcendentals=0),
    )(index)


def packed_facts(*parts):
    return pl.pallas_call(
        pack_kernel,
        in_specs=[ANY_SPEC] * 7,
        out_specs=VMEM_SPEC,
        out_shape=jax.ShapeDtypeStruct((6, DEV_PTS), F32),
        scratch_shapes=[pltpu.VMEM(part.shape, part.dtype) for part in parts[2:]] + [pltpu.SemaphoreType.DMA((7,))],
        compiler_params=pltpu.CompilerParams(vmem_limit_bytes=56 * MIB),
        cost_estimate=pl.CostEstimate(flops=1000, bytes_accessed=1000, transcendentals=0),
    )(*parts)


def add_ham(codes_ref, counts_ref, blocks_ref, copies, orbs, scale, ham, turned, scaled):
    for e in range(LISTERS):
        for copy in copies[e]:
            copy.wait()
        for b in range(BAT_DEV):
            source = orbs.at[BAT_DEV * e + b]
            factors = []
            for part in range(PTS // TB):
                at = e * DEV_PTS + b * PTS + part * TB
                factors.append(jnp.broadcast_to(scale[:, at : at + TB], (TB, TB)).T)
            missing = UB * (UB - 1) // 2
            for i in range(BB):
                block = blocks_ref[BAT_DEV * e + b, i]
                missing = missing - block
                turned[block, :, b * PTS : (b + 1) * PTS] = source[:, i * TB : (i + 1) * TB].T
                for part in range(PTS // TB):
                    piece = source[part * TB : (part + 1) * TB, i * TB : (i + 1) * TB]
                    rows = slice(b * PTS + part * TB, b * PTS + (part + 1) * TB)
                    scaled[block, rows, :] = (factors[part] * piece.astype(F32)).astype(BF16)
            scaled[missing, b * PTS : (b + 1) * PTS, :] = jnp.zeros((PTS, TB), BF16)
            turned[missing, :, b * PTS : (b + 1) * PTS] = jnp.zeros((TB, PTS), BF16)

        def some_items(step, unused):
            for item in range(GROUP):
                code = codes_ref[e, step * GROUP + item]
                tile = code & 255
                i = (code >> 8) & 15
                j = code >> 12
                ham[tile] += jnp.dot(turned[i], scaled[j], preferred_element_type=F32)
            return unused

        lax.fori_loop(0, counts_ref[e], some_items, 0)


def potential_kernel(
    moments_ref, far_ref, near_ref, trig_ref, spread_ref, weights_ref, high_ref, low_ref, pot_ref, scale_ref
):
    cos_atom, sin_atom = trig_ref[:, :HALF], trig_ref[:, HALF:]
    cos_near = moments_ref[:, :HALF] * near_ref[:, :HALF]
    sin_near = moments_ref[:, HALF:] * near_ref[:, HALF:]
    turned_cos = cos_near * cos_atom - sin_near * sin_atom
    turned_sin = cos_near * sin_atom + sin_near * cos_atom
    coef = jnp.concatenate(
        [
            jnp.concatenate([turned_cos, turned_sin], axis=1),
            jnp.concatenate([far_ref[...], jnp.zeros((ATOM_GRP - 1, KM), F32)], axis=0),
        ],
        axis=0,
    )
    coef_high, coef_low = split_bf16(coef)
    both = jnp.dot(jnp.concatenate([coef_high, coef_low], axis=0), high_ref[...], preferred_element_type=F32)
    values = both[: 2 * ATOM_GRP] + both[2 * ATOM_GRP :]
    values = values + jnp.dot(coef_high, low_ref[...], preferred_element_type=F32)
    pot = jnp.sum(values[:ATOM_GRP] * spread_ref[...], axis=0, keepdims=True) + values[ATOM_GRP : ATOM_GRP + 1]
    pot_ref[...] = pot[:, :DEV_PTS]
    scale_ref[...] = pot * weights_ref[...]


def potential_of(moments, far, near, trig, spread, weights, wave_high, wave_low):
    return pl.pallas_call(
        potential_kernel,
        in_specs=[VMEM_SPEC] * 8,
        out_specs=[VMEM_SPEC] * 2,
        out_shape=[jax.ShapeDtypeStruct((1, DEV_PTS), F32), jax.ShapeDtypeStruct((1, LIST_PTS), F32)],
        compiler_params=pltpu.CompilerParams(vmem_limit_bytes=16 * MIB),
        cost_estimate=pl.CostEstimate(flops=10**6, bytes_accessed=10**4, transcendentals=0),
    )(moments, far, near, trig, spread, weights, wave_high, wave_low)


def ham_kernel(n_starts, n_outs, codes_ref, counts_ref, blocks_ref, scale_ref, *refs):
    n_orbs = len(refs) - n_starts - n_outs - 5
    orb_refs, refs = refs[:n_orbs], refs[n_orbs:]
    starts, outs, (ham, turned, scaled, orbs, sems) = refs[:n_starts], refs[n_starts : n_starts + n_outs], refs[-5:]
    tiles = ham.shape[0] - 1
    copies = orbital_copies(*orb_refs[:3], orb_refs[3:], orbs, sems)
    for start in starts:
        copies[0].append(pltpu.make_async_copy(start, ham.at[0:tiles], sems.at[5]))
    for copy in sum(copies, []):
        copy.start()
    if n_starts == 0:

        def clear(t, unused):
            ham[t] = jnp.zeros((TB, TB), F32)
            return unused

        lax.fori_loop(0, tiles, clear, 0)
    add_ham(codes_ref, counts_ref, blocks_ref, copies, orbs, scale_ref[...], ham, turned, scaled)
    at = 0
    for out in outs:
        out[...] = ham[at : at + out.shape[0]].astype(out.dtype)
        at = at + out.shape[0]


def ham_terms(codes, counts, blocks, scale, orbs, starts, outs, flops):
    tiles = sum(count for count, unused in outs)
    return pl.pallas_call(
        functools.partial(ham_kernel, len(starts), len(outs)),
        in_specs=[SMEM_SPEC] * 3 + [VMEM_SPEC] + [ANY_SPEC] * (len(orbs) + len(starts)),
        out_specs=[VMEM_SPEC] * len(outs),
        out_shape=[jax.ShapeDtypeStruct((count, TB, TB), dtype) for count, dtype in outs],
        scratch_shapes=[
            pltpu.VMEM((tiles + 1, TB, TB), F32),
            pltpu.VMEM((UB, TB, DEV_PTS), BF16),
            pltpu.VMEM((UB, DEV_PTS, TB), BF16),
            pltpu.VMEM((LISTERS * BAT_DEV, PTS, BB * TB), BF16),
            pltpu.SemaphoreType.DMA((6,)),
        ],
        compiler_params=pltpu.CompilerParams(vmem_limit_bytes=56 * MIB),
        cost_estimate=pl.CostEstimate(flops=flops, bytes_accessed=10**4, transcendentals=0),
    )(codes, counts, blocks, scale, *orbs, *starts)


def final_kernel(own_ref, x_ref, y_ref, out_ref):
    half = TILE_DEV // 2
    step = half // 2
    got = jnp.where(pl.program_id(0) < half // step, x_ref[...].astype(F32), y_ref[...].astype(F32))
    out_ref[...] = (own_ref[...] + got).astype(BF16)


def final_tiles(own, got_x, got_y):
    step = TILE_DEV // 4
    block = (step, TB, TB)
    return pl.pallas_call(
        final_kernel,
        grid=(4,),
        in_specs=[
            pl.BlockSpec(block, lambda t: (t, 0, 0)),
            pl.BlockSpec(block, lambda t: (jnp.minimum(t, 1), 0, 0)),
            pl.BlockSpec(block, lambda t: (jnp.maximum(t - 2, 0), 0, 0)),
        ],
        out_specs=pl.BlockSpec(block, lambda t: (t, 0, 0)),
        out_shape=jax.ShapeDtypeStruct((TILE_DEV, TB, TB), BF16),
        compiler_params=pltpu.CompilerParams(vmem_limit_bytes=16 * MIB),
        cost_estimate=pl.CostEstimate(flops=10**6, bytes_accessed=10**4, transcendentals=0),
    )(own, got_x, got_y)


def kept_of(mine, places):
    rows = jnp.arange(R, dtype=jnp.int32)
    codes = places + (rows // UB) * 256 + (rows % UB) * 4096
    before = (rows[:, None] < rows[None, :])[None] & mine[:, :, None]
    rank = jnp.sum(before.astype(jnp.int32), axis=1)
    counts = jnp.sum(mine.astype(jnp.int32), axis=1)
    at = jnp.arange(LIST_LEN, dtype=jnp.int32)
    hit = (rank[:, None, :] == at[None, :, None]) & mine[:, None, :]
    listed = jnp.sum(jnp.where(hit, codes[:, None, :], 0), axis=2)
    return listed, counts, at


def lists_of(owners, slots, me):
    half = TILE_DEV // 2
    away = owners ^ me
    own = away == 0
    shared = ((away == X1) & (slots < half)) | ((away == Y1) & (slots >= half))
    found = []
    for mine in (own | shared, own, shared):
        place = jnp.where(own, slots, TILE_DEV + slots) if len(found) == 0 else slots
        listed, counts, at = kept_of(mine, place)
        dummy = PARTS if len(found) == 0 else TILE_DEV
        found.append((jnp.where(at[None] < counts[:, None], listed, dummy), (counts + GROUP - 1) // GROUP))
    return found


def what_is_listed(rows):
    ints = rows.astype(jnp.int32)
    blocks = ints[:, 2 * TB :].reshape(LISTERS * BAT_DEV, TB)[:, :BB]
    return ints[:, :R], ints[:, TB : TB + R], blocks


def on_device(
    orbitals,
    dens_tiles,
    point_coords,
    point_weights,
    batch_blocks,
    tile_owner,
    tile_slot,
    batch_atoms,
    batch_weights,
    atom_grid_index,
):
    me = lax.axis_index("dev").astype(jnp.int32)

    facts = packed_facts(
        point_coords,
        point_weights[None],
        tile_owner.reshape(1, R),
        tile_slot[None],
        batch_blocks,
        batch_atoms,
        batch_weights,
    )
    facts = (facts, swap(facts, X3), swap(facts, Y3), swap(facts, X3 ^ Y3))
    location, sent, *facts = lax.optimization_barrier((atom_places(atom_grid_index), orbitals, *facts))
    half = TILE_DEV // 2
    tile_x, tile_y = swap(dens_tiles, X1), swap(dens_tiles, Y1)
    orb_x, orb_y = swap(sent, X3), swap(sent, Y3)
    tile_low, tile_high = swap(tile_y[:half], X1), swap(tile_x[half:], Y1)
    orb_first, orb_second = swap(orb_y[0], X3), swap(orb_x[1], Y3)
    orbs = (orbitals, orb_x, orb_y, orb_first, orb_second)

    facts = jnp.stack(facts)
    coords = facts[:, :3].transpose(1, 0, 2).reshape(3, LIST_PTS)
    weights = facts[:, 3].reshape(LISTERS * BAT_DEV, PTS)
    owners, slots, blocks = what_is_listed(facts[:, 4])
    near_by = facts[:, 5].reshape(LISTERS, 2, BAT_DEV, TB)[..., :NEAR].reshape(LISTERS, 2, BAT_DEV, NEAR)
    atoms = near_by[:, 0].reshape(LISTERS * BAT_DEV, NEAR).astype(jnp.int32)
    raw_weight = near_by[:, 1].reshape(LISTERS * BAT_DEV, NEAR)
    away = owners ^ me
    tmap = jnp.where((away & 10) == 0, ((away & 1) + ((away >> 2) & 1) * 2) * TILE_DEV + slots, NO_TILE)
    codes, counts = lists_of(owners, slots, me)[0]

    wave_vecs = wave_table(KM)
    squared = jnp.sum(wave_vecs * wave_vecs, axis=0)
    near_gain = jnp.tile(0.1 / (1.0 + 0.1 * squared), 2)[None]
    far_gain = jnp.tile(0.03 / (1.0 + 0.1 * squared), 2)[None]
    phases = jnp.einsum("ca,cm->am", location, wave_vecs, precision=TOP_PRECISION) * (2.0 * math.pi / GRIDN)
    trig = jnp.concatenate([jnp.cos(phases), jnp.sin(phases)], axis=1)
    partition = raw_weight / jnp.sum(raw_weight, axis=1, keepdims=True)
    share = jnp.sum(
        jnp.where(
            atoms[None] == jnp.arange(ATOM_GRP, dtype=jnp.int32)[:, None, None],
            partition[None],
            0.0,
        ),
        axis=2,
    )
    displace = coords[:, None, :] - location[:, :, None]
    envelope = jnp.exp(-2.0 * jnp.sum(displace * displace, axis=0) / (GRIDN * GRIDN))
    spread = (envelope.reshape(ATOM_GRP, LISTERS * BAT_DEV, PTS) * share[:, :, None]).reshape(ATOM_GRP, LIST_PTS)
    wave_high, wave_low = wave_of_points(coords)
    first_tmap, first_blocks = tmap, blocks
    early = (spread, weights, wave_high, wave_low, trig, codes, counts, tmap, blocks)

    tiles = (dens_tiles, tile_x, tile_y, tile_low, tile_high)
    before = first_density(first_tmap, first_blocks, tiles, orbs)
    early, late, *unused = lax.optimization_barrier((early, orbitals, before, tile_low, tile_high, orb_first, orb_second))
    spread, weights, wave_high, wave_low, trig, codes, counts, tmap, blocks = early
    orb_far = swap(late, XY)
    part, orb_diag = density_and_moments(
        tmap, blocks, tiles, orbs, before, spread, weights, wave_high, wave_low, trig, facts[:, 4]
    )
    a = ATOM_GRP
    got = swap(part, X3)
    order = (a + 1, a, a + 3, a + 2)
    part = part + jnp.concatenate([got[:a]] + [got[r : r + 1] for r in order] + [jnp.zeros((LISTERS, KM), F32)])
    got = swap(part, Y3)
    density = part[a] + got[a + 2]
    moments, orb_far = lax.optimization_barrier((part[:a] + got[:a], orb_far))
    orb_far_x, orb_far_y = swap(orb_far, X3), swap(orb_far, Y3)
    got = swap(jnp.concatenate([moments, part[a + LISTERS :]]), X1)
    moments = moments + got[:a]
    got = swap(jnp.concatenate([moments, got[a:]]), Y1)
    orb_diag, moments = lax.optimization_barrier((orb_diag, moments + got[:a]))
    orbs_far = (orb_far, orb_far_x, orb_far_y, swap(orb_diag, XY))
    far_owners, far_slots, far_blocks = what_is_listed(got[a:])
    unused, (own_codes, own_counts), (far_codes, far_counts) = lists_of(far_owners, far_slots, me)
    structure = jnp.sum(moments[:, :1] * trig, axis=0, keepdims=True)
    for bits in (1, 2, 4):
        structure = structure + swap_grp(structure, bits)
    structure, own_codes, own_counts, far_codes, far_counts, far_blocks = lax.optimization_barrier(
        (structure, own_codes, own_counts, far_codes, far_counts, far_blocks)
    )
    structure = structure + swap_grp(structure, 8)
    potential, scale = potential_of(
        moments,
        far_gain * structure,
        near_gain,
        trig,
        spread,
        weights.reshape(1, LIST_PTS),
        wave_high,
        wave_low,
    )
    far_scale = swap(scale, XY)
    own, shared = ham_terms(
        codes, counts, blocks, scale, orbs, (), ((TILE_DEV, F32), (TILE_DEV, F32)), 10**6
    )
    half = TILE_DEV // 2
    part_x, part_y = ham_terms(
        far_codes, far_counts, far_blocks, far_scale, orbs_far, (shared,), ((half, BF16), (half, BF16)), 10**6
    )
    (own,) = ham_terms(
        own_codes, own_counts, far_blocks, far_scale, orbs_far, (own,), ((TILE_DEV, F32),), 2 * 10**10
    )
    return (density, potential.reshape(-1), final_tiles(own, swap(part_x, X1), swap(part_y, Y1)))


def solution(mesh):
    in_specs = (
        P(("grp", "dev"), None, None),
        P(("grp", "dev"), None, None),
        P(None, ("grp", "dev")),
        P(("grp", "dev")),
        P(("grp", "dev"), None),
        P(("grp", "dev"), None),
        P(("grp", "dev")),
        P(("grp", "dev"), None),
        P(("grp", "dev"), None),
        P(None, "grp"),
    )
    out_specs = (P(("grp", "dev")), P(("grp", "dev")), P(("grp", "dev"), None, None))
    return jax.shard_map(
        on_device, mesh=mesh, in_specs=in_specs, out_specs=out_specs, check_vma=False
    )
```

```python
import functools
import math

import jax
import jax.numpy as jnp
from jax import lax
from jax.experimental import pallas as pl
from jax.experimental.pallas import tpu as pltpu
from jax.sharding import PartitionSpec as P

TB = 128
BB = 8
UB = 9
R = 81
PTS = 256
BAT_DEV = 2
KM = 512
HALF = KM // 2
NEAR = 4
TILE_DEV = 32
GRIDN = 64
ATOM_GRP = 16
DEV_PTS = BAT_DEV * PTS
LISTERS = 4
LIST_PTS = LISTERS * DEV_PTS
NO_TILE = 4 * TILE_DEV
PARTS = TILE_DEV + 2 * (TILE_DEV // 2)
GROUP = 4
LIST_LEN = 32
MIB = 1024 * 1024

F32 = jnp.float32
BF16 = jnp.bfloat16
TOP_PRECISION = lax.Precision.HIGHEST
NT = (((1,), (1,)), ((), ()))


def swap(array, bits):
    return lax.ppermute(array, "dev", [(d, d ^ bits) for d in range(16)])


def swap_grp(array, bits):
    return lax.ppermute(array, "grp", [(g, g ^ bits) for g in range(16)])


X1, Y1 = 1, 4
X3, Y3 = 3, 12
XY = 5


def wave_table(count):
    mode_ids = jnp.arange(count // 2, dtype=jnp.int32)
    return jnp.stack([mode_ids % 8, mode_ids // 8 % 8, mode_ids // 64]).astype(F32)


def split_bf16(value):
    high = value.astype(BF16)
    return high, (value - high.astype(F32)).astype(BF16)


def wave_kernel(cs_ref, high_ref, low_ref):
    cos_x, sin_x = cs_ref[0:8], cs_ref[8:16]
    for fz in range(4):
        cos_z, sin_z = cs_ref[32 + fz : 33 + fz], cs_ref[40 + fz : 41 + fz]
        for fy in range(0, 8, 2):
            parts_cos, parts_sin = [], []
            for step in range(2):
                cos_y = cs_ref[16 + fy + step : 17 + fy + step]
                sin_y = cs_ref[24 + fy + step : 25 + fy + step]
                cos_yz = cos_y * cos_z - sin_y * sin_z
                sin_yz = sin_y * cos_z + cos_y * sin_z
                parts_cos.append(cos_x * cos_yz - sin_x * sin_yz)
                parts_sin.append(sin_x * cos_yz + cos_x * sin_yz)
            row = fz * 64 + fy * 8
            for base, parts in ((row, parts_cos), (HALF + row, parts_sin)):
                high, low = split_bf16(jnp.concatenate(parts, axis=0))
                high_ref[base : base + 16] = high
                low_ref[base : base + 16] = low


def wave_of_points(coords):
    points = coords.shape[1]
    chunk = 256
    angle = (jnp.arange(8, dtype=F32)[None, :, None] * coords[:, None, :]) * (2.0 * math.pi / GRIDN)
    cs = jnp.stack([jnp.cos(angle), jnp.sin(angle)], axis=1).reshape(48, points)
    out = jax.ShapeDtypeStruct((KM, points), BF16)
    return pl.pallas_call(
        wave_kernel,
        grid=(points // chunk,),
        in_specs=[pl.BlockSpec((48, chunk), lambda i: (0, i))],
        out_specs=[pl.BlockSpec((KM, chunk), lambda i: (0, i))] * 2,
        out_shape=[out, out],
        cost_estimate=pl.CostEstimate(flops=8 * KM * points, bytes_accessed=4 * KM * points, transcendentals=0),
    )(cs)


def orbital_copies(own_orb, x_orb, y_orb, diag_orbs, orbs, sems):
    return [
        [pltpu.make_async_copy(own_orb, orbs.at[0:2], sems.at[0])],
        [pltpu.make_async_copy(x_orb, orbs.at[2:4], sems.at[1])],
        [pltpu.make_async_copy(y_orb, orbs.at[4:6], sems.at[2])],
        [
            pltpu.make_async_copy(orb, orbs.at[6 + b] if len(diag_orbs) > 1 else orbs.at[6:8], sems.at[3 + b])
            for b, orb in enumerate(diag_orbs)
        ],
    ]


def tile_copies(own_tile, x_tile, y_tile, low_tile, high_tile, tiles, sems):
    half = TILE_DEV // 2
    sources = (
        (own_tile, 0),
        (x_tile, TILE_DEV),
        (y_tile, 2 * TILE_DEV),
        (low_tile, 3 * TILE_DEV),
        (high_tile, 3 * TILE_DEV + half),
    )
    return [
        pltpu.make_async_copy(source, tiles.at[at : at + source.shape[0]], sems.at[n])
        for n, (source, at) in enumerate(sources)
    ]


def batch_density(tmap_ref, blocks_ref, tiles, lister, batch, orb):
    chosen = [blocks_ref[batch, i] for i in range(BB)]
    total = jnp.zeros((PTS, TB), F32)
    for pair in range(BB // 2):
        columns = []
        for j in (2 * pair, 2 * pair + 1):
            columns.append(
                jnp.concatenate([tiles[tmap_ref[lister, chosen[i] * UB + chosen[j]]] for i in range(BB)], axis=0)
            )
        product = jnp.dot(orb[...], jnp.concatenate(columns, axis=1), preferred_element_type=F32)
        for side in range(2):
            block = orb[:, (2 * pair + side) * TB : (2 * pair + side + 1) * TB]
            total = total + product[:, side * TB : (side + 1) * TB] * block.astype(F32)
    return jnp.sum(total.T, axis=0, keepdims=True)


def first_density_kernel(
    tmap_ref,
    blocks_ref,
    own_tile,
    x_tile,
    y_tile,
    low_tile,
    high_tile,
    own_orb,
    x_orb,
    y_orb,
    out_ref,
    tiles,
    orbs,
    sems,
):
    arrivals = tile_copies(own_tile, x_tile, y_tile, low_tile, high_tile, tiles, sems)
    points = orbital_copies(own_orb, x_orb, y_orb, (), orbs, sems.at[5:8])
    for copy in arrivals + sum(points, []):
        copy.start()
    tiles[NO_TILE] = jnp.zeros((TB, TB), BF16)
    out_ref[...] = jnp.zeros(out_ref.shape, F32)
    for copy in arrivals:
        copy.wait()
    for lister in range(LISTERS - 1):
        for copy in points[lister]:
            copy.wait()

        def one_batch(batch, unused, lister=lister):
            out_ref[pl.ds(batch, 1), :] = batch_density(
                tmap_ref, blocks_ref, tiles, lister, batch, orbs.at[batch]
            )
            return unused

        lax.fori_loop(BAT_DEV * lister, BAT_DEV * (lister + 1), one_batch, 0)


def first_density(tmap, blocks, tiles, orbs):
    return pl.pallas_call(
        first_density_kernel,
        in_specs=[SMEM_SPEC] * 2 + [ANY_SPEC] * 8,
        out_specs=VMEM_SPEC,
        out_shape=jax.ShapeDtypeStruct((LISTERS * BAT_DEV, PTS), F32),
        scratch_shapes=[
            pltpu.VMEM((NO_TILE + 1, TB, TB), BF16),
            pltpu.VMEM(((LISTERS - 1) * BAT_DEV, PTS, BB * TB), BF16),
            pltpu.SemaphoreType.DMA((8,)),
        ],
        compiler_params=pltpu.CompilerParams(vmem_limit_bytes=56 * MIB),
        cost_estimate=pl.CostEstimate(flops=2 * 10**10, bytes_accessed=10**4, transcendentals=0),
    )(tmap, blocks, *tiles, *orbs[:3])


def density_kernel(
    tmap_ref,
    blocks_ref,
    own_tile,
    x_tile,
    y_tile,
    low_tile,
    high_tile,
    first_orb,
    second_orb,
    before_ref,
    spread_ref,
    weights_ref,
    high_hbm,
    low_hbm,
    trig_ref,
    rows_ref,
    out_ref,
    diag_out,
    tiles,
    orbs,
    density,
    high_ref,
    low_ref,
    sems,
):
    arrivals = tile_copies(own_tile, x_tile, y_tile, low_tile, high_tile, tiles, sems)
    waves = [
        pltpu.make_async_copy(high_hbm, high_ref, sems.at[5]),
        pltpu.make_async_copy(low_hbm, low_ref, sems.at[6]),
    ]
    points = [
        pltpu.make_async_copy(first_orb, orbs.at[0], sems.at[7]),
        pltpu.make_async_copy(second_orb, orbs.at[1], sems.at[8]),
    ]
    for copy in arrivals + points + waves:
        copy.start()
    tiles[NO_TILE] = jnp.zeros((TB, TB), BF16)
    density[...] = before_ref[...]
    for copy in arrivals + points:
        copy.wait()
    onward = pltpu.make_async_copy(orbs, diag_out, sems.at[9])
    onward.start()

    def one_batch(b, unused):
        batch = BAT_DEV * (LISTERS - 1) + b
        density[pl.ds(batch, 1), :] = batch_density(
            tmap_ref, blocks_ref, tiles, LISTERS - 1, batch, orbs.at[b]
        )
        return unused

    lax.fori_loop(0, BAT_DEV, one_batch, 0)
    for copy in waves:
        copy.wait()
    weighted = density[...] * weights_ref[...]
    charge = jnp.concatenate(
        [spread_ref[:, b * PTS : (b + 1) * PTS] * weighted[b : b + 1] for b in range(LISTERS * BAT_DEV)], axis=1
    )
    charge_high, charge_low = split_bf16(charge)
    both = lax.dot_general(
        jnp.concatenate([charge_high, charge_low], axis=0), high_ref[...], NT, preferred_element_type=F32
    )
    sums = both[:ATOM_GRP] + both[ATOM_GRP:]
    sums = sums + lax.dot_general(charge_high, low_ref[...], NT, preferred_element_type=F32)
    cos_sum, sin_sum = sums[:, :HALF], sums[:, HALF:]
    cos_atom, sin_atom = trig_ref[:, :HALF], trig_ref[:, HALF:]
    out_ref[0:ATOM_GRP, :HALF] = cos_sum * cos_atom + sin_sum * sin_atom
    out_ref[0:ATOM_GRP, HALF:] = sin_sum * cos_atom - cos_sum * sin_atom
    for e in range(LISTERS):
        for b in range(BAT_DEV):
            out_ref[ATOM_GRP + e : ATOM_GRP + e + 1, b * PTS : (b + 1) * PTS] = density[
                BAT_DEV * e + b : BAT_DEV * e + b + 1
            ]
    out_ref[ATOM_GRP + LISTERS :] = rows_ref[...]
    onward.wait()


SMEM_SPEC = pl.BlockSpec(memory_space=pltpu.SMEM)
VMEM_SPEC = pl.BlockSpec(memory_space=pltpu.VMEM)
ANY_SPEC = pl.BlockSpec(memory_space=pl.ANY)


def density_and_moments(tmap, blocks, tiles, orbs, before, spread, weights, wave_high, wave_low, trig, rows):
    return pl.pallas_call(
        density_kernel,
        in_specs=[SMEM_SPEC] * 2 + [ANY_SPEC] * 7 + [VMEM_SPEC] * 3 + [ANY_SPEC] * 2 + [VMEM_SPEC] * 2,
        out_specs=[VMEM_SPEC, ANY_SPEC],
        out_shape=[
            jax.ShapeDtypeStruct((ATOM_GRP + 8, KM), F32),
            jax.ShapeDtypeStruct((BAT_DEV, PTS, BB * TB), BF16),
        ],
        scratch_shapes=[
            pltpu.VMEM((NO_TILE + 1, TB, TB), BF16),
            pltpu.VMEM((BAT_DEV, PTS, BB * TB), BF16),
            pltpu.VMEM((LISTERS * BAT_DEV, PTS), F32),
            pltpu.VMEM((KM, LIST_PTS), BF16),
            pltpu.VMEM((KM, LIST_PTS), BF16),
            pltpu.SemaphoreType.DMA((10,)),
        ],
        compiler_params=pltpu.CompilerParams(vmem_limit_bytes=56 * MIB),
        cost_estimate=pl.CostEstimate(flops=10**6, bytes_accessed=10**4, transcendentals=0),
    )(tmap, blocks, *tiles, *orbs[3:], before, spread, weights, wave_high, wave_low, trig, rows)


def pack_kernel(coords, weights, owner, slot, blocks, atoms, shares, out_ref, owner_ref, slot_ref, blocks_ref, atoms_ref, shares_ref, sems):
    copies = [
        pltpu.make_async_copy(source, target, sems.at[n])
        for n, (source, target) in enumerate(
            (
                (coords, out_ref.at[0:3]),
                (weights, out_ref.at[3:4]),
                (owner, owner_ref),
                (slot, slot_ref),
                (blocks, blocks_ref),
                (atoms, atoms_ref),
                (shares, shares_ref),
            )
        )
    ]
    out_ref[4:6] = jnp.zeros((2, DEV_PTS), F32)
    for copy in copies:
        copy.start()
    for copy in copies:
        copy.wait()
    out_ref[4:5, :R] = owner_ref[...].astype(F32)
    out_ref[4:5, TB : TB + R] = slot_ref[...].astype(F32)
    for b in range(BAT_DEV):
        out_ref[4:5, (2 + b) * TB : (2 + b) * TB + BB] = blocks_ref[b : b + 1].astype(F32)
        out_ref[5:6, b * TB : b * TB + NEAR] = atoms_ref[b : b + 1].astype(F32)
        out_ref[5:6, (2 + b) * TB : (2 + b) * TB + NEAR] = shares_ref[b : b + 1].astype(F32)


def place_kernel(index_ref, out_ref):
    out_ref[...] = index_ref[...].astype(F32)


def atom_places(index):
    return pl.pallas_call(
        place_kernel,
        in_specs=[VMEM_SPEC],
        out_specs=VMEM_SPEC,
        out_shape=jax.ShapeDtypeStruct(index.shape, F32),
        cost_estimate=pl.CostEstimate(flops=2 * 10**10, bytes_accessed=1000, transcendentals=0),
    )(index)


def packed_facts(*parts):
    return pl.pallas_call(
        pack_kernel,
        in_specs=[ANY_SPEC] * 7,
        out_specs=VMEM_SPEC,
        out_shape=jax.ShapeDtypeStruct((6, DEV_PTS), F32),
        scratch_shapes=[pltpu.VMEM(part.shape, part.dtype) for part in parts[2:]] + [pltpu.SemaphoreType.DMA((7,))],
        compiler_params=pltpu.CompilerParams(vmem_limit_bytes=56 * MIB),
        cost_estimate=pl.CostEstimate(flops=1000, bytes_accessed=1000, transcendentals=0),
    )(*parts)


def add_ham(table_ref, base, copies, orbs, scale, ham, turned, scaled):
    for e in range(LISTERS):
        for copy in copies[e]:
            copy.wait()
        for b in range(BAT_DEV):
            source = orbs.at[BAT_DEV * e + b]
            factors = []
            for part in range(PTS // TB):
                at = e * DEV_PTS + b * PTS + part * TB
                factors.append(jnp.broadcast_to(scale[:, at : at + TB], (TB, TB)).T)
            missing = UB * (UB - 1) // 2
            for i in range(BB):
                block = table_ref[e, (2 + b) * TB + i]
                missing = missing - block
                turned[block, :, b * PTS : (b + 1) * PTS] = source[:, i * TB : (i + 1) * TB].T
                for part in range(PTS // TB):
                    piece = source[part * TB : (part + 1) * TB, i * TB : (i + 1) * TB]
                    rows = slice(b * PTS + part * TB, b * PTS + (part + 1) * TB)
                    scaled[block, rows, :] = (factors[part] * piece.astype(F32)).astype(BF16)
            scaled[missing, b * PTS : (b + 1) * PTS, :] = jnp.zeros((PTS, TB), BF16)
            turned[missing, :, b * PTS : (b + 1) * PTS] = jnp.zeros((TB, PTS), BF16)

        def some_items(step, unused):
            for item in range(GROUP):
                code = table_ref[e, base + step * GROUP + item]
                tile = code & 255
                i = (code >> 8) & 15
                j = code >> 12
                ham[tile] += jnp.dot(turned[i], scaled[j], preferred_element_type=F32)
            return unused

        lax.fori_loop(0, table_ref[e, base + LIST_LEN], some_items, 0)


def potential_kernel(
    moments_ref, far_ref, near_ref, trig_ref, spread_ref, weights_ref, high_ref, low_ref, pot_ref, scale_ref
):
    cos_atom, sin_atom = trig_ref[:, :HALF], trig_ref[:, HALF:]
    cos_near = moments_ref[:, :HALF] * near_ref[:, :HALF]
    sin_near = moments_ref[:, HALF:] * near_ref[:, HALF:]
    turned_cos = cos_near * cos_atom - sin_near * sin_atom
    turned_sin = cos_near * sin_atom + sin_near * cos_atom
    coef = jnp.concatenate(
        [
            jnp.concatenate([turned_cos, turned_sin], axis=1),
            jnp.concatenate([far_ref[...], jnp.zeros((ATOM_GRP - 1, KM), F32)], axis=0),
        ],
        axis=0,
    )
    coef_high, coef_low = split_bf16(coef)
    both = jnp.dot(jnp.concatenate([coef_high, coef_low], axis=0), high_ref[...], preferred_element_type=F32)
    values = both[: 2 * ATOM_GRP] + both[2 * ATOM_GRP :]
    values = values + jnp.dot(coef_high, low_ref[...], preferred_element_type=F32)
    pot = jnp.sum(values[:ATOM_GRP] * spread_ref[...], axis=0, keepdims=True) + values[ATOM_GRP : ATOM_GRP + 1]
    pot_ref[...] = pot[:, :DEV_PTS]
    scale_ref[...] = pot * weights_ref[...]


def potential_of(moments, far, near, trig, spread, weights, wave_high, wave_low):
    return pl.pallas_call(
        potential_kernel,
        in_specs=[VMEM_SPEC] * 8,
        out_specs=[VMEM_SPEC] * 2,
        out_shape=[jax.ShapeDtypeStruct((1, DEV_PTS), F32), jax.ShapeDtypeStruct((1, LIST_PTS), F32)],
        compiler_params=pltpu.CompilerParams(vmem_limit_bytes=16 * MIB),
        cost_estimate=pl.CostEstimate(flops=10**6, bytes_accessed=10**4, transcendentals=0),
    )(moments, far, near, trig, spread, weights, wave_high, wave_low)


def ham_kernel(n_starts, n_outs, base, table_ref, scale_ref, *refs):
    n_orbs = len(refs) - n_starts - n_outs - 5
    orb_refs, refs = refs[:n_orbs], refs[n_orbs:]
    starts, outs, (ham, turned, scaled, orbs, sems) = refs[:n_starts], refs[n_starts : n_starts + n_outs], refs[-5:]
    tiles = ham.shape[0] - 1
    copies = orbital_copies(*orb_refs[:3], orb_refs[3:], orbs, sems)
    for start in starts:
        copies[0].append(pltpu.make_async_copy(start, ham.at[0:tiles], sems.at[5]))
    for copy in sum(copies, []):
        copy.start()
    if n_starts == 0:

        def clear(t, unused):
            ham[t] = jnp.zeros((TB, TB), F32)
            return unused

        lax.fori_loop(0, tiles, clear, 0)
    add_ham(table_ref, base, copies, orbs, scale_ref[...], ham, turned, scaled)
    at = 0
    for out in outs:
        out[...] = ham[at : at + out.shape[0]].astype(out.dtype)
        at = at + out.shape[0]


def ham_terms(table, base, scale, orbs, starts, outs, flops):
    tiles = sum(count for count, unused in outs)
    return pl.pallas_call(
        functools.partial(ham_kernel, len(starts), len(outs), base),
        in_specs=[SMEM_SPEC, VMEM_SPEC] + [ANY_SPEC] * (len(orbs) + len(starts)),
        out_specs=[VMEM_SPEC] * len(outs),
        out_shape=[jax.ShapeDtypeStruct((count, TB, TB), dtype) for count, dtype in outs],
        scratch_shapes=[
            pltpu.VMEM((tiles + 1, TB, TB), F32),
            pltpu.VMEM((UB, TB, DEV_PTS), BF16),
            pltpu.VMEM((UB, DEV_PTS, TB), BF16),
            pltpu.VMEM((LISTERS * BAT_DEV, PTS, BB * TB), BF16),
            pltpu.SemaphoreType.DMA((6,)),
        ],
        compiler_params=pltpu.CompilerParams(vmem_limit_bytes=56 * MIB),
        cost_estimate=pl.CostEstimate(flops=flops, bytes_accessed=10**4, transcendentals=0),
    )(table, scale, *orbs, *starts)


def final_kernel(own_ref, x_ref, y_ref, out_ref):
    half = TILE_DEV // 2
    step = half // 2
    got = jnp.where(pl.program_id(0) < half // step, x_ref[...].astype(F32), y_ref[...].astype(F32))
    out_ref[...] = (own_ref[...] + got).astype(BF16)


def final_tiles(own, got_x, got_y):
    step = TILE_DEV // 4
    block = (step, TB, TB)
    return pl.pallas_call(
        final_kernel,
        grid=(4,),
        in_specs=[
            pl.BlockSpec(block, lambda t: (t, 0, 0)),
            pl.BlockSpec(block, lambda t: (jnp.minimum(t, 1), 0, 0)),
            pl.BlockSpec(block, lambda t: (jnp.maximum(t - 2, 0), 0, 0)),
        ],
        out_specs=pl.BlockSpec(block, lambda t: (t, 0, 0)),
        out_shape=jax.ShapeDtypeStruct((TILE_DEV, TB, TB), BF16),
        compiler_params=pltpu.CompilerParams(vmem_limit_bytes=16 * MIB),
        cost_estimate=pl.CostEstimate(flops=10**6, bytes_accessed=10**4, transcendentals=0),
    )(own, got_x, got_y)


def kept_of(mine, places):
    rows = jnp.arange(R, dtype=jnp.int32)
    codes = places + (rows // UB) * 256 + (rows % UB) * 4096
    before = (rows[:, None] < rows[None, :])[None] & mine[:, :, None]
    rank = jnp.sum(before.astype(jnp.int32), axis=1)
    counts = jnp.sum(mine.astype(jnp.int32), axis=1)
    at = jnp.arange(LIST_LEN, dtype=jnp.int32)
    hit = (rank[:, None, :] == at[None, :, None]) & mine[:, None, :]
    listed = jnp.sum(jnp.where(hit, codes[:, None, :], 0), axis=2)
    return listed, counts, at


def table_of(lists, blocks):
    parts = []
    for listed, groups in lists:
        part = jnp.concatenate([listed, groups[:, None]], axis=1)
        parts.append(jnp.pad(part, ((0, 0), (0, TB - part.shape[1]))))
    blocks = jnp.pad(blocks, ((0, 0), (0, TB - BB))).reshape(LISTERS, BAT_DEV * TB)
    return jnp.concatenate(parts + [parts[-1]] * (2 - len(parts)) + [blocks], axis=1)


def lists_of(owners, slots, me, apart):
    half = TILE_DEV // 2
    away = owners ^ me
    own = away == 0
    shared = ((away == X1) & (slots < half)) | ((away == Y1) & (slots >= half))
    found = []
    for mine in (own, shared) if apart else (own | shared,):
        place = slots if apart else jnp.where(own, slots, TILE_DEV + slots)
        listed, counts, at = kept_of(mine, place)
        dummy = TILE_DEV if apart else PARTS
        found.append((jnp.where(at[None] < counts[:, None], listed, dummy), (counts + GROUP - 1) // GROUP))
    return found


def what_is_listed(rows):
    ints = rows.astype(jnp.int32)
    blocks = ints[:, 2 * TB :].reshape(LISTERS * BAT_DEV, TB)[:, :BB]
    return ints[:, :R], ints[:, TB : TB + R], blocks


def on_device(
    orbitals,
    dens_tiles,
    point_coords,
    point_weights,
    batch_blocks,
    tile_owner,
    tile_slot,
    batch_atoms,
    batch_weights,
    atom_grid_index,
):
    me = lax.axis_index("dev").astype(jnp.int32)

    facts = packed_facts(
        point_coords,
        point_weights[None],
        tile_owner.reshape(1, R),
        tile_slot[None],
        batch_blocks,
        batch_atoms,
        batch_weights,
    )
    facts = (facts, swap(facts, X3), swap(facts, Y3), swap(facts, X3 ^ Y3))
    location, sent, *facts = lax.optimization_barrier((atom_places(atom_grid_index), orbitals, *facts))
    half = TILE_DEV // 2
    tile_x, tile_y = swap(dens_tiles, X1), swap(dens_tiles, Y1)
    orb_x, orb_y = swap(sent, X3), swap(sent, Y3)

    facts = jnp.stack(facts)
    coords = facts[:, :3].transpose(1, 0, 2).reshape(3, LIST_PTS)
    weights = facts[:, 3].reshape(LISTERS * BAT_DEV, PTS)
    owners, slots, blocks = what_is_listed(facts[:, 4])
    near_by = facts[:, 5].reshape(LISTERS, 2, BAT_DEV, TB)[..., :NEAR].reshape(LISTERS, 2, BAT_DEV, NEAR)
    atoms = near_by[:, 0].reshape(LISTERS * BAT_DEV, NEAR).astype(jnp.int32)
    raw_weight = near_by[:, 1].reshape(LISTERS * BAT_DEV, NEAR)
    away = owners ^ me
    tmap = jnp.where((away & 10) == 0, ((away & 1) + ((away >> 2) & 1) * 2) * TILE_DEV + slots, NO_TILE)
    table = table_of(lists_of(owners, slots, me, False), blocks)
    mate_table = table_of(lists_of(owners, slots, me ^ XY, True), blocks).astype(F32)

    wave_vecs = wave_table(KM)
    squared = jnp.sum(wave_vecs * wave_vecs, axis=0)
    near_gain = jnp.tile(0.1 / (1.0 + 0.1 * squared), 2)[None]
    far_gain = jnp.tile(0.03 / (1.0 + 0.1 * squared), 2)[None]
    phases = jnp.einsum("ca,cm->am", location, wave_vecs, precision=TOP_PRECISION) * (2.0 * math.pi / GRIDN)
    trig = jnp.concatenate([jnp.cos(phases), jnp.sin(phases)], axis=1)
    partition = raw_weight / jnp.sum(raw_weight, axis=1, keepdims=True)
    share = jnp.sum(
        jnp.where(
            atoms[None] == jnp.arange(ATOM_GRP, dtype=jnp.int32)[:, None, None],
            partition[None],
            0.0,
        ),
        axis=2,
    )
    displace = coords[:, None, :] - location[:, :, None]
    envelope = jnp.exp(-2.0 * jnp.sum(displace * displace, axis=0) / (GRIDN * GRIDN))
    spread = (envelope.reshape(ATOM_GRP, LISTERS * BAT_DEV, PTS) * share[:, :, None]).reshape(ATOM_GRP, LIST_PTS)
    wave_high, wave_low = wave_of_points(coords)
    first_tmap, first_blocks = tmap, blocks

    wave_high, wave_low, onward = lax.optimization_barrier((wave_high, wave_low, tile_y[:half]))
    tile_low, tile_high = swap(onward, X1), swap(tile_x[half:], Y1)
    orb_first, orb_second = swap(orb_y[0], X3), swap(orb_x[1], Y3)
    orbs = (orbitals, orb_x, orb_y, orb_first, orb_second)
    early = (spread, weights, wave_high, wave_low, trig, table, mate_table, tmap, blocks)
    tiles = (dens_tiles, tile_x, tile_y, tile_low, tile_high)
    before = first_density(first_tmap, first_blocks, tiles, orbs)
    early, late, *unused = lax.optimization_barrier((early, orbitals, before, tile_low, tile_high, orb_first, orb_second))
    spread, weights, wave_high, wave_low, trig, table, mate_table, tmap, blocks = early
    orb_far = swap(late, XY)
    part, orb_diag = density_and_moments(
        tmap, blocks, tiles, orbs, before, spread, weights, wave_high, wave_low, trig, mate_table
    )
    a = ATOM_GRP
    got = swap(part, X3)
    order = (a + 1, a, a + 3, a + 2)
    part = part + jnp.concatenate([got[:a]] + [got[r : r + 1] for r in order] + [jnp.zeros((LISTERS, KM), F32)])
    got = swap(part, Y3)
    density_got = got[a + 2]
    moments, orb_far = lax.optimization_barrier((part[:a] + got[:a], orb_far))
    orb_far_x, orb_far_y = swap(orb_far, X3), swap(orb_far, Y3)
    got = swap(jnp.concatenate([moments, part[a + LISTERS :]]), X1)
    moments = moments + got[:a]
    got = swap(jnp.concatenate([moments, got[a:]]), Y1)
    orb_diag, moments = lax.optimization_barrier((orb_diag, moments + got[:a]))
    orbs_far = (orb_far, orb_far_x, orb_far_y, swap(orb_diag, XY))
    far_table = got[a:].astype(jnp.int32)
    structure = jnp.sum(moments[:, :1] * trig, axis=0, keepdims=True)
    for bits in (1, 2, 4):
        structure = structure + swap_grp(structure, bits)
    structure = structure + swap_grp(structure, 8)
    potential, scale = potential_of(
        moments,
        far_gain * structure,
        near_gain,
        trig,
        spread,
        weights.reshape(1, LIST_PTS),
        wave_high,
        wave_low,
    )
    far_scale = swap(scale, XY)
    own, shared = ham_terms(table, 0, scale, orbs, (), ((TILE_DEV, F32), (TILE_DEV, F32)), 10**6)
    half = TILE_DEV // 2
    part_x, part_y = ham_terms(
        far_table, TB, far_scale, orbs_far, (shared,), ((half, BF16), (half, BF16)), 10**6
    )
    (own,) = ham_terms(far_table, 0, far_scale, orbs_far, (own,), ((TILE_DEV, F32),), 2 * 10**10)
    density, other, part_x = lax.optimization_barrier((part[a], density_got, part_x))
    return (density + other, potential.reshape(-1), final_tiles(own, swap(part_x, X1), swap(part_y, Y1)))


def solution(mesh):
    in_specs = (
        P(("grp", "dev"), None, None),
        P(("grp", "dev"), None, None),
        P(None, ("grp", "dev")),
        P(("grp", "dev")),
        P(("grp", "dev"), None),
        P(("grp", "dev"), None),
        P(("grp", "dev")),
        P(("grp", "dev"), None),
        P(("grp", "dev"), None),
        P(None, "grp"),
    )
    out_specs = (P(("grp", "dev")), P(("grp", "dev")), P(("grp", "dev"), None, None))
    return jax.shard_map(
        on_device, mesh=mesh, in_specs=in_specs, out_specs=out_specs, check_vma=False
    )
```

```python
import functools
import math

import jax
import jax.numpy as jnp
from jax import lax
from jax.experimental import pallas as pl
from jax.experimental.pallas import tpu as pltpu
from jax.sharding import PartitionSpec as P

TB = 128
BB = 8
UB = 9
R = 81
PTS = 256
BAT_DEV = 2
KM = 512
HALF = KM // 2
NEAR = 4
TILE_DEV = 32
GRIDN = 64
ATOM_GRP = 16
DEV_PTS = BAT_DEV * PTS
LISTERS = 4
LIST_PTS = LISTERS * DEV_PTS
NO_TILE = 4 * TILE_DEV
PARTS = TILE_DEV + 2 * (TILE_DEV // 2)
GROUP = 4
LIST_LEN = 32
MIB = 1024 * 1024

F32 = jnp.float32
BF16 = jnp.bfloat16
TOP_PRECISION = lax.Precision.HIGHEST
NT = (((1,), (1,)), ((), ()))


def swap(array, bits):
    return lax.ppermute(array, "dev", [(d, d ^ bits) for d in range(16)])


def swap_grp(array, bits):
    return lax.ppermute(array, "grp", [(g, g ^ bits) for g in range(16)])


X1, Y1 = 1, 4
X3, Y3 = 3, 12
XY = 5


def wave_table(count):
    mode_ids = jnp.arange(count // 2, dtype=jnp.int32)
    return jnp.stack([mode_ids % 8, mode_ids // 8 % 8, mode_ids // 64]).astype(F32)


def split_bf16(value):
    high = value.astype(BF16)
    return high, (value - high.astype(F32)).astype(BF16)


def wave_kernel(cs_ref, high_ref, low_ref):
    cos_x, sin_x = cs_ref[0:8], cs_ref[8:16]
    for fz in range(4):
        cos_z, sin_z = cs_ref[32 + fz : 33 + fz], cs_ref[40 + fz : 41 + fz]
        for fy in range(0, 8, 2):
            parts_cos, parts_sin = [], []
            for step in range(2):
                cos_y = cs_ref[16 + fy + step : 17 + fy + step]
                sin_y = cs_ref[24 + fy + step : 25 + fy + step]
                cos_yz = cos_y * cos_z - sin_y * sin_z
                sin_yz = sin_y * cos_z + cos_y * sin_z
                parts_cos.append(cos_x * cos_yz - sin_x * sin_yz)
                parts_sin.append(sin_x * cos_yz + cos_x * sin_yz)
            row = fz * 64 + fy * 8
            for base, parts in ((row, parts_cos), (HALF + row, parts_sin)):
                high, low = split_bf16(jnp.concatenate(parts, axis=0))
                high_ref[base : base + 16] = high
                low_ref[base : base + 16] = low


def wave_of_points(coords):
    points = coords.shape[1]
    chunk = 256
    angle = (jnp.arange(8, dtype=F32)[None, :, None] * coords[:, None, :]) * (2.0 * math.pi / GRIDN)
    cs = jnp.stack([jnp.cos(angle), jnp.sin(angle)], axis=1).reshape(48, points)
    out = jax.ShapeDtypeStruct((KM, points), BF16)
    return pl.pallas_call(
        wave_kernel,
        grid=(points // chunk,),
        in_specs=[pl.BlockSpec((48, chunk), lambda i: (0, i))],
        out_specs=[pl.BlockSpec((KM, chunk), lambda i: (0, i))] * 2,
        out_shape=[out, out],
        cost_estimate=pl.CostEstimate(flops=8 * KM * points, bytes_accessed=4 * KM * points, transcendentals=0),
    )(cs)


def orbital_copies(own_orb, x_orb, y_orb, diag_orbs, orbs, sems):
    return [
        [pltpu.make_async_copy(own_orb, orbs.at[0:2], sems.at[0])],
        [pltpu.make_async_copy(x_orb, orbs.at[2:4], sems.at[1])],
        [pltpu.make_async_copy(y_orb, orbs.at[4:6], sems.at[2])],
        [
            pltpu.make_async_copy(orb, orbs.at[6 + b] if len(diag_orbs) > 1 else orbs.at[6:8], sems.at[3 + b])
            for b, orb in enumerate(diag_orbs)
        ],
    ]


def tile_copies(own_tile, x_tile, y_tile, low_tile, high_tile, tiles, sems):
    half = TILE_DEV // 2
    sources = (
        (own_tile, 0),
        (x_tile, TILE_DEV),
        (y_tile, 2 * TILE_DEV),
        (low_tile, 3 * TILE_DEV),
        (high_tile, 3 * TILE_DEV + half),
    )
    return [
        pltpu.make_async_copy(source, tiles.at[at : at + source.shape[0]], sems.at[n])
        for n, (source, at) in enumerate(sources)
    ]


def batch_density(tmap_ref, blocks_ref, tiles, lister, batch, orb):
    chosen = [blocks_ref[batch, i] for i in range(BB)]
    total = jnp.zeros((PTS, TB), F32)
    for pair in range(BB // 2):
        columns = []
        for j in (2 * pair, 2 * pair + 1):
            columns.append(
                jnp.concatenate([tiles[tmap_ref[lister, chosen[i] * UB + chosen[j]]] for i in range(BB)], axis=0)
            )
        product = jnp.dot(orb[...], jnp.concatenate(columns, axis=1), preferred_element_type=F32)
        for side in range(2):
            block = orb[:, (2 * pair + side) * TB : (2 * pair + side + 1) * TB]
            total = total + product[:, side * TB : (side + 1) * TB] * block.astype(F32)
    return jnp.sum(total.T, axis=0, keepdims=True)


def first_density_kernel(
    tmap_ref,
    blocks_ref,
    own_tile,
    x_tile,
    y_tile,
    low_tile,
    high_tile,
    own_orb,
    x_orb,
    y_orb,
    out_ref,
    tiles,
    orbs,
    sems,
):
    arrivals = tile_copies(own_tile, x_tile, y_tile, low_tile, high_tile, tiles, sems)
    points = orbital_copies(own_orb, x_orb, y_orb, (), orbs, sems.at[5:8])
    for copy in arrivals + sum(points, []):
        copy.start()
    tiles[NO_TILE] = jnp.zeros((TB, TB), BF16)
    out_ref[...] = jnp.zeros(out_ref.shape, F32)
    for copy in arrivals:
        copy.wait()
    for lister in range(LISTERS - 1):
        for copy in points[lister]:
            copy.wait()

        def one_batch(batch, unused, lister=lister):
            out_ref[pl.ds(batch, 1), :] = batch_density(
                tmap_ref, blocks_ref, tiles, lister, batch, orbs.at[batch]
            )
            return unused

        lax.fori_loop(BAT_DEV * lister, BAT_DEV * (lister + 1), one_batch, 0)


def first_density(tmap, blocks, tiles, orbs):
    return pl.pallas_call(
        first_density_kernel,
        in_specs=[SMEM_SPEC] * 2 + [ANY_SPEC] * 8,
        out_specs=VMEM_SPEC,
        out_shape=jax.ShapeDtypeStruct((LISTERS * BAT_DEV, PTS), F32),
        scratch_shapes=[
            pltpu.VMEM((NO_TILE + 1, TB, TB), BF16),
            pltpu.VMEM(((LISTERS - 1) * BAT_DEV, PTS, BB * TB), BF16),
            pltpu.SemaphoreType.DMA((8,)),
        ],
        compiler_params=pltpu.CompilerParams(vmem_limit_bytes=56 * MIB),
        cost_estimate=pl.CostEstimate(flops=2 * 10**10, bytes_accessed=10**4, transcendentals=0),
    )(tmap, blocks, *tiles, *orbs[:3])


def density_kernel(
    tmap_ref,
    blocks_ref,
    own_tile,
    x_tile,
    y_tile,
    low_tile,
    high_tile,
    first_orb,
    second_orb,
    before_ref,
    spread_ref,
    weights_ref,
    high_hbm,
    low_hbm,
    trig_ref,
    rows_ref,
    out_ref,
    diag_out,
    tiles,
    orbs,
    density,
    high_ref,
    low_ref,
    sems,
):
    arrivals = tile_copies(own_tile, x_tile, y_tile, low_tile, high_tile, tiles, sems)
    waves = [
        pltpu.make_async_copy(high_hbm, high_ref, sems.at[5]),
        pltpu.make_async_copy(low_hbm, low_ref, sems.at[6]),
    ]
    points = [
        pltpu.make_async_copy(first_orb, orbs.at[0], sems.at[7]),
        pltpu.make_async_copy(second_orb, orbs.at[1], sems.at[8]),
    ]
    for copy in arrivals + points + waves:
        copy.start()
    tiles[NO_TILE] = jnp.zeros((TB, TB), BF16)
    density[...] = before_ref[...]
    for copy in arrivals + points:
        copy.wait()
    onward = pltpu.make_async_copy(orbs, diag_out, sems.at[9])
    onward.start()

    def one_batch(b, unused):
        batch = BAT_DEV * (LISTERS - 1) + b
        density[pl.ds(batch, 1), :] = batch_density(
            tmap_ref, blocks_ref, tiles, LISTERS - 1, batch, orbs.at[b]
        )
        return unused

    lax.fori_loop(0, BAT_DEV, one_batch, 0)
    for copy in waves:
        copy.wait()
    weighted = density[...] * weights_ref[...]
    charge = jnp.concatenate(
        [spread_ref[:, b * PTS : (b + 1) * PTS] * weighted[b : b + 1] for b in range(LISTERS * BAT_DEV)], axis=1
    )
    charge_high, charge_low = split_bf16(charge)
    both = lax.dot_general(
        jnp.concatenate([charge_high, charge_low], axis=0), high_ref[...], NT, preferred_element_type=F32
    )
    sums = both[:ATOM_GRP] + both[ATOM_GRP:]
    sums = sums + lax.dot_general(charge_high, low_ref[...], NT, preferred_element_type=F32)
    cos_sum, sin_sum = sums[:, :HALF], sums[:, HALF:]
    cos_atom, sin_atom = trig_ref[:, :HALF], trig_ref[:, HALF:]
    out_ref[0:ATOM_GRP, :HALF] = cos_sum * cos_atom + sin_sum * sin_atom
    out_ref[0:ATOM_GRP, HALF:] = sin_sum * cos_atom - cos_sum * sin_atom
    for e in range(LISTERS):
        for b in range(BAT_DEV):
            out_ref[ATOM_GRP + e : ATOM_GRP + e + 1, b * PTS : (b + 1) * PTS] = density[
                BAT_DEV * e + b : BAT_DEV * e + b + 1
            ]
    out_ref[ATOM_GRP + LISTERS :] = rows_ref[...]
    onward.wait()


SMEM_SPEC = pl.BlockSpec(memory_space=pltpu.SMEM)
VMEM_SPEC = pl.BlockSpec(memory_space=pltpu.VMEM)
ANY_SPEC = pl.BlockSpec(memory_space=pl.ANY)


def density_and_moments(tmap, blocks, tiles, orbs, before, spread, weights, wave_high, wave_low, trig, rows):
    return pl.pallas_call(
        density_kernel,
        in_specs=[SMEM_SPEC] * 2 + [ANY_SPEC] * 7 + [VMEM_SPEC] * 3 + [ANY_SPEC] * 2 + [VMEM_SPEC] * 2,
        out_specs=[VMEM_SPEC, ANY_SPEC],
        out_shape=[
            jax.ShapeDtypeStruct((ATOM_GRP + 8, KM), F32),
            jax.ShapeDtypeStruct((BAT_DEV, PTS, BB * TB), BF16),
        ],
        scratch_shapes=[
            pltpu.VMEM((NO_TILE + 1, TB, TB), BF16),
            pltpu.VMEM((BAT_DEV, PTS, BB * TB), BF16),
            pltpu.VMEM((LISTERS * BAT_DEV, PTS), F32),
            pltpu.VMEM((KM, LIST_PTS), BF16),
            pltpu.VMEM((KM, LIST_PTS), BF16),
            pltpu.SemaphoreType.DMA((10,)),
        ],
        compiler_params=pltpu.CompilerParams(vmem_limit_bytes=56 * MIB),
        cost_estimate=pl.CostEstimate(flops=10**6, bytes_accessed=10**4, transcendentals=0),
    )(tmap, blocks, *tiles, *orbs[3:], before, spread, weights, wave_high, wave_low, trig, rows)


def pack_kernel(coords, weights, owner, slot, blocks, atoms, shares, out_ref, owner_ref, slot_ref, blocks_ref, atoms_ref, shares_ref, sems):
    copies = [
        pltpu.make_async_copy(source, target, sems.at[n])
        for n, (source, target) in enumerate(
            (
                (coords, out_ref.at[0:3]),
                (weights, out_ref.at[3:4]),
                (owner, owner_ref),
                (slot, slot_ref),
                (blocks, blocks_ref),
                (atoms, atoms_ref),
                (shares, shares_ref),
            )
        )
    ]
    out_ref[4:6] = jnp.zeros((2, DEV_PTS), F32)
    for copy in copies:
        copy.start()
    for copy in copies:
        copy.wait()
    out_ref[4:5, :R] = owner_ref[...].astype(F32)
    out_ref[4:5, TB : TB + R] = slot_ref[...].astype(F32)
    for b in range(BAT_DEV):
        out_ref[4:5, (2 + b) * TB : (2 + b) * TB + BB] = blocks_ref[b : b + 1].astype(F32)
        out_ref[5:6, b * TB : b * TB + NEAR] = atoms_ref[b : b + 1].astype(F32)
        out_ref[5:6, (2 + b) * TB : (2 + b) * TB + NEAR] = shares_ref[b : b + 1].astype(F32)


def place_kernel(index_ref, out_ref):
    out_ref[...] = index_ref[...].astype(F32)


def atom_places(index):
    return pl.pallas_call(
        place_kernel,
        in_specs=[VMEM_SPEC],
        out_specs=VMEM_SPEC,
        out_shape=jax.ShapeDtypeStruct(index.shape, F32),
        cost_estimate=pl.CostEstimate(flops=2 * 10**10, bytes_accessed=1000, transcendentals=0),
    )(index)


def packed_facts(*parts):
    return pl.pallas_call(
        pack_kernel,
        in_specs=[ANY_SPEC] * 7,
        out_specs=VMEM_SPEC,
        out_shape=jax.ShapeDtypeStruct((6, DEV_PTS), F32),
        scratch_shapes=[pltpu.VMEM(part.shape, part.dtype) for part in parts[2:]] + [pltpu.SemaphoreType.DMA((7,))],
        compiler_params=pltpu.CompilerParams(vmem_limit_bytes=56 * MIB),
        cost_estimate=pl.CostEstimate(flops=1000, bytes_accessed=1000, transcendentals=0),
    )(*parts)


def add_ham(codes_ref, counts_ref, blocks_ref, copies, orbs, scale, ham, turned, scaled):
    for e in range(LISTERS):
        for copy in copies[e]:
            copy.wait()
        for b in range(BAT_DEV):
            source = orbs.at[BAT_DEV * e + b]
            factors = []
            for part in range(PTS // TB):
                at = e * DEV_PTS + b * PTS + part * TB
                factors.append(jnp.broadcast_to(scale[:, at : at + TB], (TB, TB)).T)
            missing = UB * (UB - 1) // 2
            for i in range(BB):
                block = blocks_ref[BAT_DEV * e + b, i]
                missing = missing - block
                turned[block, :, b * PTS : (b + 1) * PTS] = source[:, i * TB : (i + 1) * TB].T
                for part in range(PTS // TB):
                    piece = source[part * TB : (part + 1) * TB, i * TB : (i + 1) * TB]
                    rows = slice(b * PTS + part * TB, b * PTS + (part + 1) * TB)
                    scaled[block, rows, :] = (factors[part] * piece.astype(F32)).astype(BF16)
            scaled[missing, b * PTS : (b + 1) * PTS, :] = jnp.zeros((PTS, TB), BF16)
            turned[missing, :, b * PTS : (b + 1) * PTS] = jnp.zeros((TB, PTS), BF16)

        def some_items(step, unused):
            for item in range(GROUP):
                code = codes_ref[e, step * GROUP + item]
                tile = code & 255
                i = (code >> 8) & 15
                j = code >> 12
                ham[tile] += jnp.dot(turned[i], scaled[j], preferred_element_type=F32)
            return unused

        lax.fori_loop(0, counts_ref[e], some_items, 0)


def potential_kernel(
    moments_ref, far_ref, near_ref, trig_ref, spread_ref, weights_ref, high_ref, low_ref, pot_ref, scale_ref
):
    cos_atom, sin_atom = trig_ref[:, :HALF], trig_ref[:, HALF:]
    cos_near = moments_ref[:, :HALF] * near_ref[:, :HALF]
    sin_near = moments_ref[:, HALF:] * near_ref[:, HALF:]
    turned_cos = cos_near * cos_atom - sin_near * sin_atom
    turned_sin = cos_near * sin_atom + sin_near * cos_atom
    coef = jnp.concatenate(
        [
            jnp.concatenate([turned_cos, turned_sin], axis=1),
            jnp.concatenate([far_ref[...], jnp.zeros((ATOM_GRP - 1, KM), F32)], axis=0),
        ],
        axis=0,
    )
    coef_high, coef_low = split_bf16(coef)
    both = jnp.dot(jnp.concatenate([coef_high, coef_low], axis=0), high_ref[...], preferred_element_type=F32)
    values = both[: 2 * ATOM_GRP] + both[2 * ATOM_GRP :]
    values = values + jnp.dot(coef_high, low_ref[...], preferred_element_type=F32)
    pot = jnp.sum(values[:ATOM_GRP] * spread_ref[...], axis=0, keepdims=True) + values[ATOM_GRP : ATOM_GRP + 1]
    pot_ref[...] = pot[:, :DEV_PTS]
    scale_ref[...] = pot * weights_ref[...]


def potential_of(moments, far, near, trig, spread, weights, wave_high, wave_low):
    return pl.pallas_call(
        potential_kernel,
        in_specs=[VMEM_SPEC] * 8,
        out_specs=[VMEM_SPEC] * 2,
        out_shape=[jax.ShapeDtypeStruct((1, DEV_PTS), F32), jax.ShapeDtypeStruct((1, LIST_PTS), F32)],
        compiler_params=pltpu.CompilerParams(vmem_limit_bytes=16 * MIB),
        cost_estimate=pl.CostEstimate(flops=10**6, bytes_accessed=10**4, transcendentals=0),
    )(moments, far, near, trig, spread, weights, wave_high, wave_low)


def ham_kernel(n_starts, n_outs, codes_ref, counts_ref, blocks_ref, scale_ref, *refs):
    n_orbs = len(refs) - n_starts - n_outs - 5
    orb_refs, refs = refs[:n_orbs], refs[n_orbs:]
    starts, outs, (ham, turned, scaled, orbs, sems) = refs[:n_starts], refs[n_starts : n_starts + n_outs], refs[-5:]
    tiles = ham.shape[0] - 1
    copies = orbital_copies(*orb_refs[:3], orb_refs[3:], orbs, sems)
    for start in starts:
        copies[0].append(pltpu.make_async_copy(start, ham.at[0:tiles], sems.at[5]))
    for copy in sum(copies, []):
        copy.start()
    if n_starts == 0:

        def clear(t, unused):
            ham[t] = jnp.zeros((TB, TB), F32)
            return unused

        lax.fori_loop(0, tiles, clear, 0)
    add_ham(codes_ref, counts_ref, blocks_ref, copies, orbs, scale_ref[...], ham, turned, scaled)
    at = 0
    for out in outs:
        out[...] = ham[at : at + out.shape[0]].astype(out.dtype)
        at = at + out.shape[0]


def ham_terms(codes, counts, blocks, scale, orbs, starts, outs, flops):
    tiles = sum(count for count, unused in outs)
    return pl.pallas_call(
        functools.partial(ham_kernel, len(starts), len(outs)),
        in_specs=[SMEM_SPEC] * 3 + [VMEM_SPEC] + [ANY_SPEC] * (len(orbs) + len(starts)),
        out_specs=[VMEM_SPEC] * len(outs),
        out_shape=[jax.ShapeDtypeStruct((count, TB, TB), dtype) for count, dtype in outs],
        scratch_shapes=[
            pltpu.VMEM((tiles + 1, TB, TB), F32),
            pltpu.VMEM((UB, TB, DEV_PTS), BF16),
            pltpu.VMEM((UB, DEV_PTS, TB), BF16),
            pltpu.VMEM((LISTERS * BAT_DEV, PTS, BB * TB), BF16),
            pltpu.SemaphoreType.DMA((6,)),
        ],
        compiler_params=pltpu.CompilerParams(vmem_limit_bytes=56 * MIB),
        cost_estimate=pl.CostEstimate(flops=flops, bytes_accessed=10**4, transcendentals=0),
    )(codes, counts, blocks, scale, *orbs, *starts)


def final_kernel(own_ref, x_ref, y_ref, out_ref):
    half = TILE_DEV // 2
    step = half // 2
    got = jnp.where(pl.program_id(0) < half // step, x_ref[...].astype(F32), y_ref[...].astype(F32))
    out_ref[...] = (own_ref[...] + got).astype(BF16)


def final_tiles(own, got_x, got_y):
    step = TILE_DEV // 4
    block = (step, TB, TB)
    return pl.pallas_call(
        final_kernel,
        grid=(4,),
        in_specs=[
            pl.BlockSpec(block, lambda t: (t, 0, 0)),
            pl.BlockSpec(block, lambda t: (jnp.minimum(t, 1), 0, 0)),
            pl.BlockSpec(block, lambda t: (jnp.maximum(t - 2, 0), 0, 0)),
        ],
        out_specs=pl.BlockSpec(block, lambda t: (t, 0, 0)),
        out_shape=jax.ShapeDtypeStruct((TILE_DEV, TB, TB), BF16),
        compiler_params=pltpu.CompilerParams(vmem_limit_bytes=16 * MIB),
        cost_estimate=pl.CostEstimate(flops=10**6, bytes_accessed=10**4, transcendentals=0),
    )(own, got_x, got_y)


def kept_of(mine, places):
    rows = jnp.arange(R, dtype=jnp.int32)
    codes = places + (rows // UB) * 256 + (rows % UB) * 4096
    before = (rows[:, None] < rows[None, :])[None] & mine[:, :, None]
    rank = jnp.sum(before.astype(jnp.int32), axis=1)
    counts = jnp.sum(mine.astype(jnp.int32), axis=1)
    at = jnp.arange(LIST_LEN, dtype=jnp.int32)
    hit = (rank[:, None, :] == at[None, :, None]) & mine[:, None, :]
    listed = jnp.sum(jnp.where(hit, codes[:, None, :], 0), axis=2)
    return listed, counts, at


def lists_of(owners, slots, me):
    half = TILE_DEV // 2
    away = owners ^ me
    own = away == 0
    shared = ((away == X1) & (slots < half)) | ((away == Y1) & (slots >= half))
    found = []
    for mine in (own | shared, own, shared):
        place = jnp.where(own, slots, TILE_DEV + slots) if len(found) == 0 else slots
        listed, counts, at = kept_of(mine, place)
        dummy = PARTS if len(found) == 0 else TILE_DEV
        found.append((jnp.where(at[None] < counts[:, None], listed, dummy), (counts + GROUP - 1) // GROUP))
    return found


def what_is_listed(rows):
    ints = rows.astype(jnp.int32)
    blocks = ints[:, 2 * TB :].reshape(LISTERS * BAT_DEV, TB)[:, :BB]
    return ints[:, :R], ints[:, TB : TB + R], blocks


def on_device(
    orbitals,
    dens_tiles,
    point_coords,
    point_weights,
    batch_blocks,
    tile_owner,
    tile_slot,
    batch_atoms,
    batch_weights,
    atom_grid_index,
):
    me = lax.axis_index("dev").astype(jnp.int32)

    facts = packed_facts(
        point_coords,
        point_weights[None],
        tile_owner.reshape(1, R),
        tile_slot[None],
        batch_blocks,
        batch_atoms,
        batch_weights,
    )
    facts = (facts, swap(facts, X3), swap(facts, Y3), swap(facts, X3 ^ Y3))
    location, sent, *facts = lax.optimization_barrier((atom_places(atom_grid_index), orbitals, *facts))
    half = TILE_DEV // 2
    tile_x, tile_y = swap(dens_tiles, X1), swap(dens_tiles, Y1)
    orb_x, orb_y = swap(sent, X3), swap(sent, Y3)

    facts = jnp.stack(facts)
    coords = facts[:, :3].transpose(1, 0, 2).reshape(3, LIST_PTS)
    weights = facts[:, 3].reshape(LISTERS * BAT_DEV, PTS)
    owners, slots, blocks = what_is_listed(facts[:, 4])
    near_by = facts[:, 5].reshape(LISTERS, 2, BAT_DEV, TB)[..., :NEAR].reshape(LISTERS, 2, BAT_DEV, NEAR)
    atoms = near_by[:, 0].reshape(LISTERS * BAT_DEV, NEAR).astype(jnp.int32)
    raw_weight = near_by[:, 1].reshape(LISTERS * BAT_DEV, NEAR)
    away = owners ^ me
    tmap = jnp.where((away & 10) == 0, ((away & 1) + ((away >> 2) & 1) * 2) * TILE_DEV + slots, NO_TILE)
    codes, counts = lists_of(owners, slots, me)[0]

    wave_vecs = wave_table(KM)
    squared = jnp.sum(wave_vecs * wave_vecs, axis=0)
    near_gain = jnp.tile(0.1 / (1.0 + 0.1 * squared), 2)[None]
    far_gain = jnp.tile(0.03 / (1.0 + 0.1 * squared), 2)[None]
    phases = jnp.einsum("ca,cm->am", location, wave_vecs, precision=TOP_PRECISION) * (2.0 * math.pi / GRIDN)
    trig = jnp.concatenate([jnp.cos(phases), jnp.sin(phases)], axis=1)
    partition = raw_weight / jnp.sum(raw_weight, axis=1, keepdims=True)
    share = jnp.sum(
        jnp.where(
            atoms[None] == jnp.arange(ATOM_GRP, dtype=jnp.int32)[:, None, None],
            partition[None],
            0.0,
        ),
        axis=2,
    )
    displace = coords[:, None, :] - location[:, :, None]
    envelope = jnp.exp(-2.0 * jnp.sum(displace * displace, axis=0) / (GRIDN * GRIDN))
    spread = (envelope.reshape(ATOM_GRP, LISTERS * BAT_DEV, PTS) * share[:, :, None]).reshape(ATOM_GRP, LIST_PTS)
    wave_high, wave_low = wave_of_points(coords)
    wave_high, wave_low, onward = lax.optimization_barrier((wave_high, wave_low, tile_y[:half]))
    tile_low, tile_high = swap(onward, X1), swap(tile_x[half:], Y1)
    orb_first, orb_second = swap(orb_y[0], X3), swap(orb_x[1], Y3)
    orbs = (orbitals, orb_x, orb_y, orb_first, orb_second)
    first_tmap, first_blocks = tmap, blocks
    early = (spread, weights, wave_high, wave_low, trig, codes, counts, tmap, blocks)

    tiles = (dens_tiles, tile_x, tile_y, tile_low, tile_high)
    before = first_density(first_tmap, first_blocks, tiles, orbs)
    early, late, *unused = lax.optimization_barrier((early, orbitals, before, tile_low, tile_high, orb_first, orb_second))
    spread, weights, wave_high, wave_low, trig, codes, counts, tmap, blocks = early
    orb_far = swap(late, XY)
    part, orb_diag = density_and_moments(
        tmap, blocks, tiles, orbs, before, spread, weights, wave_high, wave_low, trig, facts[:, 4]
    )
    a = ATOM_GRP
    got = swap(part, X3)
    order = (a + 1, a, a + 3, a + 2)
    part = part + jnp.concatenate([got[:a]] + [got[r : r + 1] for r in order] + [jnp.zeros((LISTERS, KM), F32)])
    got = swap(part, Y3)
    density_got = got[a + 2]
    moments, orb_far = lax.optimization_barrier((part[:a] + got[:a], orb_far))
    orb_far_x, orb_far_y = swap(orb_far, X3), swap(orb_far, Y3)
    got = swap(jnp.concatenate([moments, part[a + LISTERS :]]), X1)
    moments = moments + got[:a]
    got = swap(jnp.concatenate([moments, got[a:]]), Y1)
    orb_diag, moments = lax.optimization_barrier((orb_diag, moments + got[:a]))
    orbs_far = (orb_far, orb_far_x, orb_far_y, swap(orb_diag, XY))
    far_owners, far_slots, far_blocks = what_is_listed(got[a:])
    unused, (own_codes, own_counts), (far_codes, far_counts) = lists_of(far_owners, far_slots, me)
    structure = jnp.sum(moments[:, :1] * trig, axis=0, keepdims=True)
    for bits in (1, 2, 4):
        structure = structure + swap_grp(structure, bits)
    structure = structure + swap_grp(structure, 8)
    potential, scale = potential_of(
        moments,
        far_gain * structure,
        near_gain,
        trig,
        spread,
        weights.reshape(1, LIST_PTS),
        wave_high,
        wave_low,
    )
    far_scale = swap(scale, XY)
    own, shared = ham_terms(
        codes, counts, blocks, scale, orbs, (), ((TILE_DEV, F32), (TILE_DEV, F32)), 10**6
    )
    half = TILE_DEV // 2
    part_x, part_y = ham_terms(
        far_codes, far_counts, far_blocks, far_scale, orbs_far, (shared,), ((half, BF16), (half, BF16)), 10**6
    )
    (own,) = ham_terms(
        own_codes, own_counts, far_blocks, far_scale, orbs_far, (own,), ((TILE_DEV, F32),), 2 * 10**10
    )
    density, other, part_x = lax.optimization_barrier((part[a], density_got, part_x))
    return (density + other, potential.reshape(-1), final_tiles(own, swap(part_x, X1), swap(part_y, Y1)))


def solution(mesh):
    in_specs = (
        P(("grp", "dev"), None, None),
        P(("grp", "dev"), None, None),
        P(None, ("grp", "dev")),
        P(("grp", "dev")),
        P(("grp", "dev"), None),
        P(("grp", "dev"), None),
        P(("grp", "dev")),
        P(("grp", "dev"), None),
        P(("grp", "dev"), None),
        P(None, "grp"),
    )
    out_specs = (P(("grp", "dev")), P(("grp", "dev")), P(("grp", "dev"), None, None))
    return jax.shard_map(
        on_device, mesh=mesh, in_specs=in_specs, out_specs=out_specs, check_vma=False
    )
```

```python
import functools
import math

import jax
import jax.numpy as jnp
from jax import lax
from jax.experimental import pallas as pl
from jax.experimental.pallas import tpu as pltpu
from jax.sharding import PartitionSpec as P

TB = 128
BB = 8
UB = 9
R = 81
PTS = 256
BAT_DEV = 2
KM = 512
HALF = KM // 2
NEAR = 4
TILE_DEV = 32
GRIDN = 64
ATOM_GRP = 16
DEV_PTS = BAT_DEV * PTS
LISTERS = 4
LIST_PTS = LISTERS * DEV_PTS
NO_TILE = 4 * TILE_DEV
PARTS = TILE_DEV + 2 * (TILE_DEV // 2)
GROUP = 4
LIST_LEN = 32
MIB = 1024 * 1024

F32 = jnp.float32
BF16 = jnp.bfloat16
TOP_PRECISION = lax.Precision.HIGHEST
NT = (((1,), (1,)), ((), ()))


def swap(array, bits):
    return lax.ppermute(array, "dev", [(d, d ^ bits) for d in range(16)])


def swap_grp(array, bits):
    return lax.ppermute(array, "grp", [(g, g ^ bits) for g in range(16)])


X1, Y1 = 1, 4
X3, Y3 = 3, 12
XY = 5


def wave_table(count):
    mode_ids = jnp.arange(count // 2, dtype=jnp.int32)
    return jnp.stack([mode_ids % 8, mode_ids // 8 % 8, mode_ids // 64]).astype(F32)


def split_bf16(value):
    high = value.astype(BF16)
    return high, (value - high.astype(F32)).astype(BF16)


def wave_kernel(cs_ref, high_ref, low_ref):
    cos_x, sin_x = cs_ref[0:8], cs_ref[8:16]
    for fz in range(4):
        cos_z, sin_z = cs_ref[32 + fz : 33 + fz], cs_ref[40 + fz : 41 + fz]
        for fy in range(0, 8, 2):
            parts_cos, parts_sin = [], []
            for step in range(2):
                cos_y = cs_ref[16 + fy + step : 17 + fy + step]
                sin_y = cs_ref[24 + fy + step : 25 + fy + step]
                cos_yz = cos_y * cos_z - sin_y * sin_z
                sin_yz = sin_y * cos_z + cos_y * sin_z
                parts_cos.append(cos_x * cos_yz - sin_x * sin_yz)
                parts_sin.append(sin_x * cos_yz + cos_x * sin_yz)
            row = fz * 64 + fy * 8
            for base, parts in ((row, parts_cos), (HALF + row, parts_sin)):
                high, low = split_bf16(jnp.concatenate(parts, axis=0))
                high_ref[base : base + 16] = high
                low_ref[base : base + 16] = low


def wave_of_points(coords):
    points = coords.shape[1]
    chunk = 256
    angle = (jnp.arange(8, dtype=F32)[None, :, None] * coords[:, None, :]) * (2.0 * math.pi / GRIDN)
    cs = jnp.stack([jnp.cos(angle), jnp.sin(angle)], axis=1).reshape(48, points)
    out = jax.ShapeDtypeStruct((KM, points), BF16)
    return pl.pallas_call(
        wave_kernel,
        grid=(points // chunk,),
        in_specs=[pl.BlockSpec((48, chunk), lambda i: (0, i))],
        out_specs=[pl.BlockSpec((KM, chunk), lambda i: (0, i))] * 2,
        out_shape=[out, out],
        cost_estimate=pl.CostEstimate(flops=8 * KM * points, bytes_accessed=4 * KM * points, transcendentals=0),
    )(cs)


def orbital_copies(own_orb, x_orb, y_orb, diag_orbs, orbs, sems):
    return [
        [pltpu.make_async_copy(own_orb, orbs.at[0:2], sems.at[0])],
        [pltpu.make_async_copy(x_orb, orbs.at[2:4], sems.at[1])],
        [pltpu.make_async_copy(y_orb, orbs.at[4:6], sems.at[2])],
        [
            pltpu.make_async_copy(orb, orbs.at[6 + b] if len(diag_orbs) > 1 else orbs.at[6:8], sems.at[3 + b])
            for b, orb in enumerate(diag_orbs)
        ],
    ]


def density_kernel(
    tmap_ref,
    blocks_ref,
    own_tile,
    x_tile,
    y_tile,
    low_tile,
    high_tile,
    own_orb,
    x_orb,
    y_orb,
    first_orb,
    second_orb,
    spread_ref,
    weights_ref,
    high_hbm,
    low_hbm,
    trig_ref,
    rows_ref,
    out_ref,
    diag_out,
    tiles,
    orbs,
    density,
    high_ref,
    low_ref,
    sems,
):
    half = TILE_DEV // 2
    arrivals = [
        pltpu.make_async_copy(source, tiles.at[at : at + source.shape[0]], sems.at[n])
        for n, (source, at) in enumerate(
            (
                (own_tile, 0),
                (x_tile, TILE_DEV),
                (y_tile, 2 * TILE_DEV),
                (low_tile, 3 * TILE_DEV),
                (high_tile, 3 * TILE_DEV + half),
            )
        )
    ]
    waves = [
        pltpu.make_async_copy(high_hbm, high_ref, sems.at[5]),
        pltpu.make_async_copy(low_hbm, low_ref, sems.at[6]),
    ]
    points = orbital_copies(own_orb, x_orb, y_orb, (first_orb, second_orb), orbs, sems.at[7:12])
    for copy in arrivals + sum(points, []) + waves:
        copy.start()
    tiles[NO_TILE] = jnp.zeros((TB, TB), BF16)
    for copy in arrivals:
        copy.wait()
    for lister in range(LISTERS):
        for copy in points[lister]:
            copy.wait()
        if lister == LISTERS - 1:
            onward = pltpu.make_async_copy(orbs.at[6:8], diag_out, sems.at[12])
            onward.start()

        def one_batch(batch, unused, lister=lister):
            chosen = [blocks_ref[batch, i] for i in range(BB)]
            total = jnp.zeros((PTS, TB), F32)
            for pair in range(BB // 2):
                columns = []
                for j in (2 * pair, 2 * pair + 1):
                    columns.append(
                        jnp.concatenate(
                            [tiles[tmap_ref[lister, chosen[i] * UB + chosen[j]]] for i in range(BB)], axis=0
                        )
                    )
                product = jnp.dot(orbs[batch], jnp.concatenate(columns, axis=1), preferred_element_type=F32)
                for side in range(2):
                    block = orbs[batch, :, (2 * pair + side) * TB : (2 * pair + side + 1) * TB]
                    total = total + product[:, side * TB : (side + 1) * TB] * block.astype(F32)
            density[pl.ds(batch, 1), :] = jnp.sum(total.T, axis=0, keepdims=True)
            return unused

        lax.fori_loop(BAT_DEV * lister, BAT_DEV * (lister + 1), one_batch, 0)
    for copy in waves:
        copy.wait()
    weighted = density[...] * weights_ref[...]
    charge = jnp.concatenate(
        [spread_ref[:, b * PTS : (b + 1) * PTS] * weighted[b : b + 1] for b in range(LISTERS * BAT_DEV)], axis=1
    )
    charge_high, charge_low = split_bf16(charge)
    both = lax.dot_general(
        jnp.concatenate([charge_high, charge_low], axis=0), high_ref[...], NT, preferred_element_type=F32
    )
    sums = both[:ATOM_GRP] + both[ATOM_GRP:]
    sums = sums + lax.dot_general(charge_high, low_ref[...], NT, preferred_element_type=F32)
    cos_sum, sin_sum = sums[:, :HALF], sums[:, HALF:]
    cos_atom, sin_atom = trig_ref[:, :HALF], trig_ref[:, HALF:]
    out_ref[0:ATOM_GRP, :HALF] = cos_sum * cos_atom + sin_sum * sin_atom
    out_ref[0:ATOM_GRP, HALF:] = sin_sum * cos_atom - cos_sum * sin_atom
    for e in range(LISTERS):
        for b in range(BAT_DEV):
            out_ref[ATOM_GRP + e : ATOM_GRP + e + 1, b * PTS : (b + 1) * PTS] = density[
                BAT_DEV * e + b : BAT_DEV * e + b + 1
            ]
    out_ref[ATOM_GRP + LISTERS :] = rows_ref[...]
    onward.wait()


SMEM_SPEC = pl.BlockSpec(memory_space=pltpu.SMEM)
VMEM_SPEC = pl.BlockSpec(memory_space=pltpu.VMEM)
ANY_SPEC = pl.BlockSpec(memory_space=pl.ANY)


def density_and_moments(tmap, blocks, tiles, orbs, spread, weights, wave_high, wave_low, trig, rows):
    return pl.pallas_call(
        density_kernel,
        in_specs=[SMEM_SPEC] * 2 + [ANY_SPEC] * 10 + [VMEM_SPEC] * 2 + [ANY_SPEC] * 2 + [VMEM_SPEC] * 2,
        out_specs=[VMEM_SPEC, ANY_SPEC],
        out_shape=[
            jax.ShapeDtypeStruct((ATOM_GRP + 8, KM), F32),
            jax.ShapeDtypeStruct((BAT_DEV, PTS, BB * TB), BF16),
        ],
        scratch_shapes=[
            pltpu.VMEM((NO_TILE + 1, TB, TB), BF16),
            pltpu.VMEM((LISTERS * BAT_DEV, PTS, BB * TB), BF16),
            pltpu.VMEM((LISTERS * BAT_DEV, PTS), F32),
            pltpu.VMEM((KM, LIST_PTS), BF16),
            pltpu.VMEM((KM, LIST_PTS), BF16),
            pltpu.SemaphoreType.DMA((13,)),
        ],
        compiler_params=pltpu.CompilerParams(vmem_limit_bytes=56 * MIB),
        cost_estimate=pl.CostEstimate(flops=10**6, bytes_accessed=10**4, transcendentals=0),
    )(tmap, blocks, *tiles, *orbs, spread, weights, wave_high, wave_low, trig, rows)


def pack_kernel(coords, weights, owner, slot, blocks, atoms, shares, out_ref, owner_ref, slot_ref, blocks_ref, atoms_ref, shares_ref, sems):
    copies = [
        pltpu.make_async_copy(source, target, sems.at[n])
        for n, (source, target) in enumerate(
            (
                (coords, out_ref.at[0:3]),
                (weights, out_ref.at[3:4]),
                (owner, owner_ref),
                (slot, slot_ref),
                (blocks, blocks_ref),
                (atoms, atoms_ref),
                (shares, shares_ref),
            )
        )
    ]
    out_ref[4:6] = jnp.zeros((2, DEV_PTS), F32)
    for copy in copies:
        copy.start()
    for copy in copies:
        copy.wait()
    out_ref[4:5, :R] = owner_ref[...].astype(F32)
    out_ref[4:5, TB : TB + R] = slot_ref[...].astype(F32)
    for b in range(BAT_DEV):
        out_ref[4:5, (2 + b) * TB : (2 + b) * TB + BB] = blocks_ref[b : b + 1].astype(F32)
        out_ref[5:6, b * TB : b * TB + NEAR] = atoms_ref[b : b + 1].astype(F32)
        out_ref[5:6, (2 + b) * TB : (2 + b) * TB + NEAR] = shares_ref[b : b + 1].astype(F32)


def place_kernel(index_ref, out_ref):
    out_ref[...] = index_ref[...].astype(F32)


def atom_places(index):
    return pl.pallas_call(
        place_kernel,
        in_specs=[VMEM_SPEC],
        out_specs=VMEM_SPEC,
        out_shape=jax.ShapeDtypeStruct(index.shape, F32),
        cost_estimate=pl.CostEstimate(flops=2 * 10**10, bytes_accessed=1000, transcendentals=0),
    )(index)


def packed_facts(*parts):
    return pl.pallas_call(
        pack_kernel,
        in_specs=[ANY_SPEC] * 7,
        out_specs=VMEM_SPEC,
        out_shape=jax.ShapeDtypeStruct((6, DEV_PTS), F32),
        scratch_shapes=[pltpu.VMEM(part.shape, part.dtype) for part in parts[2:]] + [pltpu.SemaphoreType.DMA((7,))],
        compiler_params=pltpu.CompilerParams(vmem_limit_bytes=56 * MIB),
        cost_estimate=pl.CostEstimate(flops=1000, bytes_accessed=1000, transcendentals=0),
    )(*parts)


def add_ham(codes_ref, counts_ref, blocks_ref, copies, orbs, scale, ham, turned, scaled):
    for e in range(LISTERS):
        for copy in copies[e]:
            copy.wait()
        for b in range(BAT_DEV):
            source = orbs.at[BAT_DEV * e + b]
            factors = []
            for part in range(PTS // TB):
                at = e * DEV_PTS + b * PTS + part * TB
                factors.append(jnp.broadcast_to(scale[:, at : at + TB], (TB, TB)).T)
            missing = UB * (UB - 1) // 2
            for i in range(BB):
                block = blocks_ref[BAT_DEV * e + b, i]
                missing = missing - block
                turned[block, :, b * PTS : (b + 1) * PTS] = source[:, i * TB : (i + 1) * TB].T
                for part in range(PTS // TB):
                    piece = source[part * TB : (part + 1) * TB, i * TB : (i + 1) * TB]
                    rows = slice(b * PTS + part * TB, b * PTS + (part + 1) * TB)
                    scaled[block, rows, :] = (factors[part] * piece.astype(F32)).astype(BF16)
            scaled[missing, b * PTS : (b + 1) * PTS, :] = jnp.zeros((PTS, TB), BF16)
            turned[missing, :, b * PTS : (b + 1) * PTS] = jnp.zeros((TB, PTS), BF16)

        def some_items(step, unused):
            for item in range(GROUP):
                code = codes_ref[e, step * GROUP + item]
                tile = code & 255
                i = (code >> 8) & 15
                j = code >> 12
                ham[tile] += jnp.dot(turned[i], scaled[j], preferred_element_type=F32)
            return unused

        lax.fori_loop(0, counts_ref[e], some_items, 0)


def potential_kernel(
    moments_ref, far_ref, near_ref, trig_ref, spread_ref, weights_ref, high_ref, low_ref, pot_ref, scale_ref
):
    cos_atom, sin_atom = trig_ref[:, :HALF], trig_ref[:, HALF:]
    cos_near = moments_ref[:, :HALF] * near_ref[:, :HALF]
    sin_near = moments_ref[:, HALF:] * near_ref[:, HALF:]
    turned_cos = cos_near * cos_atom - sin_near * sin_atom
    turned_sin = cos_near * sin_atom + sin_near * cos_atom
    coef = jnp.concatenate(
        [
            jnp.concatenate([turned_cos, turned_sin], axis=1),
            jnp.concatenate([far_ref[...], jnp.zeros((ATOM_GRP - 1, KM), F32)], axis=0),
        ],
        axis=0,
    )
    coef_high, coef_low = split_bf16(coef)
    both = jnp.dot(jnp.concatenate([coef_high, coef_low], axis=0), high_ref[...], preferred_element_type=F32)
    values = both[: 2 * ATOM_GRP] + both[2 * ATOM_GRP :]
    values = values + jnp.dot(coef_high, low_ref[...], preferred_element_type=F32)
    pot = jnp.sum(values[:ATOM_GRP] * spread_ref[...], axis=0, keepdims=True) + values[ATOM_GRP : ATOM_GRP + 1]
    pot_ref[...] = pot[:, :DEV_PTS]
    scale_ref[...] = pot * weights_ref[...]


def potential_of(moments, far, near, trig, spread, weights, wave_high, wave_low):
    return pl.pallas_call(
        potential_kernel,
        in_specs=[VMEM_SPEC] * 8,
        out_specs=[VMEM_SPEC] * 2,
        out_shape=[jax.ShapeDtypeStruct((1, DEV_PTS), F32), jax.ShapeDtypeStruct((1, LIST_PTS), F32)],
        compiler_params=pltpu.CompilerParams(vmem_limit_bytes=16 * MIB),
        cost_estimate=pl.CostEstimate(flops=10**6, bytes_accessed=10**4, transcendentals=0),
    )(moments, far, near, trig, spread, weights, wave_high, wave_low)


def ham_kernel(n_starts, n_outs, codes_ref, counts_ref, blocks_ref, scale_ref, *refs):
    n_orbs = len(refs) - n_starts - n_outs - 5
    orb_refs, refs = refs[:n_orbs], refs[n_orbs:]
    starts, outs, (ham, turned, scaled, orbs, sems) = refs[:n_starts], refs[n_starts : n_starts + n_outs], refs[-5:]
    tiles = ham.shape[0] - 1
    copies = orbital_copies(*orb_refs[:3], orb_refs[3:], orbs, sems)
    for start in starts:
        copies[0].append(pltpu.make_async_copy(start, ham.at[0:tiles], sems.at[5]))
    for copy in sum(copies, []):
        copy.start()
    if n_starts == 0:

        def clear(t, unused):
            ham[t] = jnp.zeros((TB, TB), F32)
            return unused

        lax.fori_loop(0, tiles, clear, 0)
    add_ham(codes_ref, counts_ref, blocks_ref, copies, orbs, scale_ref[...], ham, turned, scaled)
    at = 0
    for out in outs:
        out[...] = ham[at : at + out.shape[0]].astype(out.dtype)
        at = at + out.shape[0]


def ham_terms(codes, counts, blocks, scale, orbs, starts, outs, flops):
    tiles = sum(count for count, unused in outs)
    return pl.pallas_call(
        functools.partial(ham_kernel, len(starts), len(outs)),
        in_specs=[SMEM_SPEC] * 3 + [VMEM_SPEC] + [ANY_SPEC] * (len(orbs) + len(starts)),
        out_specs=[VMEM_SPEC] * len(outs),
        out_shape=[jax.ShapeDtypeStruct((count, TB, TB), dtype) for count, dtype in outs],
        scratch_shapes=[
            pltpu.VMEM((tiles + 1, TB, TB), F32),
            pltpu.VMEM((UB, TB, DEV_PTS), BF16),
            pltpu.VMEM((UB, DEV_PTS, TB), BF16),
            pltpu.VMEM((LISTERS * BAT_DEV, PTS, BB * TB), BF16),
            pltpu.SemaphoreType.DMA((6,)),
        ],
        compiler_params=pltpu.CompilerParams(vmem_limit_bytes=56 * MIB),
        cost_estimate=pl.CostEstimate(flops=flops, bytes_accessed=10**4, transcendentals=0),
    )(codes, counts, blocks, scale, *orbs, *starts)


def final_kernel(own_ref, x_ref, y_ref, out_ref):
    half = TILE_DEV // 2
    step = half // 2
    got = jnp.where(pl.program_id(0) < half // step, x_ref[...].astype(F32), y_ref[...].astype(F32))
    out_ref[...] = (own_ref[...] + got).astype(BF16)


def final_tiles(own, got_x, got_y):
    step = TILE_DEV // 4
    block = (step, TB, TB)
    return pl.pallas_call(
        final_kernel,
        grid=(4,),
        in_specs=[
            pl.BlockSpec(block, lambda t: (t, 0, 0)),
            pl.BlockSpec(block, lambda t: (jnp.minimum(t, 1), 0, 0)),
            pl.BlockSpec(block, lambda t: (jnp.maximum(t - 2, 0), 0, 0)),
        ],
        out_specs=pl.BlockSpec(block, lambda t: (t, 0, 0)),
        out_shape=jax.ShapeDtypeStruct((TILE_DEV, TB, TB), BF16),
        compiler_params=pltpu.CompilerParams(vmem_limit_bytes=16 * MIB),
        cost_estimate=pl.CostEstimate(flops=10**6, bytes_accessed=10**4, transcendentals=0),
    )(own, got_x, got_y)


def kept_of(mine, places):
    rows = jnp.arange(R, dtype=jnp.int32)
    codes = places + (rows // UB) * 256 + (rows % UB) * 4096
    before = (rows[:, None] < rows[None, :])[None] & mine[:, :, None]
    rank = jnp.sum(before.astype(jnp.int32), axis=1)
    counts = jnp.sum(mine.astype(jnp.int32), axis=1)
    at = jnp.arange(LIST_LEN, dtype=jnp.int32)
    hit = (rank[:, None, :] == at[None, :, None]) & mine[:, None, :]
    listed = jnp.sum(jnp.where(hit, codes[:, None, :], 0), axis=2)
    return listed, counts, at


def lists_of(owners, slots, me):
    half = TILE_DEV // 2
    away = owners ^ me
    own = away == 0
    shared = ((away == X1) & (slots < half)) | ((away == Y1) & (slots >= half))
    found = []
    for mine in (own | shared, own, shared):
        place = jnp.where(own, slots, TILE_DEV + slots) if len(found) == 0 else slots
        listed, counts, at = kept_of(mine, place)
        dummy = PARTS if len(found) == 0 else TILE_DEV
        found.append((jnp.where(at[None] < counts[:, None], listed, dummy), (counts + GROUP - 1) // GROUP))
    return found


def what_is_listed(rows):
    ints = rows.astype(jnp.int32)
    blocks = ints[:, 2 * TB :].reshape(LISTERS * BAT_DEV, TB)[:, :BB]
    return ints[:, :R], ints[:, TB : TB + R], blocks


def on_device(
    orbitals,
    dens_tiles,
    point_coords,
    point_weights,
    batch_blocks,
    tile_owner,
    tile_slot,
    batch_atoms,
    batch_weights,
    atom_grid_index,
):
    me = lax.axis_index("dev").astype(jnp.int32)

    facts = packed_facts(
        point_coords,
        point_weights[None],
        tile_owner.reshape(1, R),
        tile_slot[None],
        batch_blocks,
        batch_atoms,
        batch_weights,
    )
    facts = (facts, swap(facts, X3), swap(facts, Y3), swap(facts, X3 ^ Y3))
    location, sent, *facts = lax.optimization_barrier((atom_places(atom_grid_index), orbitals, *facts))
    half = TILE_DEV // 2
    tile_x, tile_y = swap(dens_tiles, X1), swap(dens_tiles, Y1)
    orb_x, orb_y = swap(sent, X3), swap(sent, Y3)
    tile_low, tile_high = swap(tile_y[:half], X1), swap(tile_x[half:], Y1)
    orb_first, orb_second = swap(orb_y[0], X3), swap(orb_x[1], Y3)
    orbs = (orbitals, orb_x, orb_y, orb_first, orb_second)

    facts = jnp.stack(facts)
    coords = facts[:, :3].transpose(1, 0, 2).reshape(3, LIST_PTS)
    weights = facts[:, 3].reshape(LISTERS * BAT_DEV, PTS)
    owners, slots, blocks = what_is_listed(facts[:, 4])
    near_by = facts[:, 5].reshape(LISTERS, 2, BAT_DEV, TB)[..., :NEAR].reshape(LISTERS, 2, BAT_DEV, NEAR)
    atoms = near_by[:, 0].reshape(LISTERS * BAT_DEV, NEAR).astype(jnp.int32)
    raw_weight = near_by[:, 1].reshape(LISTERS * BAT_DEV, NEAR)
    away = owners ^ me
    tmap = jnp.where((away & 10) == 0, ((away & 1) + ((away >> 2) & 1) * 2) * TILE_DEV + slots, NO_TILE)
    codes, counts = lists_of(owners, slots, me)[0]

    wave_vecs = wave_table(KM)
    squared = jnp.sum(wave_vecs * wave_vecs, axis=0)
    near_gain = jnp.tile(0.1 / (1.0 + 0.1 * squared), 2)[None]
    far_gain = jnp.tile(0.03 / (1.0 + 0.1 * squared), 2)[None]
    phases = jnp.einsum("ca,cm->am", location, wave_vecs, precision=TOP_PRECISION) * (2.0 * math.pi / GRIDN)
    trig = jnp.concatenate([jnp.cos(phases), jnp.sin(phases)], axis=1)
    partition = raw_weight / jnp.sum(raw_weight, axis=1, keepdims=True)
    share = jnp.sum(
        jnp.where(
            atoms[None] == jnp.arange(ATOM_GRP, dtype=jnp.int32)[:, None, None],
            partition[None],
            0.0,
        ),
        axis=2,
    )
    displace = coords[:, None, :] - location[:, :, None]
    envelope = jnp.exp(-2.0 * jnp.sum(displace * displace, axis=0) / (GRIDN * GRIDN))
    spread = (envelope.reshape(ATOM_GRP, LISTERS * BAT_DEV, PTS) * share[:, :, None]).reshape(ATOM_GRP, LIST_PTS)
    wave_high, wave_low = wave_of_points(coords)
    early, late = (spread, weights, wave_high, wave_low, trig, codes, counts, tmap, blocks), orbitals
    early, late, *unused = lax.optimization_barrier((early, late, tile_low, tile_high, orb_first, orb_second))
    spread, weights, wave_high, wave_low, trig, codes, counts, tmap, blocks = early
    orb_far = swap(late, XY)

    part, orb_diag = density_and_moments(
        tmap,
        blocks,
        (dens_tiles, tile_x, tile_y, tile_low, tile_high),
        orbs,
        spread,
        weights,
        wave_high,
        wave_low,
        trig,
        facts[:, 4],
    )
    a = ATOM_GRP
    got = swap(part, X3)
    order = (a + 1, a, a + 3, a + 2)
    part = part + jnp.concatenate([got[:a]] + [got[r : r + 1] for r in order] + [jnp.zeros((LISTERS, KM), F32)])
    got = swap(part, Y3)
    density_got = got[a + 2]
    moments, orb_far = lax.optimization_barrier((part[:a] + got[:a], orb_far))
    orb_far_x, orb_far_y = swap(orb_far, X3), swap(orb_far, Y3)
    got = swap(jnp.concatenate([moments, part[a + LISTERS :]]), X1)
    moments = moments + got[:a]
    got = swap(jnp.concatenate([moments, got[a:]]), Y1)
    orb_diag, moments = lax.optimization_barrier((orb_diag, moments + got[:a]))
    orbs_far = (orb_far, orb_far_x, orb_far_y, swap(orb_diag, XY))
    far_owners, far_slots, far_blocks = what_is_listed(got[a:])
    unused, (own_codes, own_counts), (far_codes, far_counts) = lists_of(far_owners, far_slots, me)
    structure = jnp.sum(moments[:, :1] * trig, axis=0, keepdims=True)
    for bits in (1, 2, 4, 8):
        structure = structure + swap_grp(structure, bits)
    potential, scale = potential_of(
        moments,
        far_gain * structure,
        near_gain,
        trig,
        spread,
        weights.reshape(1, LIST_PTS),
        wave_high,
        wave_low,
    )
    far_scale = swap(scale, XY)
    own, shared = ham_terms(
        codes, counts, blocks, scale, orbs, (), ((TILE_DEV, F32), (TILE_DEV, F32)), 10**6
    )
    half = TILE_DEV // 2
    part_x, part_y = ham_terms(
        far_codes, far_counts, far_blocks, far_scale, orbs_far, (shared,), ((half, BF16), (half, BF16)), 10**6
    )
    (own,) = ham_terms(
        own_codes, own_counts, far_blocks, far_scale, orbs_far, (own,), ((TILE_DEV, F32),), 2 * 10**10
    )
    density, other, part_x = lax.optimization_barrier((part[a], density_got, part_x))
    return (density + other, potential.reshape(-1), final_tiles(own, swap(part_x, X1), swap(part_y, Y1)))


def solution(mesh):
    in_specs = (
        P(("grp", "dev"), None, None),
        P(("grp", "dev"), None, None),
        P(None, ("grp", "dev")),
        P(("grp", "dev")),
        P(("grp", "dev"), None),
        P(("grp", "dev"), None),
        P(("grp", "dev")),
        P(("grp", "dev"), None),
        P(("grp", "dev"), None),
        P(None, "grp"),
    )
    out_specs = (P(("grp", "dev")), P(("grp", "dev")), P(("grp", "dev"), None, None))
    return jax.shard_map(
        on_device, mesh=mesh, in_specs=in_specs, out_specs=out_specs, check_vma=False
    )
```
